128 devices in a mesh: wide: 64 (over x, z, y), narrow: 2 (over core).
Axes of the slice: x: 4, y: 4, z: 4, core: 2. Of those that a mesh axis runs over, the one named last changes fastest.
Arguments:
- block_input: bfloat16 [256, 256, 1024], P(('wide', 'narrow'))
- attn_gain: bfloat16 [1024], replicated, may hold values from 0.5 to 1.5
- attn_shift: bfloat16 [1024], replicated, may hold values from -1 to 1
- query_key_value_weight: bfloat16 [1024, 3072], replicated, may hold values from -0.1875 to 0.1875
- output_weight: bfloat16 [1024, 1024], replicated, may hold values from -0.75 to 0.75
- ffn_gain: bfloat16 [1024], replicated, may hold values from 0.5 to 1.5
- ffn_shift: bfloat16 [1024], replicated, may hold values from -1 to 1
- expert_in: bfloat16 [64, 1024, 4096], P('wide'), may hold values from -0.1875 to 0.1875
- expert_out: bfloat16 [64, 4096, 1024], P('wide'), may hold values from -0.09375 to 0.09375
- hash_ids: int32 [256, 256], P(('wide', 'narrow')), may hold values from 0 to 63
- seq_lengths: int32 [256], P(('wide', 'narrow')), may hold values from 64 to 256, as said below
- prev_counts: int32 [64], replicated, may hold values from 0 to 2047
- out_grad: bfloat16 [256, 256, 1024], P(('wide', 'narrow')), may hold values from -6 to 6
Outputs:
- block_output: bfloat16 [256, 256, 1024], P(('wide', 'narrow'))
- input_grad: float32 [256, 256, 1024], P(('wide', 'narrow'))
- attn_gain_grad: float32 [1024], P(('wide', 'narrow'))
- attn_shift_grad: float32 [1024], P(('wide', 'narrow'))
- qkv_grad: float32 [1024, 3072], P(('wide', 'narrow'))
- out_weight_grad: float32 [1024, 1024], P(('wide', 'narrow'))
- ffn_gain_grad: float32 [1024], P(('wide', 'narrow'))
- ffn_shift_grad: float32 [1024], P(('wide', 'narrow'))
- expert_in_grad: float32 [64, 1024, 4096], P('wide', None, 'narrow')
- expert_out_grad: float32 [64, 4096, 1024], P('wide', 'narrow')
- new_average: float32 [64], replicated
The draws below stay inside these ranges and needn't reach their ends.
Inputs may be any that keep to these rules, and one draw needn't show every extreme that they name: `hash_ids`: the expert of each token; the last rows of a sequence past its length are padding and ignored. `seq_lengths`: some sequence has 256 tokens and some has 64.
All inputs are finite; a program needn't handle non-finite values.
Results may differ from the reference program's by a relative error of at most 0.0085.
The reference program's roundings to bfloat16 on the way count: a program that leaves them out, or rounds other values in their place, can miss the bound.
Values may be sent and summed in bfloat16 or wider, within the bound.
No kernel may reach another device: no remote copies, remote signals or barrier semaphores. Data moves between devices by JAX's collectives and lax.ppermute only.
A program may use at most 256 MiB of HBM per device.

```python
import math
import jax
import jax.numpy as jnp
import numpy as np
from jax import lax

D = 1024
HEADS = 16
HEAD_DIM = 64
FF = 4096
SEQS_DEV = 2
LEN = 256
MIN_LEN = 64
EXPERTS = 64
BATCH = 256
CAP = 6


def draw_block_input(key, part):
    key = jax.random.fold_in(key, 11)
    first, second, third = jax.random.split(key, 3)
    base = jax.random.normal(first, (BATCH, LEN, D), jnp.float32)
    row_scale = jnp.exp(jax.random.uniform(second, (BATCH, LEN, 1), jnp.float32, 0.0, math.log(8.0)))
    col_scale = jnp.exp(jax.random.uniform(third, (1, 1, D), jnp.float32, -0.7, 0.7))
    return (base * row_scale * col_scale * 0.5).astype(jnp.bfloat16)


def draw_seq_lengths(key, part):
    key = jax.random.fold_in(key, 23)
    first, second = jax.random.split(key)
    drawn = jax.random.randint(first, (BATCH,), MIN_LEN, LEN + 1)
    places = jax.random.permutation(second, BATCH)
    drawn = drawn.at[places[0]].set(LEN).at[places[1]].set(MIN_LEN)
    return drawn.astype(jnp.int32)


def with_ends(values, rng, low, high):
    shape = values.shape
    index_at = [jax.random.randint(jax.random.fold_in(rng, axis), (), 0, shape[axis]) for axis in range(len(shape))]
    values = values.at[tuple(index_at)].set(low)
    longest = shape.index(max(shape))
    index_at[longest] = (index_at[longest] + 1) % shape[longest]
    return values.at[tuple(index_at)].set(high)


def steps_of(rng, extent, shards, least, high):
    factor_of, own = 1.0, jax.random.fold_in(rng, 6)
    for dim, parts in shards:
        heights = jnp.exp(jax.random.uniform(jax.random.fold_in(own, dim), (parts,), jnp.float32, least / len(shards), high / len(shards)))
        factor_of = factor_of * jnp.repeat(heights, extent[dim] // parts).reshape([-1 if axis == dim else 1 for axis in range(len(extent))])
    return factor_of


def rank_table(amount, lean):
    loads = [(1 << 20) // math.isqrt(rank ** lean) + 1 for rank in range(1, amount + 1)]
    width = 1 + sum(loads) // (1 << 30)
    return np.cumsum(np.array([max(1, weight // width) for weight in loads]))


def ranked(own_key, extent, count, skew):
    grid = rank_table(count, skew)
    ticket = jax.random.randint(jax.random.fold_in(own_key, 1), extent, 0, int(grid[count - 1]))
    standing = jnp.searchsorted(jnp.asarray(grid, jnp.int32), ticket, side="right")
    return jax.random.permutation(jax.random.fold_in(own_key, 2), count)[standing].astype(jnp.int32)


def gaussian(own_key, dims, scale, bound, cuts=(), kind=jnp.bfloat16):
    level = steps_of(own_key, dims, cuts, -0.22, 0.18) if cuts else 1.0
    entries = jax.random.normal(own_key, dims, jnp.float32) * scale * level
    return jnp.minimum(jnp.maximum(entries, -bound), bound).astype(kind)


def setup_inputs(seed: int = 0) -> dict:
    splits = jax.random.split(jax.random.key(seed), 14)
    return {
        "block_input": draw_block_input(jax.random.fold_in(splits[13], 71), 0),
        "attn_gain": jnp.clip(1.0 + 0.1 * jax.random.normal(splits[1], (D,), jnp.float32), 0.5, 1.5).astype(jnp.bfloat16),
        "attn_shift": gaussian(splits[2], (D,), 0.2, 1.0),
        "query_key_value_weight": gaussian(splits[3], (D, 3 * D), D ** -0.5, 0.1875),
        "output_weight": gaussian(splits[4], (D, D), (D // 16) ** -0.5, 0.75),
        "ffn_gain": jnp.clip(1.0 + 0.1 * jax.random.normal(splits[5], (D,), jnp.float32), 0.5, 1.5).astype(jnp.bfloat16),
        "ffn_shift": gaussian(splits[6], (D,), 0.2, 1.0),
        "expert_in": gaussian(splits[7], (EXPERTS, D, FF), D ** -0.5, 0.1875, ((0, 64),)),
        "expert_out": gaussian(splits[8], (EXPERTS, FF, D), FF ** -0.5, 0.09375, ((0, 64),)),
        "hash_ids": with_ends(ranked(splits[9], (BATCH, LEN), EXPERTS, 1), jax.random.fold_in(splits[9], 3), 0, EXPERTS - 1).astype(jnp.int32),
        "seq_lengths": draw_seq_lengths(jax.random.fold_in(splits[13], 71), 0),
        "prev_counts": with_ends(jax.random.randint(splits[11], (EXPERTS,), 0, 2 * BATCH * LEN // EXPERTS), jax.random.fold_in(splits[11], 1), 0, (2 * BATCH * LEN // EXPERTS) - 1).astype(jnp.int32),
        "out_grad": gaussian(splits[12], (BATCH, LEN, D), 1.0, 6.0, ((0, 128),)),
    }


@jax.custom_vjp
def low(v):
    return lax.optimization_barrier(v.astype(jnp.bfloat16)).astype(jnp.float32)

@jax.custom_vjp
def low_back(v):
    return v

def low_keep(v):
    return (low(v), None)

def low_pass(kept, grad):
    return (grad,)

def back_keep(v):
    return (v, None)

def back_low(kept, grad):
    return (low(grad),)
low.defvjp(low_keep, low_pass)
low_back.defvjp(back_keep, back_low)
highest = lax.Precision.HIGHEST
norm_eps = 1e-05
momentum = 0.9

def layer_norm(features, norm_gain, norm_shift):
    centered = features - lax.optimization_barrier(jnp.mean(features, axis=-1, keepdims=True))
    spread = lax.optimization_barrier(jnp.mean(centered * centered, axis=-1, keepdims=True))
    return centered * lax.rsqrt(spread + norm_eps) * norm_gain + norm_shift

def gelu_tanh(values_in):
    return jax.nn.gelu(values_in, approximate=True)

def attend(normalized_input, lengths, query_key_value_weight, output_weight):
    group_size = normalized_input.shape[0]
    query_key_value_mixed = jnp.einsum('gld,de->gle', normalized_input, query_key_value_weight, precision=highest)
    query_key_value_mixed = low(low_back(query_key_value_mixed)).reshape(group_size, LEN, 3, HEADS, HEAD_DIM)
    queries = query_key_value_mixed[:, :, 0]
    key_rows = query_key_value_mixed[:, :, 1]
    values = query_key_value_mixed[:, :, 2]
    raw = jnp.einsum('gqhe,gkhe->ghqk', queries, key_rows, precision=highest) * (1.0 / math.sqrt(HEAD_DIM))
    position = jnp.arange(LEN)
    causal = (position[None, :] <= position[:, None])[None, None]
    live_keys = position[None, None, None, :] < lengths[:, None, None, None]
    scores = low_back(jnp.where(causal & live_keys, raw, -1000000000.0))
    shifted = scores - lax.optimization_barrier(jnp.max(scores, axis=-1, keepdims=True))
    expd = jnp.exp(shifted)
    attn_probs = low(expd / lax.optimization_barrier(jnp.sum(expd, axis=-1, keepdims=True)))
    attention_result = jnp.einsum('ghqk,gkhe->gqhe', attn_probs, values, precision=highest)
    attention_result = low(low_back(attention_result)).reshape(group_size, LEN, D)
    return low_back(jnp.einsum('gld,de->gle', attention_result, output_weight, precision=highest))

def reference(block_input, attn_gain, attn_shift, query_key_value_weight, output_weight, ffn_gain, ffn_shift, expert_in, expert_out, hash_ids, seq_lengths, prev_counts, out_grad):
    tok_rows = SEQS_DEV * LEN
    block_count = BATCH // SEQS_DEV
    position = jnp.arange(LEN)
    is_valid = (position[None, :] < seq_lengths[:, None]).reshape(block_count, tok_rows)
    chosen = hash_ids.reshape(block_count, tok_rows)
    onehot = ((chosen[:, :, None] == jnp.arange(EXPERTS)[None, None, :]) & is_valid[:, :, None]).astype(jnp.int32)
    before = jnp.cumsum(onehot, axis=1) - onehot
    slot_rank = lax.optimization_barrier(jnp.sum(before * onehot, axis=2))
    is_kept = is_valid & (slot_rank < CAP)
    dump_slot = block_count * EXPERTS * CAP
    slot_index = jnp.where(is_kept, (jnp.arange(block_count)[:, None] * EXPERTS + chosen) * CAP + slot_rank, dump_slot)
    slot_index = slot_index.reshape(-1).astype(jnp.int32)
    counts = lax.optimization_barrier(jnp.sum(onehot, axis=(0, 1)))
    group_size = math.gcd(BATCH, 16)

    def forward(inputs, gain_one, shift_one, qkv_full, out_full, gain_two, shift_two, first_all, second_all):
        normalized_input = low(layer_norm(inputs, gain_one, shift_one))
        grouped = normalized_input.reshape(BATCH // group_size, group_size, LEN, D)
        lengths = seq_lengths.reshape(BATCH // group_size, group_size)
        checked = jax.checkpoint(attend)
        residual_branch = lax.map(lambda pieces: checked(pieces[0], pieces[1], qkv_full, out_full), (grouped, lengths))
        hidden = inputs + residual_branch.reshape(BATCH, LEN, D)
        moved = low(low_back(layer_norm(hidden, gain_two, shift_two))).reshape(-1, D)
        buffer = jnp.zeros((dump_slot + 1, D), jnp.float32).at[slot_index].add(moved)[:-1]
        buffer = buffer.reshape(block_count, EXPERTS, CAP, D).transpose(1, 0, 2, 3).reshape(EXPERTS, block_count * CAP, D)

        def one_expert(pieces):
            rows_in, w_first, w_second = pieces
            lifted = low_back(jnp.dot(rows_in, w_first, precision=highest))
            active = low(gelu_tanh(lifted))
            return low(low_back(jnp.dot(active, w_second, precision=highest)))
        returned = lax.map(jax.checkpoint(one_expert), (buffer, first_all, second_all))
        returned = returned.reshape(EXPERTS, block_count, CAP, D).transpose(1, 0, 2, 3).reshape(-1, D)
        padded_back = jnp.concatenate([returned, jnp.zeros((1, D), jnp.float32)], axis=0)
        back_rows = padded_back[slot_index]
        return hidden + back_rows.reshape(BATCH, LEN, D)
    primals = (block_input.astype(jnp.float32), attn_gain.astype(jnp.float32), attn_shift.astype(jnp.float32), query_key_value_weight.astype(jnp.float32), output_weight.astype(jnp.float32), ffn_gain.astype(jnp.float32), ffn_shift.astype(jnp.float32), expert_in.astype(jnp.float32), expert_out.astype(jnp.float32))
    result, pullback = jax.vjp(forward, *primals)
    grads = pullback(out_grad.astype(jnp.float32))
    new_average = (momentum * prev_counts.astype(jnp.float32) + (1.0 - momentum) * counts.astype(jnp.float32)) * (float(EXPERTS) / float(BATCH * LEN))
    return (result.astype(jnp.bfloat16), grads[0], grads[1], grads[2], grads[3], grads[4], grads[5], grads[6], grads[7], grads[8], new_average)
```

```python
import math

import jax
import jax.numpy as jnp
from jax import lax
from jax.sharding import Mesh
from jax.sharding import PartitionSpec as P

HEADS = 16
WIDE = ("wide_0", "wide_1", "wide_2")
WIDE_NARROW = ("wide_0", "wide_1", "wide_2", "narrow")


norm_eps = 1e-05
momentum = 0.9
F32 = jnp.float32
BF16 = jnp.bfloat16


def swapped(shard):
    return lax.ppermute(shard, "narrow", [(0, 1), (1, 0)])


def exchanged(shard):
    return lax.all_to_all(shard, WIDE, 0, 0, tiled=True)


def dot(left, right, left_dim=1, right_dim=0):
    return lax.dot_general(
        left, right, (((left_dim,), (right_dim,)), ((), ())), preferred_element_type=F32
    )


def layer_norm(features, norm_gain, norm_shift):
    centered = features - jnp.mean(features, axis=-1, keepdims=True)
    spread = jnp.mean(centered * centered, axis=-1, keepdims=True)
    return centered * lax.rsqrt(spread + norm_eps) * norm_gain + norm_shift


def gelu_tanh(values_in):
    return jax.nn.gelu(values_in, approximate=True)


def per_device(
    block_input,
    attn_gain,
    attn_shift,
    query_key_value_weight,
    output_weight,
    ffn_gain,
    ffn_shift,
    expert_in,
    expert_out,
    hash_ids,
    seq_lengths,
    prev_counts,
    out_grad,
):
    seq_count, seq_len, width = block_input.shape
    head_count = HEADS
    head_width = width // head_count
    rows = seq_count * seq_len
    wide_size = lax.axis_size(WIDE)
    narrow_size = lax.axis_size("narrow")
    experts = wide_size
    capacity = max(2, 3 * rows // (4 * experts))
    ff_width = expert_in.shape[2]
    half_width = ff_width // narrow_size
    n_slots = experts * capacity
    core = lax.axis_index("narrow")
    own_rows = width // (wide_size * narrow_size)

    inputs = block_input.astype(F32)
    gain_one = attn_gain.astype(F32)
    shift_one = attn_shift.astype(F32)
    gain_two = ffn_gain.astype(F32)
    shift_two = ffn_shift.astype(F32)

    position = jnp.arange(seq_len)
    is_valid_keys = position[None, :] < seq_lengths[:, None]
    allowed = (position[None, :] <= position[:, None])[None, None] & is_valid_keys[:, None, None, :]
    chosen = hash_ids.reshape(rows)
    is_valid = is_valid_keys.reshape(rows)
    member = (chosen[:, None] == jnp.arange(experts)[None, :]) & is_valid[:, None]
    onehot = member.astype(BF16)
    earlier = (jnp.arange(rows)[None, :] < jnp.arange(rows)[:, None]).astype(BF16)
    before = dot(earlier, onehot)
    slot_rank = jnp.sum(jnp.where(member, before, 0.0), axis=1).astype(jnp.int32)
    counts = lax.psum(jnp.sum(member.astype(F32), axis=0), WIDE_NARROW)
    is_kept = is_valid & (slot_rank < capacity)
    slot_index = jnp.where(is_kept, chosen * capacity + slot_rank, -1)
    dispatch = (jnp.arange(n_slots)[:, None] == slot_index[None, :]).astype(BF16)
    combine = (slot_index[:, None] == jnp.arange(n_slots)[None, :]).astype(BF16)

    column = jnp.arange(width)
    picked = jnp.arange(width // narrow_size)

    def picks(which):
        source = picked // own_rows * (own_rows * narrow_size) + which * own_rows + picked % own_rows
        return (column[:, None] == source[None, :]).astype(BF16)

    def shared_columns(values):
        mine = dot(values, picks(core)).astype(BF16)
        other = dot(values, picks(1 - core)).astype(BF16)
        return jnp.concatenate([mine, swapped(other)], axis=0)

    def shared(values):
        return jnp.concatenate([values, swapped(values)], axis=0)

    normed = layer_norm(inputs, gain_one, shift_one).astype(BF16).reshape(rows, width)
    normed_cols = shared_columns(normed)
    mixed = dot(normed, query_key_value_weight).astype(BF16)
    mixed = mixed.reshape(seq_count, seq_len, 3, head_count, head_width)
    queries = mixed[:, :, 0]
    key_rows = mixed[:, :, 1]
    values = mixed[:, :, 2]
    score_scale = 1.0 / math.sqrt(head_width)

    def score_of():
        raw = (
            jnp.einsum("sqhe,skhe->shqk", queries, key_rows, preferred_element_type=F32)
            * score_scale
        )
        return jnp.where(allowed, raw, -1000000000.0)

    scores = score_of()
    row_max = jnp.max(scores, axis=-1, keepdims=True)
    log_total = row_max + jnp.log(jnp.sum(jnp.exp(scores - row_max), axis=-1, keepdims=True))
    attn_probs = jnp.exp(scores - log_total)
    attended = jnp.einsum(
        "shqk,skhe->sqhe", attn_probs.astype(BF16), values, preferred_element_type=F32
    ).astype(BF16)
    attended = attended.reshape(rows, width)
    attended_cols = shared_columns(attended)
    hidden = inputs.reshape(rows, width) + dot(attended, output_weight)
    moved = layer_norm(hidden, gain_two, shift_two).astype(BF16)

    grad_rows = out_grad.reshape(rows, width)
    sent = dot(dispatch, jnp.concatenate([moved, grad_rows], axis=1)).astype(BF16)
    sent = sent.reshape(n_slots, 2, width).transpose(1, 0, 2)
    chunk = capacity * width // 8
    packed = jnp.concatenate(
        [sent[0].reshape(experts, 8, chunk), sent[1].reshape(experts, 8, chunk)], axis=2
    )
    arrived = exchanged(packed)
    rows_in = arrived[:, :, :chunk].reshape(n_slots, width)
    grad_in = arrived[:, :, chunk:].reshape(n_slots, width)

    w_in = expert_in[0]
    w_out = expert_out[0]
    lifted = dot(rows_in, w_in)
    gelu_out, gelu_back = jax.vjp(gelu_tanh, lifted)
    active = gelu_out.astype(BF16)
    grad_lifted = gelu_back(dot(grad_in, w_out, 1, 1))[0].astype(BF16)
    grad_moved = dot(grad_lifted, w_in, 1, 1).astype(BF16)
    grad_came = exchanged(grad_moved.reshape(experts, 8, chunk)).reshape(n_slots, width)

    def shared_half(values):
        mine = lax.dynamic_slice_in_dim(values, core * half_width, half_width, 1)
        other = lax.dynamic_slice_in_dim(values, (1 - core) * half_width, half_width, 1)
        return jnp.concatenate([mine, swapped(other)], axis=0)

    rows_both = shared(rows_in)
    grad_both = shared(grad_in)
    expert_in_grad = dot(rows_both, shared_half(grad_lifted), 0, 0)[None]
    expert_out_grad = dot(shared_half(active), grad_both, 0, 0)[None]
    produced = dot(active, w_out).astype(BF16)

    grad_ffn_normed = dot(combine, grad_came)
    _, norm_two_back = jax.vjp(layer_norm, hidden, gain_two, shift_two)
    grad_hidden_part, ffn_gain_part, ffn_shift_part = norm_two_back(grad_ffn_normed)
    grad_hidden = grad_rows.astype(F32) + grad_hidden_part
    branch = grad_hidden.astype(BF16)
    out_weight_part = dot(attended_cols, shared(branch), 0, 0)
    grad_attended = dot(branch, output_weight, 1, 1).astype(BF16)
    grad_attended = grad_attended.reshape(seq_count, seq_len, head_count, head_width)
    probs_again = jnp.exp(score_of() - log_total)
    grad_probs = jnp.einsum("sqhe,skhe->shqk", grad_attended, values, preferred_element_type=F32)
    values_grad = jnp.einsum(
        "shqk,sqhe->skhe", probs_again.astype(BF16), grad_attended, preferred_element_type=F32
    )
    inner_sum = jnp.sum(probs_again * grad_probs, axis=-1, keepdims=True)
    grad_scores = (probs_again * (grad_probs - inner_sum)).astype(BF16)
    queries_grad = (
        jnp.einsum("shqk,skhe->sqhe", grad_scores, key_rows, preferred_element_type=F32)
        * score_scale
    )
    key_grad = (
        jnp.einsum("shqk,sqhe->skhe", grad_scores, queries, preferred_element_type=F32)
        * score_scale
    )
    mixed_gradient = (
        jnp.stack([queries_grad, key_grad, values_grad], axis=2)
        .reshape(rows, 3 * width)
        .astype(BF16)
    )
    qkv_part = dot(normed_cols, shared(mixed_gradient), 0, 0)
    normalized_gradient = dot(mixed_gradient, query_key_value_weight, 1, 1)
    _, norm_one_back = jax.vjp(layer_norm, inputs.reshape(rows, width), gain_one, shift_one)
    grad_input_part, attn_gain_part, attn_shift_part = norm_one_back(normalized_gradient)
    input_grad = (grad_hidden + grad_input_part).reshape(seq_count, seq_len, width)

    small = jnp.stack([attn_gain_part, attn_shift_part, ffn_gain_part, ffn_shift_part])
    small = small + swapped(small)
    small = small.reshape(4, wide_size, narrow_size, own_rows)
    small = lax.dynamic_index_in_dim(small, core, 2, keepdims=False).transpose(1, 2, 0)
    small = jnp.pad(small, ((0, 0), (0, 0), (0, 124)))
    tail = jnp.concatenate(
        [
            qkv_part.astype(BF16).reshape(wide_size, own_rows, 3 * width),
            out_weight_part.astype(BF16).reshape(wide_size, own_rows, width),
            small.astype(BF16),
            produced.reshape(experts, 8, chunk),
        ],
        axis=2,
    )
    landed = exchanged(tail)
    summed = jnp.sum(landed[:, :, : 4 * width + 128].astype(F32), axis=0)
    came_back = landed[:, :, 4 * width + 128 :].reshape(n_slots, width)
    back_rows = dot(combine, came_back)
    block_output = (hidden + back_rows).astype(BF16).reshape(seq_count, seq_len, width)

    total_tokens = float(rows * wide_size * narrow_size)
    new_average = (momentum * prev_counts.astype(F32) + (1.0 - momentum) * counts) * (
        float(experts) / total_tokens
    )
    return (
        block_output,
        input_grad,
        summed[:, 4 * width],
        summed[:, 4 * width + 1],
        summed[:, : 3 * width],
        summed[:, 3 * width : 4 * width],
        summed[:, 4 * width + 2],
        summed[:, 4 * width + 3],
        expert_in_grad,
        expert_out_grad,
        new_average,
    )


def solution(mesh):
    finer = Mesh(
        mesh.devices.reshape(4, 4, 4, mesh.shape["narrow"]),
        ("wide_0", "wide_1", "wide_2", "narrow"),
    )
    placed = (
        P(WIDE_NARROW, None, None),
        P(),
        P(),
        P(),
        P(),
        P(),
        P(),
        P(WIDE, None, None),
        P(WIDE, None, None),
        P(WIDE_NARROW, None),
        P(WIDE_NARROW),
        P(),
        P(WIDE_NARROW, None, None),
    )
    return jax.shard_map(
        per_device,
        mesh=finer,
        in_specs=placed,
        out_specs=(
            P(WIDE_NARROW, None, None),
            P(WIDE_NARROW, None, None),
            P(WIDE_NARROW),
            P(WIDE_NARROW),
            P(WIDE_NARROW, None),
            P(WIDE_NARROW, None),
            P(WIDE_NARROW),
            P(WIDE_NARROW),
            P(WIDE, None, "narrow"),
            P(WIDE, "narrow", None),
            P(),
        ),
        check_vma=False,
    )
```

```python
import functools
import math

import jax
import jax.experimental.pallas as pl
import jax.experimental.pallas.tpu as pltpu
import jax.numpy as jnp
from jax import lax
from jax.sharding import Mesh
from jax.sharding import PartitionSpec as P

HEADS = 16
WIDE = ("wide_0", "wide_1", "wide_2")
WIDE_NARROW = ("wide_0", "wide_1", "wide_2", "narrow")

norm_eps = 1e-05
momentum = 0.9
F32 = jnp.float32
BF16 = jnp.bfloat16
LANES = 128
MIB = 1 << 20


def swapped(shard):
    return lax.ppermute(shard, "narrow", [(0, 1), (1, 0)])


def exchanged(lines):
    shard = lines.reshape(lax.axis_size(WIDE), -1, lines.shape[1])
    return lax.all_to_all(shard, WIDE, 0, 0, tiled=True).reshape(lines.shape)


def dot(left, right, left_dim=1, right_dim=0):
    return lax.dot_general(
        left, right, (((left_dim,), (right_dim,)), ((), ())), preferred_element_type=F32
    )


def params(mib):
    return pltpu.CompilerParams(vmem_limit_bytes=mib * MIB)


def normalize(features):
    centered = features - jnp.mean(features, axis=-1, keepdims=True)
    spread = jnp.mean(centered * centered, axis=-1, keepdims=True)
    scale = lax.rsqrt(spread + norm_eps)
    return centered * scale, scale


def norm_backward(scaled, scale, gained):
    mean = jnp.mean(gained, axis=-1, keepdims=True)
    along = jnp.mean(gained * scaled, axis=-1, keepdims=True)
    return scale * (gained - mean - scaled * along)


def to_lines(store, rows, experts, capacity, lane_tile):
    for rank in range(capacity):
        for part in range(8):
            at = rank % 2 * 8 + part
            store[lane_tile + rank // 2, pl.ds(at, experts, stride=16), :] = rows[
                rank * experts : (rank + 1) * experts, part * LANES : (part + 1) * LANES
            ]


def from_lines(store, rows_ref, experts, capacity, lane_tile):
    for rank in range(capacity):
        for part in range(8):
            at = rank % 2 * 8 + part
            rows_ref[
                rank * experts : (rank + 1) * experts, part * LANES : (part + 1) * LANES
            ] = store[lane_tile + rank // 2, pl.ds(at, experts, stride=16), :].astype(BF16)


def fill_store(store, lines_ref, lane_tile, count, source_tile):
    for tile in range(count):
        at = (source_tile + tile) * LANES
        store[lane_tile + tile] = lines_ref[:, at : at + LANES].astype(F32)


def spill_store(store, lines_ref, count, target_tile):
    for tile in range(count):
        at = (target_tile + tile) * LANES
        lines_ref[:, at : at + LANES] = store[tile].astype(BF16)


def forward_kernel(
    experts,
    capacity,
    len_ref,
    ids_ref,
    x_ref,
    gain_one_ref,
    shift_one_ref,
    qkv_weight_ref,
    out_weight_ref,
    gain_two_ref,
    shift_two_ref,
    grad_ref,
    normed_ref,
    mixed_ref,
    probs_ref,
    attended_ref,
    hidden_ref,
    dispatch_ref,
    send_ref,
    moved_ref,
    store,
):
    rows, width = x_ref.shape
    seq_count, seq_len = ids_ref.shape
    gain_one = gain_one_ref[...].astype(F32)
    shift_one = shift_one_ref[...].astype(F32)
    gain_two = gain_two_ref[...].astype(F32)
    shift_two = shift_two_ref[...].astype(F32)

    step = 128

    def norm_one(i, _):
        at = pl.ds(pl.multiple_of(i * step, step), step)
        scaled, _ = normalize(x_ref[at, :].astype(F32))
        normed_ref[at, :] = (scaled * gain_one + shift_one).astype(BF16)
        return 0

    lax.fori_loop(0, rows // step, norm_one, 0)

    span = 512

    def project(i, _):
        at = pl.ds(pl.multiple_of(i * span, span), span)
        mixed_ref[:, at] = dot(normed_ref[...], qkv_weight_ref[:, at]).astype(BF16)
        return 0

    lax.fori_loop(0, 3 * width // span, project, 0)

    pairs = HEADS // 2
    low = (lax.broadcasted_iota(jnp.int32, (1, LANES), 1) < 64).astype(F32)
    score_scale = 1.0 / math.sqrt(width // HEADS)
    low_scaled = (low * score_scale).astype(BF16)
    high_scaled = ((1.0 - low) * score_scale).astype(BF16)
    query_at = lax.broadcasted_iota(jnp.int32, (2 * seq_len, seq_len), 0) % seq_len
    key_at = lax.broadcasted_iota(jnp.int32, (2 * seq_len, seq_len), 1)

    for s in range(seq_count):
        allowed = (key_at <= query_at) & (key_at < len_ref[s])
        here = slice(s * seq_len, (s + 1) * seq_len)

        def attend(p, _):
            at = pl.multiple_of(p * LANES, LANES)
            q = mixed_ref[here, pl.ds(at, LANES)]
            k = mixed_ref[here, pl.ds(width + at, LANES)]
            v = mixed_ref[here, pl.ds(2 * width + at, LANES)]
            both = jnp.concatenate([q * low_scaled, q * high_scaled], axis=0)
            scores = jnp.where(allowed, dot(both, k, 1, 1), -1000000000.0)
            raised = jnp.exp(scores - jnp.max(scores, axis=-1, keepdims=True))
            total = jnp.sum(raised, axis=-1, keepdims=True)
            probs = (raised * (1.0 / total)).astype(BF16)
            probs_ref[s, p] = probs
            out = dot(probs, v)
            out = out[:seq_len] * low + out[seq_len:] * (1.0 - low)
            attended_ref[here, pl.ds(at, LANES)] = out.astype(BF16)
            return 0

        lax.fori_loop(0, pairs, attend, 0, unroll=2)

    def norm_two(i, _):
        at = pl.ds(pl.multiple_of(i * 256, 256), 256)
        hidden = x_ref[at, :].astype(F32) + dot(attended_ref[at, :], out_weight_ref[...])
        hidden_ref[at, :] = hidden
        scaled, _ = normalize(hidden)
        moved_ref[at, :] = (scaled * gain_two + shift_two).astype(BF16)
        return 0

    lax.fori_loop(0, rows // 256, norm_two, 0)

    ids = jnp.concatenate([ids_ref[s : s + 1, :] for s in range(seq_count)], axis=1)
    lane = lax.broadcasted_iota(jnp.int32, (1, rows), 1)
    length = jnp.where(lane < seq_len, len_ref[0], len_ref[1])
    is_valid = lane % seq_len < length
    member = (lax.broadcasted_iota(jnp.int32, (experts, rows), 0) == ids) & is_valid
    onehot = member.astype(F32)
    earlier = (
        lax.broadcasted_iota(jnp.int32, (rows, rows), 0)
        < lax.broadcasted_iota(jnp.int32, (rows, rows), 1)
    ).astype(F32)
    before = dot(onehot.astype(BF16), earlier.astype(BF16))
    rank = jnp.sum(onehot * before, axis=0, keepdims=True).astype(jnp.int32)
    slot = jnp.where(is_valid & (rank < capacity), rank * experts + ids, -1)
    at_slot = lax.broadcasted_iota(jnp.int32, (experts * capacity, rows), 0)
    dispatch_ref[...] = (at_slot == slot).astype(F32).astype(BF16)
    to_lines(store, dot(dispatch_ref[...], moved_ref[...]), experts, capacity, 0)
    to_lines(store, dot(dispatch_ref[...], grad_ref[...]), experts, capacity, 3)
    counts = jnp.sum(onehot, axis=1, keepdims=True)
    upper = jnp.floor(counts * (1.0 / 64.0))
    column = lax.broadcasted_iota(jnp.int32, (experts, LANES), 1)
    store[6] = jnp.zeros(store.shape[1:], F32)
    store[6, pl.ds(0, experts, stride=16), :] = jnp.where(
        column == 0, upper, jnp.where(column == 1, counts - 64.0 * upper, 0.0)
    )
    spill_store(store, send_ref, 7, 0)


def gelu_parts(u):
    inner = 0.7978845608028654 * (u + 0.044715 * (u * u * u))
    t = jnp.tanh(inner)
    half = 0.5 * (1.0 + t)
    slope = half + 0.5 * u * (1.0 - t * t) * (0.7978845608028654 * (1.0 + 0.134145 * (u * u)))
    return u * half, slope


def expert_kernel(
    experts,
    capacity,
    blocks,
    core_ref,
    lines_ref,
    w_in_ref,
    w_out_ref,
    rows_ref,
    grads_ref,
    active_other_ref,
    active_mine_ref,
    lifted_other_ref,
    lifted_mine_ref,
    back_ref,
    store,
    total,
):
    f = pl.program_id(0)

    @pl.when(f == 0)
    def _():
        fill_store(store, lines_ref, 0, 6, 0)
        from_lines(store, rows_ref, experts, capacity, 0)
        from_lines(store, grads_ref, experts, capacity, 3)
        total[...] = jnp.zeros_like(total)

    lifted = dot(rows_ref[...], w_in_ref[...])
    grad_active = dot(grads_ref[...], w_out_ref[...], 1, 1)
    gelu, slope = gelu_parts(lifted)
    active = gelu.astype(BF16)
    grad_lifted = (grad_active * slope).astype(BF16)
    total[...] += dot(grad_lifted, w_in_ref[...], 1, 1)

    @pl.when(f < blocks // 2)
    def _():
        active_other_ref[...] = active
        lifted_other_ref[...] = grad_lifted

    @pl.when(f >= blocks // 2)
    def _():
        active_mine_ref[...] = active
        lifted_mine_ref[...] = grad_lifted

    @pl.when(f == blocks - 1)
    def _():
        to_lines(store, total, experts, capacity, 0)
        spill_store(store, back_ref, 3, 0)
        arrived = lines_ref[:, 6 * LANES : 7 * LANES].astype(F32)
        sums = jnp.sum(arrived, axis=0, keepdims=True)
        column = lax.broadcasted_iota(jnp.int32, sums.shape, 1)
        count = jnp.sum(jnp.where(column == 0, 64.0 * sums, sums), axis=1, keepdims=True)
        upper = jnp.floor(count * (1.0 / 256.0))
        pair = jnp.where(column == 0, upper, jnp.where(column == 1, count - 256.0 * upper, 0.0))
        back_ref[:, 3 * LANES : 4 * LANES] = jnp.broadcast_to(
            pair, (back_ref.shape[0], LANES)
        ).astype(BF16)


def produce_kernel(
    experts, capacity, blocks, core_ref, other_ref, mine_ref, w_out_ref, lines_ref, store, total
):
    f = pl.program_id(0)

    @pl.when(f == 0)
    def _():
        total[...] = jnp.zeros_like(total)

    @pl.when(f < blocks // 2)
    def _():
        total[...] += dot(other_ref[...], w_out_ref[...])

    @pl.when(f >= blocks // 2)
    def _():
        total[...] += dot(mine_ref[...], w_out_ref[...])

    @pl.when(f == blocks - 1)
    def _():
        to_lines(store, total, experts, capacity, 0)
        spill_store(store, lines_ref, 3, 0)


def outer_kernel(left_a, left_b, right_a, right_b, out_ref):
    out_ref[...] = dot(left_a[...], right_a[...], 0, 0) + dot(left_b[...], right_b[...], 0, 0)


def hidden_kernel(
    experts,
    capacity,
    lines_ref,
    dispatch_ref,
    hidden_ref,
    grad_ref,
    gain_ref,
    weight_ref,
    grad_hidden_ref,
    branch_ref,
    attended_ref,
    gains_ref,
    store,
    came,
    normed,
):
    rows, width = hidden_ref.shape
    fill_store(store, lines_ref, 0, 3, 0)
    from_lines(store, came, experts, capacity, 0)
    gain = gain_ref[...].astype(F32)
    normed[...] = dot(dispatch_ref[...], came[...], 0, 0)
    gains_ref[...] = jnp.zeros_like(gains_ref)
    step = 128

    def body(i, _):
        at = pl.ds(pl.multiple_of(i * step, step), step)
        scaled, scale = normalize(hidden_ref[at, :])
        grad = normed[at, :]
        grad_hidden = grad_ref[at, :].astype(F32) + norm_backward(scaled, scale, grad * gain)
        grad_hidden_ref[at, :] = grad_hidden
        branch_ref[at, :] = grad_hidden.astype(BF16)
        gains_ref[0:1, :] += jnp.sum(grad * scaled, axis=0, keepdims=True)
        gains_ref[1:2, :] += jnp.sum(grad, axis=0, keepdims=True)
        return 0

    lax.fori_loop(0, rows // step, body, 0)
    attended_ref[...] = dot(branch_ref[...], weight_ref[...], 1, 1).astype(BF16)


def attention_kernel(seq_count, group_ref, q_ref, k_ref, v_ref, grad_ref, probs_ref, out_ref):
    seq_len = q_ref.shape[0] // seq_count
    low = (lax.broadcasted_iota(jnp.int32, (1, LANES), 1) < 64).astype(F32)
    score_scale = 1.0 / math.sqrt(64)
    low_half = low.astype(BF16)
    high_half = (1.0 - low).astype(BF16)
    for s in range(seq_count):
        here = slice(s * seq_len, (s + 1) * seq_len)
        q, k, v = q_ref[here, :], k_ref[here, :], v_ref[here, :]
        grad = grad_ref[here, :]
        probs = probs_ref[s, 0]
        grad_both = jnp.concatenate([grad * low_half, grad * high_half], axis=0)
        query_both = jnp.concatenate([q * low_half, q * high_half], axis=0)
        grad_probs = dot(grad_both, v, 1, 1)
        out_ref[2, here, :] = dot(probs, grad_both, 0, 0).astype(BF16)
        wide = probs.astype(F32)
        inner = jnp.sum(wide * grad_probs, axis=-1, keepdims=True)
        grad_scores = (wide * (grad_probs - inner)).astype(BF16)
        queries = dot(grad_scores, k) * score_scale
        queries = queries[:seq_len] * low + queries[seq_len:] * (1.0 - low)
        out_ref[0, here, :] = queries.astype(BF16)
        out_ref[1, here, :] = (dot(grad_scores, query_both, 0, 0) * score_scale).astype(BF16)


def input_kernel(
    core_ref,
    mine_ref,
    other_ref,
    weight_ref,
    x_ref,
    grad_hidden_ref,
    gain_ref,
    ffn_gains_ref,
    input_grad_ref,
    small_ref,
    normed,
    gains,
):
    rows, width = x_ref.shape
    half = width // 2
    core = core_ref[0]
    total = None
    for part in range(3):
        for ref, group in ((mine_ref, core), (other_ref, 1 - core)):
            at = pl.multiple_of(part * width + group * half, half)
            term = dot(ref[part], weight_ref[:, pl.ds(at, half)], 1, 1)
            total = term if total is None else total + term
    normed[...] = total
    gain = gain_ref[...].astype(F32)
    gains[...] = jnp.zeros_like(gains)
    gains[2:4, :] = ffn_gains_ref[0:2, :]
    step = 128

    def body(i, _):
        at = pl.ds(pl.multiple_of(i * step, step), step)
        scaled, scale = normalize(x_ref[at, :].astype(F32))
        grad = normed[at, :]
        input_grad_ref[at, :] = grad_hidden_ref[at, :] + norm_backward(scaled, scale, grad * gain)
        gains[0:1, :] += jnp.sum(grad * scaled, axis=0, keepdims=True)
        gains[1:2, :] += jnp.sum(grad, axis=0, keepdims=True)
        return 0

    lax.fori_loop(0, rows // step, body, 0)
    small_ref[...] = gains[...].T


def weights_kernel(
    core_ref,
    normed_a,
    normed_b,
    attended_a,
    attended_b,
    mixed_a,
    mixed_b,
    branch_a,
    branch_b,
    small_ref,
    produced_ref,
    out_ref,
):
    half = branch_b.shape[1]
    out_ref[:, : 3 * LANES] = produced_ref[...]
    out_ref[:, 3 * LANES : 4 * LANES] = small_ref[...].astype(BF16)
    at = 4 * LANES
    for part in range(3):
        block = dot(normed_a[...], mixed_a[part], 0, 0) + dot(normed_b[...], mixed_b[part], 0, 0)
        out_ref[:, at + part * half : at + (part + 1) * half] = block.astype(BF16)
    block = dot(attended_a[...], branch_a[...], 0, 0) + dot(attended_b[...], branch_b[...], 0, 0)
    out_ref[:, at + 3 * half : at + 4 * half] = block.astype(BF16)


def sum_kernel(sources, lines_ref, out_ref):
    i = pl.program_id(0)
    wide = lines_ref[...].astype(F32)
    total = wide[0:16]
    for source in range(1, sources):
        total = total + wide[16 * source : 16 * (source + 1)]

    @pl.when(i == 0)
    def _():
        out_ref[...] = total

    @pl.when(i > 0)
    def _():
        out_ref[...] += total


def output_kernel(experts, capacity, lines_ref, dispatch_ref, hidden_ref, out_ref, store, came):
    fill_store(store, lines_ref, 0, 3, 0)
    from_lines(store, came, experts, capacity, 0)
    back = dot(dispatch_ref[...], came[...], 0, 0)
    out_ref[...] = (hidden_ref[...] + back).astype(BF16)


def whole(shape):
    return pl.BlockSpec(shape, lambda *_: (0,) * len(shape))


def shaped(shape, dtype):
    return jax.ShapeDtypeStruct(shape, dtype)


def per_device(
    block_input,
    attn_gain,
    attn_shift,
    query_key_value_weight,
    output_weight,
    ffn_gain,
    ffn_shift,
    expert_in,
    expert_out,
    hash_ids,
    seq_lengths,
    prev_counts,
    out_grad,
):
    seq_count, seq_len, width = block_input.shape
    rows = seq_count * seq_len
    chips = lax.axis_size(WIDE)
    experts = chips
    capacity = max(2, 3 * rows // (4 * experts))
    n_slots = experts * capacity
    ff_width = expert_in.shape[2]
    half_ff = ff_width // 2
    half = width // 2
    pairs = HEADS // 2
    lines = 16 * chips
    core = lax.axis_index("narrow").astype(jnp.int32)
    core_at = core.reshape(1)
    other_at = (1 - core).reshape(1)
    x = block_input.reshape(rows, width)
    grad_rows = out_grad.reshape(rows, width)
    w_in = expert_in[0]
    w_out = expert_out[0]
    smem = pl.BlockSpec(memory_space=pltpu.SMEM)
    vmem = pl.BlockSpec(memory_space=pltpu.VMEM)

    normed, mixed, probs, attended, hidden, dispatch, send = pl.pallas_call(
        functools.partial(forward_kernel, experts, capacity),
        out_shape=(
            shaped((rows, width), BF16),
            shaped((rows, 3 * width), BF16),
            shaped((seq_count, pairs, 2 * seq_len, seq_len), BF16),
            shaped((rows, width), BF16),
            shaped((rows, width), F32),
            shaped((n_slots, rows), BF16),
            shaped((lines, 7 * LANES), BF16),
        ),
        in_specs=[smem] + [vmem] * 9,
        out_specs=[vmem] * 7,
        scratch_shapes=[pltpu.VMEM((rows, width), BF16), pltpu.VMEM((7, lines, LANES), F32)],
        compiler_params=params(56),
        name="forward",
    )(
        seq_lengths,
        hash_ids,
        x,
        attn_gain.reshape(1, width),
        attn_shift.reshape(1, width),
        query_key_value_weight,
        output_weight,
        ffn_gain.reshape(1, width),
        ffn_shift.reshape(1, width),
        grad_rows,
    )
    arrived = exchanged(send)
    normed_other = swapped(normed)
    attended_other = swapped(attended)

    blocks = 8
    tile = ff_width // blocks
    per_half = blocks // 2

    def in_order(f, core_ref):
        first = f // per_half
        group = jnp.where(first == 0, 1 - core_ref[0], core_ref[0])
        return group * per_half + f % per_half

    def early(f, core_ref):
        return (0, jnp.minimum(f, per_half - 1))

    def late(f, core_ref):
        return (0, jnp.maximum(f - per_half, 0))

    row_block = whole((n_slots, width))
    half_block = shaped((n_slots, half_ff), BF16)
    rows_in, grads_in, active_other, active_mine, lifted_other, lifted_mine, back = pl.pallas_call(
        functools.partial(expert_kernel, experts, capacity, blocks),
        out_shape=(
            shaped((n_slots, width), BF16),
            shaped((n_slots, width), BF16),
            half_block,
            half_block,
            half_block,
            half_block,
            shaped((lines, 4 * LANES), BF16),
        ),
        grid_spec=pltpu.PrefetchScalarGridSpec(
            num_scalar_prefetch=1,
            grid=(blocks,),
            in_specs=[
                whole((lines, 7 * LANES)),
                pl.BlockSpec((width, tile), lambda f, c: (0, in_order(f, c))),
                pl.BlockSpec((tile, width), lambda f, c: (in_order(f, c), 0)),
            ],
            out_specs=[
                row_block,
                row_block,
                pl.BlockSpec((n_slots, tile), early),
                pl.BlockSpec((n_slots, tile), late),
                pl.BlockSpec((n_slots, tile), early),
                pl.BlockSpec((n_slots, tile), late),
                whole((lines, 4 * LANES)),
            ],
            scratch_shapes=[
                pltpu.VMEM((6, lines, LANES), F32),
                pltpu.VMEM((n_slots, width), F32),
            ],
        ),
        compiler_params=params(32),
        name="expert",
    )(core_at, arrived, w_in, w_out)
    returned = exchanged(back)

    produced = pl.pallas_call(
        functools.partial(produce_kernel, experts, capacity, blocks),
        out_shape=shaped((lines, 3 * LANES), BF16),
        grid_spec=pltpu.PrefetchScalarGridSpec(
            num_scalar_prefetch=1,
            grid=(blocks,),
            in_specs=[
                pl.BlockSpec((n_slots, tile), early),
                pl.BlockSpec((n_slots, tile), late),
                pl.BlockSpec((tile, width), lambda f, c: (in_order(f, c), 0)),
            ],
            out_specs=whole((lines, 3 * LANES)),
            scratch_shapes=[
                pltpu.VMEM((3, lines, LANES), F32),
                pltpu.VMEM((n_slots, width), F32),
            ],
        ),
        compiler_params=params(24),
        name="produce",
    )(core_at, active_other, active_mine, w_out)

    rows_other = swapped(rows_in)
    grads_other = swapped(grads_in)
    active_came = swapped(active_other)
    lifted_came = swapped(lifted_other)
    tile = half_ff // 4
    column = pl.BlockSpec((n_slots, tile), lambda f: (0, f))
    expert_out_grad = pl.pallas_call(
        outer_kernel,
        out_shape=shaped((half_ff, width), F32),
        grid=(4,),
        in_specs=[column, column, row_block, row_block],
        out_specs=pl.BlockSpec((tile, width), lambda f: (f, 0)),
        compiler_params=params(24),
        name="expert_out_grad",
    )(active_mine, active_came, grads_in, grads_other)
    returned, produced, expert_out_grad = lax.optimization_barrier(
        (returned, produced, expert_out_grad)
    )

    grad_hidden, branch, grad_attended, ffn_gains = pl.pallas_call(
        functools.partial(hidden_kernel, experts, capacity),
        out_shape=(
            shaped((rows, width), F32),
            shaped((rows, width), BF16),
            shaped((rows, width), BF16),
            shaped((8, width), F32),
        ),
        in_specs=[vmem] * 6,
        out_specs=[vmem] * 4,
        scratch_shapes=[
            pltpu.VMEM((3, lines, LANES), F32),
            pltpu.VMEM((n_slots, width), BF16),
            pltpu.VMEM((rows, width), F32),
        ],
        compiler_params=params(40),
        name="hidden_backward",
    )(returned[:, : 3 * LANES], dispatch, hidden, grad_rows, ffn_gain.reshape(1, width), output_weight)
    branch_out = lax.dynamic_slice_in_dim(branch, (1 - core) * half, half, 1)
    branch_other = swapped(branch_out)

    def attention_backward(group):
        def column_of(part):
            return pl.BlockSpec(
                (rows, LANES), lambda p, g: (0, part * pairs + g[0] * (pairs // 2) + p)
            )

        return pl.pallas_call(
            functools.partial(attention_kernel, seq_count),
            out_shape=shaped((3, rows, half), BF16),
            grid_spec=pltpu.PrefetchScalarGridSpec(
                num_scalar_prefetch=1,
                grid=(pairs // 2,),
                in_specs=[
                    column_of(0),
                    column_of(1),
                    column_of(2),
                    column_of(0),
                    pl.BlockSpec(
                        (seq_count, 1, 2 * seq_len, seq_len),
                        lambda p, g: (0, g[0] * (pairs // 2) + p, 0, 0),
                    ),
                ],
                out_specs=pl.BlockSpec((3, rows, LANES), lambda p, g: (0, 0, p)),
            ),
            compiler_params=params(24),
            name="attention_backward",
        )(group, mixed, mixed, mixed, grad_attended, probs)

    mixed_out = attention_backward(other_at)
    mixed_came = swapped(mixed_out)
    mixed_mine = attention_backward(core_at)

    input_grad, small = pl.pallas_call(
        input_kernel,
        out_shape=(shaped((rows, width), F32), shaped((width, LANES), F32)),
        in_specs=[smem] + [vmem] * 7,
        out_specs=[vmem] * 2,
        scratch_shapes=[pltpu.VMEM((rows, width), F32), pltpu.VMEM((LANES, width), F32)],
        compiler_params=params(40),
        name="input_backward",
    )(
        core_at,
        mixed_mine,
        mixed_out,
        query_key_value_weight,
        x,
        grad_hidden,
        attn_gain.reshape(1, width),
        ffn_gains,
    )

    tail_lanes = 4 * LANES + 4 * half
    block = width // 4
    column = pl.BlockSpec((rows, block), lambda i, c: (0, i))
    tail = pl.pallas_call(
        weights_kernel,
        out_shape=shaped((width, tail_lanes), BF16),
        grid_spec=pltpu.PrefetchScalarGridSpec(
            num_scalar_prefetch=1,
            grid=(4,),
            in_specs=[
                column,
                column,
                column,
                column,
                whole((3, rows, half)),
                whole((3, rows, half)),
                pl.BlockSpec((rows, half), lambda i, c: (0, c[0])),
                whole((rows, half)),
                pl.BlockSpec((block, LANES), lambda i, c: (i, 0)),
                pl.BlockSpec((block, 3 * LANES), lambda i, c: (i, 0)),
            ],
            out_specs=pl.BlockSpec((block, tail_lanes), lambda i, c: (i, 0)),
        ),
        compiler_params=params(40),
        name="weight_gradients",
    )(
        core_at,
        normed,
        normed_other,
        attended,
        attended_other,
        mixed_mine,
        mixed_came,
        branch,
        branch_other,
        small,
        produced,
    )
    landed = exchanged(tail)
    tail, rows_in, lifted_mine = lax.optimization_barrier((tail, rows_in, lifted_mine))
    column = pl.BlockSpec((n_slots, tile), lambda f: (0, f))
    expert_in_grad = pl.pallas_call(
        outer_kernel,
        out_shape=shaped((width, half_ff), F32),
        grid=(4,),
        in_specs=[row_block, row_block, column, column],
        out_specs=pl.BlockSpec((width, tile), lambda f: (0, f)),
        compiler_params=params(24),
        name="expert_in_grad",
    )(rows_in, rows_other, lifted_mine, lifted_came)

    steps = 8
    summed = pl.pallas_call(
        functools.partial(sum_kernel, chips // steps),
        out_shape=shaped((16, tail_lanes), F32),
        grid=(steps,),
        in_specs=[pl.BlockSpec((lines // steps, tail_lanes), lambda i: (i, 0))],
        out_specs=whole((16, tail_lanes)),
        compiler_params=params(24),
        name="sum",
    )(landed)
    summed = summed[:, 3 * LANES :]
    own = lax.dynamic_slice_in_dim(summed, core * 8, 8, 0)
    came = swapped(lax.dynamic_slice_in_dim(summed, (1 - core) * 8, 8, 0))
    vectors = own[:, :4] + came[:, :4]
    own = own[:, LANES:].reshape(8, 4, 1, half)
    came = came[:, LANES:].reshape(8, 4, 1, half)
    joined = jnp.where(
        core == 0,
        jnp.concatenate([own, came], axis=2),
        jnp.concatenate([came, own], axis=2),
    ).reshape(8, 4 * width)

    block_output = pl.pallas_call(
        functools.partial(output_kernel, experts, capacity),
        out_shape=shaped((rows, width), BF16),
        grid=(1,),
        in_specs=[
            whole((lines, 3 * LANES)),
            whole((n_slots, rows)),
            whole((rows, width)),
        ],
        out_specs=whole((rows, width)),
        scratch_shapes=[
            pltpu.VMEM((3, lines, LANES), F32),
            pltpu.VMEM((n_slots, width), BF16),
        ],
        compiler_params=params(32),
        name="block_output",
    )(landed, dispatch, hidden)

    pair = returned[:, 3 * LANES : 3 * LANES + 2].reshape(chips, 16, 2)[:, 0].astype(F32)
    counts = 256.0 * pair[:, 0] + pair[:, 1]
    counts = counts + swapped(counts)
    total_tokens = float(rows * chips * 2)
    new_average = (momentum * prev_counts.astype(F32) + (1.0 - momentum) * counts) * (
        float(experts) / total_tokens
    )
    return (
        block_output.reshape(seq_count, seq_len, width),
        input_grad.reshape(seq_count, seq_len, width),
        vectors[:, 0],
        vectors[:, 1],
        joined[:, : 3 * width],
        joined[:, 3 * width :],
        vectors[:, 2],
        vectors[:, 3],
        expert_in_grad[None],
        expert_out_grad[None],
        new_average,
    )


def solution(mesh):
    finer = Mesh(
        mesh.devices.reshape(4, 4, 4, mesh.shape["narrow"]),
        ("wide_0", "wide_1", "wide_2", "narrow"),
    )
    placed = (
        P(WIDE_NARROW, None, None),
        P(),
        P(),
        P(),
        P(),
        P(),
        P(),
        P(WIDE, None, None),
        P(WIDE, None, None),
        P(WIDE_NARROW, None),
        P(WIDE_NARROW),
        P(),
        P(WIDE_NARROW, None, None),
    )
    return jax.shard_map(
        per_device,
        mesh=finer,
        in_specs=placed,
        out_specs=(
            P(WIDE_NARROW, None, None),
            P(WIDE_NARROW, None, None),
            P(WIDE_NARROW),
            P(WIDE_NARROW),
            P(WIDE_NARROW, None),
            P(WIDE_NARROW, None),
            P(WIDE_NARROW),
            P(WIDE_NARROW),
            P(WIDE, None, "narrow"),
            P(WIDE, "narrow", None),
            P(),
        ),
        check_vma=False,
    )
```

```python
import functools
import math

import jax
import jax.experimental.pallas as pl
import jax.experimental.pallas.tpu as pltpu
import jax.numpy as jnp
from jax import lax
from jax.sharding import Mesh
from jax.sharding import PartitionSpec as P

HEADS = 16
WIDE = ("wide_0", "wide_1", "wide_2")
WIDE_NARROW = ("wide_0", "wide_1", "wide_2", "narrow")

norm_eps = 1e-05
momentum = 0.9
F32 = jnp.float32
BF16 = jnp.bfloat16
LANES = 128
MIB = 1 << 20


def swapped(shard):
    return lax.ppermute(shard, "narrow", [(0, 1), (1, 0)])


def exchanged(lines):
    shard = lines.reshape(lax.axis_size(WIDE), -1, lines.shape[1])
    return lax.all_to_all(shard, WIDE, 0, 0, tiled=True).reshape(lines.shape)


def crossed(shard, axis, first):
    pairs = []
    for i in range(lax.axis_size(WIDE[axis])):
        for core in range(2):
            flip = 1 if first == (core == 0) else 3
            pairs.append((i * 2 + core, (i ^ flip) * 2 + core))
    return lax.ppermute(shard, (WIDE[axis], "narrow"), pairs)


def dot(left, right, left_dim=1, right_dim=0):
    return lax.dot_general(
        left, right, (((left_dim,), (right_dim,)), ((), ())), preferred_element_type=F32
    )


def params(mib):
    return pltpu.CompilerParams(vmem_limit_bytes=mib * MIB)


def cost(gigaflops, megabytes):
    return pl.CostEstimate(
        flops=int(gigaflops * 1e9), bytes_accessed=int(megabytes * 1e6), transcendentals=0
    )


def normalize(features):
    centered = features - jnp.mean(features, axis=-1, keepdims=True)
    spread = jnp.mean(centered * centered, axis=-1, keepdims=True)
    scale = lax.rsqrt(spread + norm_eps)
    return centered * scale, scale


def as_row(tile_ref):
    tile = tile_ref[...].astype(F32)
    return jnp.concatenate([tile[i : i + 1, :] for i in range(tile.shape[0])], axis=1)


def norm_backward(scaled, scale, gained):
    mean = jnp.mean(gained, axis=-1, keepdims=True)
    along = jnp.mean(gained * scaled, axis=-1, keepdims=True)
    return scale * (gained - mean - scaled * along)


def to_lines(store, rows, experts, capacity, lane_tile):
    for rank in range(capacity):
        for part in range(8):
            at = rank % 2 * 8 + part
            store[lane_tile + rank // 2, pl.ds(at, experts, stride=16), :] = rows[
                rank * experts : (rank + 1) * experts, part * LANES : (part + 1) * LANES
            ]


def from_lines(store, rows_ref, experts, capacity, lane_tile):
    for rank in range(capacity):
        for part in range(8):
            at = rank % 2 * 8 + part
            rows_ref[
                rank * experts : (rank + 1) * experts, part * LANES : (part + 1) * LANES
            ] = store[lane_tile + rank // 2, pl.ds(at, experts, stride=16), :].astype(BF16)


def fill_store(store, lines_ref, lane_tile, count, source_tile):
    for tile in range(count):
        at = (source_tile + tile) * LANES
        store[lane_tile + tile] = lines_ref[:, at : at + LANES].astype(F32)


def spill_store(store, lines_ref, count, target_tile):
    for tile in range(count):
        at = (target_tile + tile) * LANES
        lines_ref[:, at : at + LANES] = store[tile].astype(BF16)


def forward_kernel(
    experts,
    capacity,
    len_ref,
    ids_ref,
    x_ref,
    gain_one_ref,
    shift_one_ref,
    gain_two_ref,
    shift_two_ref,
    qkv_weight_hbm,
    out_weight_hbm,
    grad_hbm,
    normed_hbm,
    mixed_hbm,
    probs_hbm,
    attended_hbm,
    hidden_hbm,
    dispatch_ref,
    send_ref,
    qkv_weight_ref,
    out_weight_ref,
    grad_ref,
    normed_ref,
    mixed_ref,
    probs_ref,
    attended_ref,
    hidden_ref,
    moved_ref,
    store,
    sems,
):
    rows, width = x_ref.shape
    seq_count, seq_len = ids_ref.shape
    pieces = 3
    span = 3 * width // pieces

    def fetch(i):
        at = slice(i * span, (i + 1) * span)
        return pltpu.make_async_copy(qkv_weight_hbm.at[:, at], qkv_weight_ref.at[:, at], sems.at[i])

    out_weight_copy = pltpu.make_async_copy(out_weight_hbm, out_weight_ref, sems.at[3])
    grad_copy = pltpu.make_async_copy(grad_hbm, grad_ref, sems.at[4])
    for i in range(pieces):
        fetch(i).start()
    out_weight_copy.start()
    grad_copy.start()
    normed_copy = pltpu.make_async_copy(normed_ref, normed_hbm, sems.at[5])
    mixed_copy = pltpu.make_async_copy(mixed_ref, mixed_hbm, sems.at[6])
    probs_copy = pltpu.make_async_copy(probs_ref, probs_hbm, sems.at[7])
    attended_copy = pltpu.make_async_copy(attended_ref, attended_hbm, sems.at[8])
    hidden_copy = pltpu.make_async_copy(hidden_ref, hidden_hbm, sems.at[9])

    gain_one, shift_one = as_row(gain_one_ref), as_row(shift_one_ref)
    gain_two, shift_two = as_row(gain_two_ref), as_row(shift_two_ref)
    step = 128

    def norm_one(i, _):
        at = pl.ds(pl.multiple_of(i * step, step), step)
        scaled, _ = normalize(x_ref[at, :].astype(F32))
        normed_ref[at, :] = (scaled * gain_one + shift_one).astype(BF16)
        return 0

    lax.fori_loop(0, rows // step, norm_one, 0, unroll=2)
    normed_copy.start()

    ids = jnp.concatenate([ids_ref[s : s + 1, :] for s in range(seq_count)], axis=1)
    lane = lax.broadcasted_iota(jnp.int32, (1, rows), 1)
    length = jnp.where(lane < seq_len, len_ref[0], len_ref[1])
    is_valid = lane % seq_len < length
    member = (lax.broadcasted_iota(jnp.int32, (experts, rows), 0) == ids) & is_valid
    onehot = member.astype(F32)
    earlier = (
        lax.broadcasted_iota(jnp.int32, (rows, rows), 0)
        < lax.broadcasted_iota(jnp.int32, (rows, rows), 1)
    ).astype(F32)
    before = dot(onehot.astype(BF16), earlier.astype(BF16))
    rank = jnp.sum(onehot * before, axis=0, keepdims=True).astype(jnp.int32)
    slot = jnp.where(is_valid & (rank < capacity), rank * experts + ids, -1)
    at_slot = lax.broadcasted_iota(jnp.int32, (experts * capacity, rows), 0)
    dispatch_ref[...] = (at_slot == slot).astype(F32).astype(BF16)
    counts = jnp.sum(onehot, axis=1, keepdims=True)
    upper = jnp.floor(counts * (1.0 / 64.0))
    column = lax.broadcasted_iota(jnp.int32, (experts, LANES), 1)
    store[6] = jnp.zeros(store.shape[1:], F32)
    store[6, pl.ds(0, experts, stride=16), :] = jnp.where(
        column == 0, upper, jnp.where(column == 1, counts - 64.0 * upper, 0.0)
    )

    for i in range(pieces):
        fetch(i).wait()

        def project(j, _):
            at = pl.ds(pl.multiple_of(i * span + j * 512, 512), 512)
            block = dot(normed_ref[...], qkv_weight_ref[:, at]).astype(BF16)
            for tile in range(4):
                mixed_ref[(i * span + j * 512) // LANES + tile] = block[
                    :, tile * LANES : (tile + 1) * LANES
                ]
            return 0

        lax.fori_loop(0, span // 512, project, 0)
    mixed_copy.start()

    pairs = HEADS // 2
    low = (lax.broadcasted_iota(jnp.int32, (1, LANES), 1) < 64).astype(F32)
    score_scale = 1.0 / math.sqrt(width // HEADS)
    low_scaled = (low * score_scale).astype(BF16)
    high_scaled = ((1.0 - low) * score_scale).astype(BF16)
    query_at = lax.broadcasted_iota(jnp.int32, (2 * seq_len, seq_len), 0) % seq_len
    key_at = lax.broadcasted_iota(jnp.int32, (2 * seq_len, seq_len), 1)

    def attend(p, _):
        at = pl.multiple_of(p * LANES, LANES)
        for s in range(seq_count):
            here = slice(s * seq_len, (s + 1) * seq_len)
            allowed = (key_at <= query_at) & (key_at < len_ref[s])
            q = mixed_ref[p, here, :]
            k = mixed_ref[pairs + p, here, :]
            v = mixed_ref[2 * pairs + p, here, :]
            both = jnp.concatenate([q * low_scaled, q * high_scaled], axis=0)
            scores = jnp.where(allowed, dot(both, k, 1, 1), -1000000000.0)
            raised = jnp.exp(scores - jnp.max(scores, axis=-1, keepdims=True))
            total = jnp.sum(raised, axis=-1, keepdims=True)
            probs = (raised * (1.0 / total)).astype(BF16)
            probs_ref[s, p] = probs
            out = dot(probs, v)
            out = out[:seq_len] * low + out[seq_len:] * (1.0 - low)
            attended_ref[here, pl.ds(at, LANES)] = out.astype(BF16)
        return 0

    lax.fori_loop(0, pairs, attend, 0, unroll=2)
    probs_copy.start()
    attended_copy.start()

    out_weight_copy.wait()

    def norm_two(i, _):
        at = pl.ds(pl.multiple_of(i * 256, 256), 256)
        hidden = x_ref[at, :].astype(F32) + dot(attended_ref[at, :], out_weight_ref[...])
        hidden_ref[at, :] = hidden
        scaled, _ = normalize(hidden)
        moved_ref[at, :] = (scaled * gain_two + shift_two).astype(BF16)
        return 0

    lax.fori_loop(0, rows // 256, norm_two, 0)
    hidden_copy.start()

    grad_copy.wait()
    to_lines(store, dot(dispatch_ref[...], grad_ref[...]), experts, capacity, 3)
    to_lines(store, dot(dispatch_ref[...], moved_ref[...]), experts, capacity, 0)
    spill_store(store, send_ref, 7, 0)
    for copy in (normed_copy, mixed_copy, probs_copy, attended_copy, hidden_copy):
        copy.wait()


def places(position, core):
    near = 1 + 2 * core
    return jnp.where(
        position == 0,
        0,
        jnp.where(position == 1, 4 - near, jnp.where(position == 2, near, 2)),
    )


def order_matrix(at_ref):
    line = lax.broadcasted_iota(jnp.int32, (256, 256), 0)
    column = lax.broadcasted_iota(jnp.int32, (256, 256), 1)
    core, z, y = at_ref[0], at_ref[2], at_ref[3]
    source_z = places(line // 64, core) ^ z
    source_y = places(line // 16 % 4, core) ^ y
    return (column == source_z * 64 + source_y * 16 + line % 16).astype(F32)


def prepare_kernel(
    at_ref,
    normed_a,
    normed_b,
    attended_a,
    attended_b,
    query_ref,
    key_ref,
    value_ref,
    gain_ref,
    shift_ref,
    normed_ref,
    attended_ref,
    weight_ref,
    scale_ref,
):
    order = order_matrix(at_ref).astype(BF16)
    rows = normed_a.shape[0]
    normed_ref[:, :rows] = dot(order, normed_a[...], 1, 1).astype(BF16)
    normed_ref[:, rows:] = dot(order, normed_b[...], 1, 1).astype(BF16)
    attended_ref[:, :rows] = dot(order, attended_a[...], 1, 1).astype(BF16)
    attended_ref[:, rows:] = dot(order, attended_b[...], 1, 1).astype(BF16)
    half = query_ref.shape[1]
    for part, ref in enumerate((query_ref, key_ref, value_ref)):
        weight_ref[:, part * half : (part + 1) * half] = dot(order, ref[...]).astype(BF16)
    tile_at = 2 * at_ref[4 + pl.program_id(0)]
    tile = lax.broadcasted_iota(jnp.int32, (8, LANES), 0)
    line = lax.broadcasted_iota(jnp.int32, (LANES, 256), 0)

    def columns(ref):
        wide = ref[...].astype(F32)
        parts = [
            jnp.sum(jnp.where(tile == tile_at + i, wide, 0.0), axis=0, keepdims=True)
            for i in range(2)
        ]
        return jnp.concatenate(parts, axis=1)

    both = jnp.where(line == 0, columns(gain_ref), jnp.where(line == 1, columns(shift_ref), 0.0))
    scale_ref[...] = dot(order, both.astype(BF16), 1, 1)


def gelu_parts(u):
    inner = 0.7978845608028654 * (u + 0.044715 * (u * u * u))
    t = jnp.tanh(inner)
    half = 0.5 * (1.0 + t)
    slope = half + 0.5 * u * (1.0 - t * t) * (0.7978845608028654 * (1.0 + 0.134145 * (u * u)))
    return u * half, slope


def expert_kernel(
    experts,
    capacity,
    blocks,
    core_ref,
    lines_ref,
    w_in_ref,
    w_out_ref,
    rows_ref,
    grads_ref,
    active_other_ref,
    active_mine_ref,
    lifted_other_ref,
    lifted_mine_ref,
    back_ref,
    store,
    total,
    produced,
):
    f = pl.program_id(0)

    @pl.when(f == 0)
    def _():
        fill_store(store, lines_ref, 0, 6, 0)
        from_lines(store, rows_ref, experts, capacity, 0)
        from_lines(store, grads_ref, experts, capacity, 3)
        total[...] = jnp.zeros_like(total)
        produced[...] = jnp.zeros_like(produced)

    lifted = dot(rows_ref[...], w_in_ref[...])
    grad_active = dot(grads_ref[...], w_out_ref[...], 1, 1)
    gelu, slope = gelu_parts(lifted)
    active = gelu.astype(BF16)
    grad_lifted = (grad_active * slope).astype(BF16)
    total[...] += dot(grad_lifted, w_in_ref[...], 1, 1)
    produced[...] += dot(active, w_out_ref[...])

    @pl.when(f < blocks // 2)
    def _():
        active_other_ref[...] = active
        lifted_other_ref[...] = grad_lifted

    @pl.when(f >= blocks // 2)
    def _():
        active_mine_ref[...] = active
        lifted_mine_ref[...] = grad_lifted

    @pl.when(f == blocks - 1)
    def _():
        to_lines(store, total, experts, capacity, 0)
        to_lines(store, produced, experts, capacity, 3)
        spill_store(store, back_ref, 6, 0)
        arrived = lines_ref[:, 6 * LANES : 7 * LANES].astype(F32)
        sums = jnp.sum(arrived, axis=0, keepdims=True)
        column = lax.broadcasted_iota(jnp.int32, sums.shape, 1)
        count = jnp.sum(jnp.where(column == 0, 64.0 * sums, sums), axis=1, keepdims=True)
        upper = jnp.floor(count * (1.0 / 256.0))
        pair = jnp.where(column == 0, upper, jnp.where(column == 1, count - 256.0 * upper, 0.0))
        back_ref[:, 6 * LANES : 7 * LANES] = jnp.broadcast_to(
            pair, (back_ref.shape[0], LANES)
        ).astype(BF16)


def outer_kernel(left_a, left_b, right_a, right_b, out_ref):
    out_ref[...] = dot(left_a[...], right_a[...], 0, 0) + dot(left_b[...], right_b[...], 0, 0)


def attention_pair(q, k, v, grad, probs):
    seq_len = q.shape[0]
    low = (lax.broadcasted_iota(jnp.int32, (1, LANES), 1) < 64).astype(F32)
    score_scale = 1.0 / math.sqrt(64)
    low_half = low.astype(BF16)
    high_half = (1.0 - low).astype(BF16)
    grad_both = jnp.concatenate([grad * low_half, grad * high_half], axis=0)
    query_both = jnp.concatenate([q * low_half, q * high_half], axis=0)
    grad_probs = dot(grad_both, v, 1, 1)
    values = dot(probs, grad_both, 0, 0)
    wide = probs.astype(F32)
    inner = jnp.sum(wide * grad_probs, axis=-1, keepdims=True)
    grad_scores = (wide * (grad_probs - inner)).astype(BF16)
    queries = dot(grad_scores, k) * score_scale
    queries = queries[:seq_len] * low + queries[seq_len:] * (1.0 - low)
    keys = dot(grad_scores, query_both, 0, 0) * score_scale
    return queries.astype(BF16), keys.astype(BF16), values.astype(BF16)


def hidden_kernel(
    experts,
    capacity,
    at_ref,
    lines_ref,
    dispatch_ref,
    gain_ref,
    hidden_hbm,
    grad_hbm,
    weight_hbm,
    mixed_hbm,
    probs_hbm,
    grad_hidden_hbm,
    branch_mine_ref,
    branch_other_ref,
    attended_hbm,
    gains_ref,
    out_ref,
    store,
    came,
    normed,
    branch_ref,
    hidden_ref,
    grad_ref,
    weight_ref,
    mixed_ref,
    probs_ref,
    grad_hidden_ref,
    attended_ref,
    sems,
):
    rows, width = hidden_ref.shape
    seq_count = probs_ref.shape[0]
    seq_len = rows // seq_count
    pairs = probs_ref.shape[1]
    half = width // 2
    core = at_ref[0]
    other = (1 - core) * pairs
    copies = [
        pltpu.make_async_copy(hidden_hbm, hidden_ref, sems.at[0]),
        pltpu.make_async_copy(grad_hbm, grad_ref, sems.at[1]),
        pltpu.make_async_copy(weight_hbm, weight_ref, sems.at[2]),
    ]
    for part in range(3):
        copies.append(
            pltpu.make_async_copy(
                mixed_hbm.at[pl.ds(2 * part * pairs + other, pairs)],
                mixed_ref.at[part],
                sems.at[3 + part],
            )
        )
    for s in range(seq_count):
        copies.append(
            pltpu.make_async_copy(
                probs_hbm.at[s, pl.ds(other, pairs)], probs_ref.at[s], sems.at[6 + s]
            )
        )
    for copy in copies:
        copy.start()
    grad_hidden_copy = pltpu.make_async_copy(grad_hidden_ref, grad_hidden_hbm, sems.at[8])
    attended_copy = pltpu.make_async_copy(attended_ref, attended_hbm, sems.at[9])

    fill_store(store, lines_ref, 0, 3, 0)
    from_lines(store, came, experts, capacity, 0)
    gain = as_row(gain_ref)
    normed[...] = dot(dispatch_ref[...], came[...], 0, 0)
    gains_ref[...] = jnp.zeros_like(gains_ref)
    step = 128
    copies[0].wait()
    copies[1].wait()

    def body(i, _):
        at = pl.ds(pl.multiple_of(i * step, step), step)
        scaled, scale = normalize(hidden_ref[at, :])
        grad = normed[at, :]
        grad_hidden = grad_ref[at, :].astype(F32) + norm_backward(scaled, scale, grad * gain)
        grad_hidden_ref[at, :] = grad_hidden
        branch_ref[at, :] = grad_hidden.astype(BF16)
        gains_ref[0:1, :] += jnp.sum(grad * scaled, axis=0, keepdims=True)
        gains_ref[1:2, :] += jnp.sum(grad, axis=0, keepdims=True)
        return 0

    lax.fori_loop(0, rows // step, body, 0, unroll=2)
    grad_hidden_copy.start()
    branch_mine_ref[...] = branch_ref[:, pl.ds(pl.multiple_of(core * half, half), half)]
    branch_other_ref[...] = branch_ref[:, pl.ds(pl.multiple_of((1 - core) * half, half), half)]
    copies[2].wait()
    grad_attended = dot(branch_ref[...], weight_ref[...], 1, 1).astype(BF16)
    for tile in range(2 * pairs):
        attended_ref[tile] = grad_attended[:, tile * LANES : (tile + 1) * LANES]
    attended_copy.start()
    for copy in copies[3:]:
        copy.wait()

    def pair(p, _):
        for s in range(seq_count):
            here = slice(s * seq_len, (s + 1) * seq_len)
            grads = attention_pair(
                mixed_ref[0, p, here, :],
                mixed_ref[1, p, here, :],
                mixed_ref[2, p, here, :],
                attended_ref[other + p, here, :],
                probs_ref[s, p],
            )
            for part in range(3):
                out_ref[part, p, here, :] = grads[part]
        return 0

    lax.fori_loop(0, pairs, pair, 0)
    grad_hidden_copy.wait()
    attended_copy.wait()


def attention_kernel(seq_count, at_ref, q_ref, k_ref, v_ref, grad_ref, probs_ref, out_ref):
    seq_len = q_ref.shape[1] // seq_count
    for s in range(seq_count):
        here = slice(s * seq_len, (s + 1) * seq_len)
        grads = attention_pair(
            q_ref[0, here, :],
            k_ref[0, here, :],
            v_ref[0, here, :],
            grad_ref[0, here, :],
            probs_ref[s, 0],
        )
        for part in range(3):
            out_ref[part, 0, here, :] = grads[part]


def all_lanes(tiles):
    return jnp.concatenate([tiles[i] for i in range(tiles.shape[0])], axis=1)


def input_kernel(
    at_ref,
    mine_ref,
    other_ref,
    gain_ref,
    weight_hbm,
    x_hbm,
    grad_hidden_hbm,
    input_grad_hbm,
    weight_ref,
    x_ref,
    grad_hidden_ref,
    normed,
    sems,
):
    rows, width = x_ref.shape
    half = width // 2
    core = at_ref[0]
    chunks = []
    for part in range(3):
        at = slice(part * width, (part + 1) * width)
        chunks.append(
            pltpu.make_async_copy(weight_hbm.at[:, at], weight_ref.at[:, at], sems.at[part])
        )
    x_copy = pltpu.make_async_copy(x_hbm, x_ref, sems.at[3])
    grad_copy = pltpu.make_async_copy(grad_hidden_hbm, grad_hidden_ref, sems.at[4])
    for copy in (*chunks, x_copy, grad_copy):
        copy.start()
    total = None
    for part in range(3):
        chunks[part].wait()
        for ref, group in ((mine_ref, core), (other_ref, 1 - core)):
            at = pl.multiple_of(part * width + group * half, half)
            term = dot(all_lanes(ref[part]), weight_ref[:, pl.ds(at, half)], 1, 1)
            total = term if total is None else total + term
    normed[...] = total
    gain = as_row(gain_ref)
    x_copy.wait()
    grad_copy.wait()
    step = 128
    out_copies = []
    for i in range(rows // step):
        at = slice(i * step, (i + 1) * step)
        scaled, scale = normalize(x_ref[at, :].astype(F32))
        grad_hidden_ref[at, :] += norm_backward(scaled, scale, normed[at, :] * gain)
        out_copies.append(
            pltpu.make_async_copy(grad_hidden_ref.at[at], input_grad_hbm.at[at], sems.at[5 + i])
        )
        out_copies[-1].start()
    for copy in out_copies:
        copy.wait()


def weights_kernel(
    at_ref,
    normed_ref,
    attended_ref,
    mixed_a,
    mixed_b,
    branch_a,
    branch_b,
    weight_ref,
    scale_ref,
    ffn_gains_ref,
    send_x,
    keep_x,
    send_z,
    keep_z,
    send_y,
    keep_y,
    sums,
):
    rows, half = branch_b.shape
    step = pl.program_id(0)
    size = normed_ref.shape[0]

    @pl.when(step == 0)
    def _():
        for part in range(3):
            total = jnp.zeros((1, half), F32)
            for ref in (mixed_a, mixed_b):
                for at in range(0, rows, 128):
                    wide = all_lanes(ref[part, :, at : at + 128, :]).astype(F32)
                    total = total + jnp.sum(wide, axis=0, keepdims=True)
            sums[part : part + 1, :] = total

    lane = lax.broadcasted_iota(jnp.int32, (size, LANES), 1)
    gain = jnp.zeros((size, 1), F32)
    shift = jnp.zeros((size, 1), F32)
    parts = []
    for part in range(3):
        block = dot(normed_ref[:, :rows], all_lanes(mixed_a[part]))
        block = block + dot(normed_ref[:, rows:], all_lanes(mixed_b[part]))
        weight = weight_ref[:, part * half : (part + 1) * half].astype(F32)
        gain = gain + jnp.sum(block * weight, axis=1, keepdims=True)
        shift = shift + jnp.sum(sums[part : part + 1, :] * weight, axis=1, keepdims=True)
        parts.append(block.astype(BF16))
    out = dot(attended_ref[:, :rows], branch_a[...]) + dot(attended_ref[:, rows:], branch_b[...])
    out = out.astype(BF16)
    scale = scale_ref[...]
    gain = (gain - scale[:, 1:2] * shift) / scale[:, 0:1]
    order = order_matrix(at_ref)
    ffn = []
    for i in range(size // 256):
        block_at = at_ref[4 + step * (size // 256) + i]
        ffn.append(
            lax.dot_general(
                order,
                ffn_gains_ref[:, pl.ds(pl.multiple_of(block_at * 256, 256), 256)],
                (((1,), (1,)), ((), ())),
                precision=lax.Precision.HIGHEST,
                preferred_element_type=F32,
            )
        )
    ffn = jnp.concatenate(ffn, axis=0)
    small = jnp.where(lane == 0, gain, jnp.where(lane == 1, shift, 0.0))
    small = jnp.where(lane == 2, ffn[:, 0:1], jnp.where(lane == 3, ffn[:, 1:2], small))
    small = small.astype(BF16)

    @pl.when(step == 0)
    def _():
        keep_x[:, :half] = parts[0]
        keep_x[:, half:] = out[:, : half // 2]

    @pl.when(step == 1)
    def _():
        send_x[:, :half] = parts[0]
        send_x[:, half:] = out[:, : half // 2]

    side = out[:, half // 2 : 3 * half // 4]
    for group in range(size // 16):
        x, chip = group // 16, group % 16
        here = slice(group * 16, (group + 1) * 16)
        ref = keep_z if chip < 8 else send_z
        ref[chip % 8, x, :, :half] = parts[1][here]
        ref[chip % 8, x, :, half:] = side[here]
    side = out[:, 3 * half // 4 :]
    for group in range(size // 16):
        x, z, y = group // 16, group // 4 % 4, group % 4
        here = slice(group * 16, (group + 1) * 16)
        ref = keep_y if y < 2 else send_y
        ref[y % 2, x, z, :, :half] = parts[2][here]
        ref[y % 2, x, z, :, half : half + LANES] = side[here]
        ref[y % 2, x, z, :, half + LANES :] = small[here]


def output_kernel(experts, capacity, lines_ref, dispatch_ref, hidden_ref, out_ref, store, came):
    fill_store(store, lines_ref, 0, 3, 3)
    from_lines(store, came, experts, capacity, 0)
    back = dot(dispatch_ref[...], came[...], 0, 0)
    out_ref[...] = (hidden_ref[...] + back).astype(BF16)


def whole(shape):
    return pl.BlockSpec(shape, lambda *_: (0,) * len(shape))


def shaped(shape, dtype):
    return jax.ShapeDtypeStruct(shape, dtype)


def per_device(
    block_input,
    attn_gain,
    attn_shift,
    query_key_value_weight,
    output_weight,
    ffn_gain,
    ffn_shift,
    expert_in,
    expert_out,
    hash_ids,
    seq_lengths,
    prev_counts,
    out_grad,
):
    seq_count, seq_len, width = block_input.shape
    rows = seq_count * seq_len
    chips = lax.axis_size(WIDE)
    experts = chips
    capacity = max(2, 3 * rows // (4 * experts))
    n_slots = experts * capacity
    ff_width = expert_in.shape[2]
    half_ff = ff_width // 2
    half = width // 2
    pairs = HEADS // 2
    lines = 16 * chips
    core = lax.axis_index("narrow").astype(jnp.int32)
    core_at = core.reshape(1)
    other_at = (1 - core).reshape(1)
    x = block_input.reshape(rows, width)
    grad_rows = out_grad.reshape(rows, width)
    w_in = expert_in[0]
    w_out = expert_out[0]
    scales = [v.reshape(8, LANES) for v in (attn_gain, attn_shift, ffn_gain, ffn_shift)]
    smem = pl.BlockSpec(memory_space=pltpu.SMEM)
    vmem = pl.BlockSpec(memory_space=pltpu.VMEM)
    hbm = pl.BlockSpec(memory_space=pl.ANY)
    coordinates = [lax.axis_index(name).astype(jnp.int32) for name in WIDE]
    blocks_x = [places(place, core) ^ coordinates[0] for place in range(4)]
    spot = jnp.stack([core] + coordinates + blocks_x).astype(jnp.int32)

    normed, mixed, probs, attended, hidden, dispatch, send = pl.pallas_call(
        functools.partial(forward_kernel, experts, capacity),
        out_shape=(
            shaped((rows, width), BF16),
            shaped((3 * pairs, rows, LANES), BF16),
            shaped((seq_count, pairs, 2 * seq_len, seq_len), BF16),
            shaped((rows, width), BF16),
            shaped((rows, width), F32),
            shaped((n_slots, rows), BF16),
            shaped((lines, 7 * LANES), BF16),
        ),
        in_specs=[smem] + [vmem] * 6 + [hbm] * 3,
        out_specs=[hbm] * 5 + [vmem] * 2,
        scratch_shapes=[
            pltpu.VMEM((width, 3 * width), BF16),
            pltpu.VMEM((width, width), BF16),
            pltpu.VMEM((rows, width), BF16),
            pltpu.VMEM((rows, width), BF16),
            pltpu.VMEM((3 * pairs, rows, LANES), BF16),
            pltpu.VMEM((seq_count, pairs, 2 * seq_len, seq_len), BF16),
            pltpu.VMEM((rows, width), BF16),
            pltpu.VMEM((rows, width), F32),
            pltpu.VMEM((rows, width), BF16),
            pltpu.VMEM((7, lines, LANES), F32),
            pltpu.SemaphoreType.DMA((10,)),
        ],
        compiler_params=params(60),
        name="forward",
        cost_estimate=cost(10, 20),
    )(
        seq_lengths,
        hash_ids,
        x,
        *scales,
        query_key_value_weight,
        output_weight,
        grad_rows,
    )
    arrived = exchanged(send)
    normed_other = swapped(normed)
    attended_other = swapped(attended)
    block = width // 4
    column = pl.BlockSpec((rows, block), lambda i, at: (0, at[4 + i]))
    weight_part = [
        pl.BlockSpec((block, half), lambda i, at, part=part: (at[4 + i], 2 * part + at[0]))
        for part in range(3)
    ]
    normed_lines, attended_lines, weight_lines, scale_lines = pl.pallas_call(
        prepare_kernel,
        out_shape=(
            shaped((width, 2 * rows), BF16),
            shaped((width, 2 * rows), BF16),
            shaped((width, 3 * half), BF16),
            shaped((width, LANES), F32),
        ),
        grid_spec=pltpu.PrefetchScalarGridSpec(
            num_scalar_prefetch=1,
            grid=(4,),
            in_specs=[column] * 4 + weight_part + [whole((8, LANES))] * 2,
            out_specs=[
                pl.BlockSpec((block, 2 * rows), lambda i, at: (i, 0)),
                pl.BlockSpec((block, 2 * rows), lambda i, at: (i, 0)),
                pl.BlockSpec((block, 3 * half), lambda i, at: (i, 0)),
                pl.BlockSpec((block, LANES), lambda i, at: (i, 0)),
            ],
        ),
        compiler_params=params(60),
        name="prepare",
        cost_estimate=cost(4, 8),
    )(
        spot,
        normed,
        normed_other,
        attended,
        attended_other,
        query_key_value_weight,
        query_key_value_weight,
        query_key_value_weight,
        *scales[:2],
    )
    arrived, normed_lines = lax.optimization_barrier((arrived, normed_lines))

    blocks = 8
    tile = ff_width // blocks
    per_half = blocks // 2

    def in_order(f, core_ref):
        first = f // per_half
        group = jnp.where(first == 0, 1 - core_ref[0], core_ref[0])
        return group * per_half + f % per_half

    def early(f, core_ref):
        return (0, jnp.minimum(f, per_half - 1))

    def late(f, core_ref):
        return (0, jnp.maximum(f - per_half, 0))

    row_block = whole((n_slots, width))
    half_block = shaped((n_slots, half_ff), BF16)
    rows_in, grads_in, active_other, active_mine, lifted_other, lifted_mine, back = pl.pallas_call(
        functools.partial(expert_kernel, experts, capacity, blocks),
        out_shape=(
            shaped((n_slots, width), BF16),
            shaped((n_slots, width), BF16),
            half_block,
            half_block,
            half_block,
            half_block,
            shaped((lines, 7 * LANES), BF16),
        ),
        grid_spec=pltpu.PrefetchScalarGridSpec(
            num_scalar_prefetch=1,
            grid=(blocks,),
            in_specs=[
                whole((lines, 7 * LANES)),
                pl.BlockSpec((width, tile), lambda f, c: (0, in_order(f, c))),
                pl.BlockSpec((tile, width), lambda f, c: (in_order(f, c), 0)),
            ],
            out_specs=[
                row_block,
                row_block,
                pl.BlockSpec((n_slots, tile), early),
                pl.BlockSpec((n_slots, tile), late),
                pl.BlockSpec((n_slots, tile), early),
                pl.BlockSpec((n_slots, tile), late),
                whole((lines, 7 * LANES)),
            ],
            scratch_shapes=[
                pltpu.VMEM((6, lines, LANES), F32),
                pltpu.VMEM((n_slots, width), F32),
                pltpu.VMEM((n_slots, width), F32),
            ],
        ),
        compiler_params=params(60),
        name="expert",
        cost_estimate=cost(16, 25),
    )(core_at, arrived, w_in, w_out)
    returned = exchanged(back)

    rows_other = swapped(rows_in)
    grads_other = swapped(grads_in)
    active_came = swapped(active_other)
    lifted_came = swapped(lifted_other)
    tile = half_ff // 4
    column = pl.BlockSpec((n_slots, tile), lambda f: (0, f))
    expert_out_grad = pl.pallas_call(
        outer_kernel,
        out_shape=shaped((half_ff, width), F32),
        grid=(4,),
        in_specs=[column, column, row_block, row_block],
        out_specs=pl.BlockSpec((tile, width), lambda f: (f, 0)),
        compiler_params=params(60),
        name="expert_out_grad",
        cost_estimate=cost(5, 14),
    )(active_mine, active_came, grads_in, grads_other)
    expert_in_grad = pl.pallas_call(
        outer_kernel,
        out_shape=shaped((width, half_ff), F32),
        grid=(4,),
        in_specs=[row_block, row_block, column, column],
        out_specs=pl.BlockSpec((width, tile), lambda f: (0, f)),
        compiler_params=params(60),
        name="expert_in_grad",
        cost_estimate=cost(5, 14),
    )(rows_in, rows_other, lifted_mine, lifted_came)

    returned, expert_out_grad, expert_in_grad = lax.optimization_barrier(
        (returned, expert_out_grad, expert_in_grad)
    )

    half_pairs = pairs // 2
    grad_hidden, branch, branch_out, grad_attended, ffn_gains, mixed_out = pl.pallas_call(
        functools.partial(hidden_kernel, experts, capacity),
        out_shape=(
            shaped((rows, width), F32),
            shaped((rows, half), BF16),
            shaped((rows, half), BF16),
            shaped((pairs, rows, LANES), BF16),
            shaped((8, width), F32),
            shaped((3, half_pairs, rows, LANES), BF16),
        ),
        in_specs=[smem, vmem, vmem, vmem] + [hbm] * 5,
        out_specs=[hbm, vmem, vmem, hbm, vmem, vmem],
        scratch_shapes=[
            pltpu.VMEM((3, lines, LANES), F32),
            pltpu.VMEM((n_slots, width), BF16),
            pltpu.VMEM((rows, width), F32),
            pltpu.VMEM((rows, width), BF16),
            pltpu.VMEM((rows, width), F32),
            pltpu.VMEM((rows, width), BF16),
            pltpu.VMEM((width, width), BF16),
            pltpu.VMEM((3, half_pairs, rows, LANES), BF16),
            pltpu.VMEM((seq_count, half_pairs, 2 * seq_len, seq_len), BF16),
            pltpu.VMEM((rows, width), F32),
            pltpu.VMEM((pairs, rows, LANES), BF16),
            pltpu.SemaphoreType.DMA((10,)),
        ],
        compiler_params=params(60),
        name="hidden_backward",
        cost_estimate=cost(6, 14),
    )(spot, returned, dispatch, scales[2], hidden, grad_rows, output_weight, mixed, probs)
    mixed_came = swapped(mixed_out)
    branch_other = swapped(branch_out)

    def tile_of(part):
        return pl.BlockSpec(
            (1, rows, LANES), lambda p, at: (part * pairs + at[0] * half_pairs + p, 0, 0)
        )

    mixed_mine = pl.pallas_call(
        functools.partial(attention_kernel, seq_count),
        out_shape=shaped((3, half_pairs, rows, LANES), BF16),
        grid_spec=pltpu.PrefetchScalarGridSpec(
            num_scalar_prefetch=1,
            grid=(half_pairs,),
            in_specs=[
                tile_of(0),
                tile_of(1),
                tile_of(2),
                tile_of(0),
                pl.BlockSpec(
                    (seq_count, 1, 2 * seq_len, seq_len),
                    lambda p, at: (0, at[0] * half_pairs + p, 0, 0),
                ),
            ],
            out_specs=pl.BlockSpec((3, 1, rows, LANES), lambda p, at: (0, p, 0, 0)),
        ),
        compiler_params=params(60),
        name="attention_backward",
        cost_estimate=cost(4, 5),
    )(spot, mixed, mixed, mixed, grad_attended, probs)

    spans = (half + half // 2, half + half // 4, half + half // 2)
    size = width // 2
    shapes = ((256 * 2,), (8, 4, 16), (2, 4, 4, 16))
    halves = pl.pallas_call(
        weights_kernel,
        out_shape=[
            shaped(shape + (span,), BF16) for shape, span in zip(shapes, spans) for _ in range(2)
        ],
        grid_spec=pltpu.PrefetchScalarGridSpec(
            num_scalar_prefetch=1,
            grid=(2,),
            in_specs=[
                pl.BlockSpec((size, 2 * rows), lambda i, c: (i, 0)),
                pl.BlockSpec((size, 2 * rows), lambda i, c: (i, 0)),
                whole((3, half_pairs, rows, LANES)),
                whole((3, half_pairs, rows, LANES)),
                whole((rows, half)),
                whole((rows, half)),
                pl.BlockSpec((size, 3 * half), lambda i, c: (i, 0)),
                pl.BlockSpec((size, LANES), lambda i, c: (i, 0)),
                whole((8, width)),
            ],
            out_specs=[
                whole((512, spans[0])),
                whole((512, spans[0])),
                pl.BlockSpec((8, 2, 16, spans[1]), lambda i, c: (0, i, 0, 0)),
                pl.BlockSpec((8, 2, 16, spans[1]), lambda i, c: (0, i, 0, 0)),
                pl.BlockSpec((2, 2, 4, 16, spans[2]), lambda i, c: (0, i, 0, 0, 0)),
                pl.BlockSpec((2, 2, 4, 16, spans[2]), lambda i, c: (0, i, 0, 0, 0)),
            ],
            scratch_shapes=[pltpu.VMEM((8, half), F32)],
        ),
        compiler_params=params(60),
        name="weight_gradients",
        cost_estimate=cost(6, 14),
    )(
        spot,
        normed_lines,
        attended_lines,
        mixed_mine,
        mixed_came,
        branch,
        branch_other,
        weight_lines,
        scale_lines,
        ffn_gains,
    )
    input_grad = pl.pallas_call(
        input_kernel,
        out_shape=shaped((rows, width), F32),
        in_specs=[smem, vmem, vmem, vmem, hbm, hbm, hbm],
        out_specs=hbm,
        scratch_shapes=[
            pltpu.VMEM((width, 3 * width), BF16),
            pltpu.VMEM((rows, width), BF16),
            pltpu.VMEM((rows, width), F32),
            pltpu.VMEM((rows, width), F32),
            pltpu.SemaphoreType.DMA((9,)),
        ],
        compiler_params=params(60),
        name="input_backward",
        cost_estimate=cost(6, 14),
    )(spot, mixed_mine, mixed_out, scales[0], query_key_value_weight, x, grad_hidden)

    block_output = pl.pallas_call(
        functools.partial(output_kernel, experts, capacity),
        out_shape=shaped((rows, width), BF16),
        grid=(1,),
        in_specs=[
            whole((lines, 7 * LANES)),
            whole((n_slots, rows)),
            whole((rows, width)),
        ],
        out_specs=whole((rows, width)),
        scratch_shapes=[
            pltpu.VMEM((3, lines, LANES), F32),
            pltpu.VMEM((n_slots, width), BF16),
        ],
        compiler_params=params(60),
        name="block_output",
        cost_estimate=cost(1, 5),
    )(returned, dispatch, hidden)

    orders = ((0, 1, 2), (1, 2, 0), (2, 0, 1))
    sent = [part.reshape(2, 4, 4, 16, -1) for part in halves[0::2]]
    kept = [part.reshape(2, 4, 4, 16, -1) for part in halves[1::2]]
    came = [crossed(part, order[0], True) for part, order in zip(sent, orders)]
    came, input_grad = lax.optimization_barrier((came, input_grad))
    for step in (1, 2):
        slow = (slice(None),) * step + (slice(2, 4),)
        fast = (slice(None),) * step + (slice(0, 2),)
        sent = [
            (k[slow].astype(F32) + c[slow].astype(F32)).astype(BF16) for k, c in zip(kept, came)
        ]
        kept = [k[fast].astype(F32) + c[fast].astype(F32) for k, c in zip(kept, came)]
        came = [crossed(part, order[step], True) for part, order in zip(sent, orders)]
    came, block_output = lax.optimization_barrier((came, block_output))
    backs = ((0, 1, 2, 3, 4), (2, 0, 1, 3, 4), (1, 2, 0, 3, 4))
    kept = [(k + c.astype(F32)).transpose(back) for k, c, back in zip(kept, came, backs)]
    kept = jnp.concatenate(kept, axis=-1)
    for axis in range(3):
        kept = kept[0] + crossed(kept[1].astype(BF16), axis, False).astype(F32)
    own = lax.dynamic_slice_in_dim(kept, core * 8, 8, 0)
    came = swapped(lax.dynamic_slice_in_dim(kept, (1 - core) * 8, 8, 0))
    vectors = own[:, -LANES : 4 - LANES] + came[:, -LANES : 4 - LANES]

    def joined(at, span):
        mine, other = own[:, at : at + span], came[:, at : at + span]
        return jnp.where(
            core == 0,
            jnp.concatenate([mine, other], axis=1),
            jnp.concatenate([other, mine], axis=1),
        )

    q_at, k_at, v_at = 0, spans[0], spans[0] + spans[1]
    qkv_grad = jnp.concatenate([joined(at, half) for at in (q_at, k_at, v_at)], axis=1)

    def out_columns(shard):
        return jnp.concatenate(
            [
                shard[:, at + half : at + span]
                for at, span in zip((q_at, k_at, v_at), (*spans[:2], half + half // 4))
            ],
            axis=1,
        )

    mine, other = out_columns(own), out_columns(came)
    out_weight_grad = jnp.where(
        core == 0,
        jnp.concatenate([mine, other], axis=1),
        jnp.concatenate([other, mine], axis=1),
    )

    pair = returned[:, 6 * LANES : 6 * LANES + 2].reshape(chips, 16, 2)[:, 0].astype(F32)
    counts = 256.0 * pair[:, 0] + pair[:, 1]
    counts = counts + swapped(counts)
    total_tokens = float(rows * chips * 2)
    new_average = (momentum * prev_counts.astype(F32) + (1.0 - momentum) * counts) * (
        float(experts) / total_tokens
    )
    return (
        block_output.reshape(seq_count, seq_len, width),
        input_grad.reshape(seq_count, seq_len, width),
        vectors[:, 0],
        vectors[:, 1],
        qkv_grad,
        out_weight_grad,
        vectors[:, 2],
        vectors[:, 3],
        expert_in_grad[None],
        expert_out_grad[None],
        new_average,
    )


def solution(mesh):
    finer = Mesh(
        mesh.devices.reshape(4, 4, 4, mesh.shape["narrow"]),
        ("wide_0", "wide_1", "wide_2", "narrow"),
    )
    placed = (
        P(WIDE_NARROW, None, None),
        P(),
        P(),
        P(),
        P(),
        P(),
        P(),
        P(WIDE, None, None),
        P(WIDE, None, None),
        P(WIDE_NARROW, None),
        P(WIDE_NARROW),
        P(),
        P(WIDE_NARROW, None, None),
    )
    return jax.shard_map(
        per_device,
        mesh=finer,
        in_specs=placed,
        out_specs=(
            P(WIDE_NARROW, None, None),
            P(WIDE_NARROW, None, None),
            P(WIDE_NARROW),
            P(WIDE_NARROW),
            P(WIDE_NARROW, None),
            P(WIDE_NARROW, None),
            P(WIDE_NARROW),
            P(WIDE_NARROW),
            P(WIDE, None, "narrow"),
            P(WIDE, "narrow", None),
            P(),
        ),
        check_vma=False,
    )
```

```python
import functools
import math

import jax
import jax.experimental.pallas as pl
import jax.experimental.pallas.tpu as pltpu
import jax.numpy as jnp
from jax import lax
from jax.sharding import Mesh
from jax.sharding import PartitionSpec as P

HEADS = 16
WIDE = ("wide_0", "wide_1", "wide_2")
WIDE_NARROW = ("wide_0", "wide_1", "wide_2", "narrow")

norm_eps = 1e-05
momentum = 0.9
F32 = jnp.float32
BF16 = jnp.bfloat16
LANES = 128
MIB = 1 << 20


def swapped(shard):
    return lax.ppermute(shard, "narrow", [(0, 1), (1, 0)])


def exchanged(lines):
    shard = lines.reshape(lax.axis_size(WIDE), -1, lines.shape[1])
    return lax.all_to_all(shard, WIDE, 0, 0, tiled=True).reshape(lines.shape)


def crossed(shard, axis, first):
    pairs = []
    for i in range(lax.axis_size(WIDE[axis])):
        for core in range(2):
            flip = 1 if first == (core == 0) else 3
            pairs.append((i * 2 + core, (i ^ flip) * 2 + core))
    return lax.ppermute(shard, (WIDE[axis], "narrow"), pairs)


def dot(left, right, left_dim=1, right_dim=0):
    return lax.dot_general(
        left, right, (((left_dim,), (right_dim,)), ((), ())), preferred_element_type=F32
    )


def params(mib):
    return pltpu.CompilerParams(vmem_limit_bytes=mib * MIB)


def cost(gigaflops, megabytes):
    return pl.CostEstimate(
        flops=int(gigaflops * 1e9), bytes_accessed=int(megabytes * 1e6), transcendentals=0
    )


def normalize(features):
    centered = features - jnp.mean(features, axis=-1, keepdims=True)
    spread = jnp.mean(centered * centered, axis=-1, keepdims=True)
    scale = lax.rsqrt(spread + norm_eps)
    return centered * scale, scale


def as_row(tile_ref):
    tile = tile_ref[...].astype(F32)
    return jnp.concatenate([tile[i : i + 1, :] for i in range(tile.shape[0])], axis=1)


def norm_backward(scaled, scale, gained):
    mean = jnp.mean(gained, axis=-1, keepdims=True)
    along = jnp.mean(gained * scaled, axis=-1, keepdims=True)
    return scale * (gained - mean - scaled * along)


def to_lines(store, rows, experts, capacity, lane_tile):
    for rank in range(capacity):
        for part in range(8):
            at = rank % 2 * 8 + part
            store[lane_tile + rank // 2, pl.ds(at, experts, stride=16), :] = rows[
                rank * experts : (rank + 1) * experts, part * LANES : (part + 1) * LANES
            ]


def from_lines(store, rows_ref, experts, capacity, lane_tile):
    for rank in range(capacity):
        for part in range(8):
            at = rank % 2 * 8 + part
            rows_ref[
                rank * experts : (rank + 1) * experts, part * LANES : (part + 1) * LANES
            ] = store[lane_tile + rank // 2, pl.ds(at, experts, stride=16), :].astype(BF16)


def fill_store(store, lines_ref, lane_tile, count, source_tile):
    for tile in range(count):
        at = (source_tile + tile) * LANES
        store[lane_tile + tile] = lines_ref[:, at : at + LANES].astype(F32)


def spill_store(store, lines_ref, count, target_tile):
    for tile in range(count):
        at = (target_tile + tile) * LANES
        lines_ref[:, at : at + LANES] = store[tile].astype(BF16)


def forward_kernel(
    experts,
    capacity,
    len_ref,
    ids_ref,
    x_ref,
    gain_one_ref,
    shift_one_ref,
    gain_two_ref,
    shift_two_ref,
    qkv_weight_hbm,
    out_weight_hbm,
    grad_hbm,
    normed_hbm,
    mixed_hbm,
    probs_hbm,
    attended_hbm,
    hidden_hbm,
    dispatch_ref,
    send_ref,
    qkv_weight_ref,
    out_weight_ref,
    grad_ref,
    normed_ref,
    mixed_ref,
    probs_ref,
    attended_ref,
    hidden_ref,
    moved_ref,
    barred,
    store,
    sems,
):
    rows, width = x_ref.shape
    seq_count, seq_len = ids_ref.shape
    pieces = 3
    span = 3 * width // pieces

    def fetch(i):
        at = slice(i * span, (i + 1) * span)
        return pltpu.make_async_copy(qkv_weight_hbm.at[:, at], qkv_weight_ref.at[:, at], sems.at[i])

    out_weight_copy = pltpu.make_async_copy(out_weight_hbm, out_weight_ref, sems.at[3])
    grad_copy = pltpu.make_async_copy(grad_hbm, grad_ref, sems.at[4])
    for i in range(pieces):
        fetch(i).start()
    out_weight_copy.start()
    grad_copy.start()
    normed_copy = pltpu.make_async_copy(normed_ref, normed_hbm, sems.at[5])
    mixed_copy = pltpu.make_async_copy(mixed_ref, mixed_hbm, sems.at[6])
    probs_copy = pltpu.make_async_copy(probs_ref, probs_hbm, sems.at[7])
    attended_copy = pltpu.make_async_copy(attended_ref, attended_hbm, sems.at[8])
    hidden_copy = pltpu.make_async_copy(hidden_ref, hidden_hbm, sems.at[9])

    gain_one, shift_one = as_row(gain_one_ref), as_row(shift_one_ref)
    gain_two, shift_two = as_row(gain_two_ref), as_row(shift_two_ref)
    step = 128

    def norm_one(i, _):
        at = pl.ds(pl.multiple_of(i * step, step), step)
        scaled, _ = normalize(x_ref[at, :].astype(F32))
        normed_ref[at, :] = (scaled * gain_one + shift_one).astype(BF16)
        return 0

    lax.fori_loop(0, rows // step, norm_one, 0, unroll=2)
    normed_copy.start()

    ids = jnp.concatenate([ids_ref[s : s + 1, :] for s in range(seq_count)], axis=1)
    lane = lax.broadcasted_iota(jnp.int32, (1, rows), 1)
    length = jnp.where(lane < seq_len, len_ref[0], len_ref[1])
    is_valid = lane % seq_len < length
    member = (lax.broadcasted_iota(jnp.int32, (experts, rows), 0) == ids) & is_valid
    onehot = member.astype(F32)
    earlier = (
        lax.broadcasted_iota(jnp.int32, (rows, rows), 0)
        < lax.broadcasted_iota(jnp.int32, (rows, rows), 1)
    ).astype(F32)
    before = dot(onehot.astype(BF16), earlier.astype(BF16))
    rank = jnp.sum(onehot * before, axis=0, keepdims=True).astype(jnp.int32)
    slot = jnp.where(is_valid & (rank < capacity), rank * experts + ids, -1)
    at_slot = lax.broadcasted_iota(jnp.int32, (experts * capacity, rows), 0)
    dispatch_ref[...] = (at_slot == slot).astype(F32).astype(BF16)
    counts = jnp.sum(onehot, axis=1, keepdims=True)
    upper = jnp.floor(counts * (1.0 / 64.0))
    column = lax.broadcasted_iota(jnp.int32, (experts, LANES), 1)
    store[6] = jnp.zeros(store.shape[1:], F32)
    store[6, pl.ds(0, experts, stride=16), :] = jnp.where(
        column == 0, upper, jnp.where(column == 1, counts - 64.0 * upper, 0.0)
    )

    for i in range(pieces):
        fetch(i).wait()

        def project(j, _):
            at = pl.ds(pl.multiple_of(i * span + j * 512, 512), 512)
            block = dot(normed_ref[...], qkv_weight_ref[:, at]).astype(BF16)
            for tile in range(4):
                mixed_ref[(i * span + j * 512) // LANES + tile] = block[
                    :, tile * LANES : (tile + 1) * LANES
                ]
            return 0

        lax.fori_loop(0, span // 512, project, 0)
    mixed_copy.start()

    pairs = HEADS // 2
    low = (lax.broadcasted_iota(jnp.int32, (1, LANES), 1) < 64).astype(F32)
    score_scale = 1.0 / math.sqrt(width // HEADS)
    low_scaled = (low * score_scale).astype(BF16)
    high_scaled = ((1.0 - low) * score_scale).astype(BF16)
    query_at = lax.broadcasted_iota(jnp.int32, (seq_len, 2 * seq_len), 1) % seq_len
    key_at = lax.broadcasted_iota(jnp.int32, (seq_len, 2 * seq_len), 0)
    for s in range(seq_count):
        allowed = (key_at <= query_at) & (key_at < len_ref[s])
        barred[s] = jnp.where(allowed, 0.0, -3e38)

    def attend(p, _):
        at = pl.multiple_of(p * LANES, LANES)
        for s in range(seq_count):
            here = slice(s * seq_len, (s + 1) * seq_len)
            q = mixed_ref[p, here, :]
            k = mixed_ref[pairs + p, here, :]
            v = mixed_ref[2 * pairs + p, here, :]
            both = jnp.concatenate([q * low_scaled, q * high_scaled], axis=0)
            scores = dot(k, both, 1, 1) + barred[s]
            raised = jnp.exp(scores - jnp.max(scores, axis=0, keepdims=True))
            total = jnp.sum(raised, axis=0, keepdims=True)
            probs = (raised * (1.0 / total)).astype(BF16)
            probs_ref[s, p] = probs
            out = dot(probs, v, 0, 0)
            out = out[:seq_len] * low + out[seq_len:] * (1.0 - low)
            attended_ref[here, pl.ds(at, LANES)] = out.astype(BF16)
        return 0

    lax.fori_loop(0, pairs, attend, 0, unroll=2)
    probs_copy.start()
    attended_copy.start()

    out_weight_copy.wait()

    def norm_two(i, _):
        at = pl.ds(pl.multiple_of(i * 256, 256), 256)
        hidden = x_ref[at, :].astype(F32) + dot(attended_ref[at, :], out_weight_ref[...])
        hidden_ref[at, :] = hidden
        scaled, _ = normalize(hidden)
        moved_ref[at, :] = (scaled * gain_two + shift_two).astype(BF16)
        return 0

    lax.fori_loop(0, rows // 256, norm_two, 0)
    hidden_copy.start()

    grad_copy.wait()
    to_lines(store, dot(dispatch_ref[...], grad_ref[...]), experts, capacity, 3)
    to_lines(store, dot(dispatch_ref[...], moved_ref[...]), experts, capacity, 0)
    spill_store(store, send_ref, 7, 0)
    for copy in (normed_copy, mixed_copy, probs_copy, attended_copy, hidden_copy):
        copy.wait()


def places(position, core):
    near = 1 + 2 * core
    return jnp.where(
        position == 0,
        0,
        jnp.where(position == 1, 4 - near, jnp.where(position == 2, near, 2)),
    )


def order_matrix(at_ref):
    line = lax.broadcasted_iota(jnp.int32, (256, 256), 0)
    column = lax.broadcasted_iota(jnp.int32, (256, 256), 1)
    core, z, y = at_ref[0], at_ref[2], at_ref[3]
    source_z = places(line // 64, core) ^ z
    source_y = places(line // 16 % 4, core) ^ y
    return (column == source_z * 64 + source_y * 16 + line % 16).astype(F32)


def prepare_kernel(
    at_ref,
    normed_a,
    normed_b,
    attended_a,
    attended_b,
    query_ref,
    key_ref,
    value_ref,
    gain_ref,
    shift_ref,
    normed_ref,
    attended_ref,
    weight_ref,
    scale_ref,
):
    order = order_matrix(at_ref).astype(BF16)
    rows = normed_a.shape[0]
    normed_ref[:, :rows] = dot(order, normed_a[...], 1, 1).astype(BF16)
    normed_ref[:, rows:] = dot(order, normed_b[...], 1, 1).astype(BF16)
    attended_ref[:, :rows] = dot(order, attended_a[...], 1, 1).astype(BF16)
    attended_ref[:, rows:] = dot(order, attended_b[...], 1, 1).astype(BF16)
    half = query_ref.shape[1]
    for part, ref in enumerate((query_ref, key_ref, value_ref)):
        weight_ref[:, part * half : (part + 1) * half] = dot(order, ref[...]).astype(BF16)
    tile_at = 2 * at_ref[4 + pl.program_id(0)]
    tile = lax.broadcasted_iota(jnp.int32, (8, LANES), 0)
    line = lax.broadcasted_iota(jnp.int32, (LANES, 256), 0)

    def columns(ref):
        wide = ref[...].astype(F32)
        parts = [
            jnp.sum(jnp.where(tile == tile_at + i, wide, 0.0), axis=0, keepdims=True)
            for i in range(2)
        ]
        return jnp.concatenate(parts, axis=1)

    both = jnp.where(line == 0, columns(gain_ref), jnp.where(line == 1, columns(shift_ref), 0.0))
    scale_ref[...] = dot(order, both.astype(BF16), 1, 1)


def gelu_parts(u):
    inner = 0.7978845608028654 * (u + 0.044715 * (u * u * u))
    t = jnp.tanh(inner)
    half = 0.5 * (1.0 + t)
    slope = half + 0.5 * u * (1.0 - t * t) * (0.7978845608028654 * (1.0 + 0.134145 * (u * u)))
    return u * half, slope


def expert_kernel(
    experts,
    capacity,
    core_ref,
    lines_hbm,
    w_in_hbm,
    w_out_hbm,
    active_other_hbm,
    active_mine_hbm,
    lifted_other_hbm,
    lifted_mine_hbm,
    back_ref,
    lines_ref,
    w_in_ref,
    w_out_ref,
    rows_ref,
    grads_ref,
    active_ref,
    lifted_ref,
    store,
    total,
    produced,
    sems,
):
    chunks, _, tile = w_in_ref.shape
    core = core_ref[0]
    lines_copy = pltpu.make_async_copy(lines_hbm, lines_ref, sems.at[0])
    lines_copy.start()
    fetches = []
    for c in range(chunks):
        group = 1 - core if c < chunks // 2 else core
        at = pl.multiple_of((group * (chunks // 2) + c % (chunks // 2)) * tile, tile)
        fetches.append(
            (
                pltpu.make_async_copy(
                    w_in_hbm.at[:, pl.ds(at, tile)], w_in_ref.at[c], sems.at[1 + c]
                ),
                pltpu.make_async_copy(
                    w_out_hbm.at[pl.ds(at, tile), :], w_out_ref.at[c], sems.at[1 + chunks + c]
                ),
            )
        )
        for copy in fetches[-1]:
            copy.start()
    lines_copy.wait()
    fill_store(store, lines_ref, 0, 6, 0)
    from_lines(store, rows_ref, experts, capacity, 0)
    from_lines(store, grads_ref, experts, capacity, 3)

    leaving = []
    for c in range(chunks):
        for copy in fetches[c]:
            copy.wait()
        lifted = dot(rows_ref[...], w_in_ref[c])
        grad_active = dot(grads_ref[...], w_out_ref[c], 1, 1)
        gelu, slope = gelu_parts(lifted)
        active_ref[c] = gelu.astype(BF16)
        lifted_ref[c] = (grad_active * slope).astype(BF16)
        early = c < chunks // 2
        at = slice(c % (chunks // 2) * tile, (c % (chunks // 2) + 1) * tile)
        for i, (ref, hbm) in enumerate(
            (
                (active_ref, active_other_hbm if early else active_mine_hbm),
                (lifted_ref, lifted_other_hbm if early else lifted_mine_hbm),
            )
        ):
            copy = pltpu.make_async_copy(
                ref.at[c], hbm.at[:, at], sems.at[1 + (2 + i) * chunks + c]
            )
            copy.start()
            leaving.append(copy)
        moved = dot(lifted_ref[c], w_in_ref[c], 1, 1)
        made = dot(active_ref[c], w_out_ref[c])
        if c == 0:
            total[...] = moved
            produced[...] = made
        else:
            total[...] += moved
            produced[...] += made

    to_lines(store, total, experts, capacity, 0)
    to_lines(store, produced, experts, capacity, 3)
    spill_store(store, back_ref, 6, 0)
    arrived = lines_ref[:, 6 * LANES : 7 * LANES].astype(F32)
    sums = jnp.sum(arrived, axis=0, keepdims=True)
    column = lax.broadcasted_iota(jnp.int32, sums.shape, 1)
    count = jnp.sum(jnp.where(column == 0, 64.0 * sums, sums), axis=1, keepdims=True)
    upper = jnp.floor(count * (1.0 / 256.0))
    pair = jnp.where(column == 0, upper, jnp.where(column == 1, count - 256.0 * upper, 0.0))
    back_ref[:, 6 * LANES : 7 * LANES] = jnp.broadcast_to(pair, (back_ref.shape[0], LANES)).astype(
        BF16
    )
    for copy in leaving:
        copy.wait()


def expert_gradients_kernel(
    experts,
    capacity,
    steps,
    lines_a,
    lines_b,
    active_a,
    active_b,
    lifted_a,
    lifted_b,
    out_grad_ref,
    in_grad_ref,
    store,
    rows_ref,
    grads_ref,
):
    f = pl.program_id(0)
    own = rows_ref.shape[0] // 2

    @pl.when(f == 0)
    def _():
        for i, lines in enumerate((lines_a, lines_b)):
            fill_store(store, lines, 0, 6, 0)
            here = pl.ds(i * own, own)
            from_lines(store, rows_ref.at[here], experts, capacity, 0)
            from_lines(store, grads_ref.at[here], experts, capacity, 3)

    @pl.when(f < steps)
    def _():
        active = jnp.concatenate([active_a[...], active_b[...]], axis=0)
        out_grad_ref[...] = dot(active, grads_ref[...], 0, 0)

    @pl.when(f >= steps)
    def _():
        lifted = jnp.concatenate([lifted_a[...], lifted_b[...]], axis=0)
        in_grad_ref[...] = dot(rows_ref[...], lifted, 0, 0)


def attention_pair(q, k, v, grad, probs):
    seq_len = q.shape[0]
    low = (lax.broadcasted_iota(jnp.int32, (1, LANES), 1) < 64).astype(F32)
    score_scale = 1.0 / math.sqrt(64)
    low_half = low.astype(BF16)
    high_half = (1.0 - low).astype(BF16)
    grad_both = jnp.concatenate([grad * low_half, grad * high_half], axis=0)
    query_both = jnp.concatenate([q * low_half, q * high_half], axis=0)
    grad_probs = dot(v, grad_both, 1, 1)
    values = dot(probs, grad_both)
    wide = probs.astype(F32)
    inner = jnp.sum(wide * grad_probs, axis=0, keepdims=True)
    grad_scores = (wide * (grad_probs - inner)).astype(BF16)
    keys = dot(grad_scores, query_both) * score_scale
    queries = dot(grad_scores, k, 0, 0) * score_scale
    queries = queries[:seq_len] * low + queries[seq_len:] * (1.0 - low)
    return queries.astype(BF16), keys.astype(BF16), values.astype(BF16)


def hidden_kernel(
    experts,
    capacity,
    at_ref,
    lines_ref,
    dispatch_ref,
    gain_ref,
    hidden_hbm,
    grad_hbm,
    weight_hbm,
    mixed_hbm,
    probs_hbm,
    grad_hidden_hbm,
    branch_mine_ref,
    branch_other_ref,
    attended_hbm,
    gains_ref,
    out_ref,
    store,
    came,
    normed,
    branch_ref,
    hidden_ref,
    grad_ref,
    weight_ref,
    mixed_ref,
    probs_ref,
    grad_hidden_ref,
    attended_ref,
    sems,
):
    rows, width = hidden_ref.shape
    seq_count = probs_ref.shape[0]
    seq_len = rows // seq_count
    pairs = probs_ref.shape[1]
    half = width // 2
    core = at_ref[0]
    other = (1 - core) * pairs
    copies = [
        pltpu.make_async_copy(hidden_hbm, hidden_ref, sems.at[0]),
        pltpu.make_async_copy(grad_hbm, grad_ref, sems.at[1]),
        pltpu.make_async_copy(weight_hbm, weight_ref, sems.at[2]),
    ]
    for part in range(3):
        copies.append(
            pltpu.make_async_copy(
                mixed_hbm.at[pl.ds(2 * part * pairs + other, pairs)],
                mixed_ref.at[part],
                sems.at[3 + part],
            )
        )
    for s in range(seq_count):
        copies.append(
            pltpu.make_async_copy(
                probs_hbm.at[s, pl.ds(other, pairs)], probs_ref.at[s], sems.at[6 + s]
            )
        )
    for copy in copies:
        copy.start()
    grad_hidden_copy = pltpu.make_async_copy(grad_hidden_ref, grad_hidden_hbm, sems.at[8])
    attended_copy = pltpu.make_async_copy(attended_ref, attended_hbm, sems.at[9])

    fill_store(store, lines_ref, 0, 3, 0)
    from_lines(store, came, experts, capacity, 0)
    gain = as_row(gain_ref)
    normed[...] = dot(dispatch_ref[...], came[...], 0, 0)
    gains_ref[...] = jnp.zeros_like(gains_ref)
    step = 128
    copies[0].wait()
    copies[1].wait()

    def body(i, _):
        at = pl.ds(pl.multiple_of(i * step, step), step)
        scaled, scale = normalize(hidden_ref[at, :])
        grad = normed[at, :]
        grad_hidden = grad_ref[at, :].astype(F32) + norm_backward(scaled, scale, grad * gain)
        grad_hidden_ref[at, :] = grad_hidden
        branch_ref[at, :] = grad_hidden.astype(BF16)
        gains_ref[0:1, :] += jnp.sum(grad * scaled, axis=0, keepdims=True)
        gains_ref[1:2, :] += jnp.sum(grad, axis=0, keepdims=True)
        return 0

    lax.fori_loop(0, rows // step, body, 0, unroll=2)
    grad_hidden_copy.start()
    branch_mine_ref[...] = branch_ref[:, pl.ds(pl.multiple_of(core * half, half), half)]
    branch_other_ref[...] = branch_ref[:, pl.ds(pl.multiple_of((1 - core) * half, half), half)]
    copies[2].wait()
    grad_attended = dot(branch_ref[...], weight_ref[...], 1, 1).astype(BF16)
    for tile in range(2 * pairs):
        attended_ref[tile] = grad_attended[:, tile * LANES : (tile + 1) * LANES]
    attended_copy.start()
    for copy in copies[3:]:
        copy.wait()

    def pair(p, _):
        for s in range(seq_count):
            here = slice(s * seq_len, (s + 1) * seq_len)
            grads = attention_pair(
                mixed_ref[0, p, here, :],
                mixed_ref[1, p, here, :],
                mixed_ref[2, p, here, :],
                attended_ref[other + p, here, :],
                probs_ref[s, p],
            )
            for part in range(3):
                out_ref[part, here, pl.ds(pl.multiple_of(p * LANES, LANES), LANES)] = grads[part]
        return 0

    lax.fori_loop(0, pairs, pair, 0)
    grad_hidden_copy.wait()
    attended_copy.wait()


def input_kernel(
    at_ref,
    mine_ref,
    other_ref,
    gain_ref,
    weight_hbm,
    x_hbm,
    grad_hidden_hbm,
    input_grad_hbm,
    weight_ref,
    x_ref,
    grad_hidden_ref,
    normed,
    sems,
):
    rows, width = x_ref.shape
    half = width // 2
    core = at_ref[0]
    chunks = []
    for part in range(3):
        at = slice(part * width, (part + 1) * width)
        chunks.append(
            pltpu.make_async_copy(weight_hbm.at[:, at], weight_ref.at[:, at], sems.at[part])
        )
    x_copy = pltpu.make_async_copy(x_hbm, x_ref, sems.at[3])
    grad_copy = pltpu.make_async_copy(grad_hidden_hbm, grad_hidden_ref, sems.at[4])
    for copy in (*chunks, x_copy, grad_copy):
        copy.start()
    total = None
    for part in range(3):
        chunks[part].wait()
        for ref, group in ((mine_ref, core), (other_ref, 1 - core)):
            at = pl.multiple_of(part * width + group * half, half)
            term = dot(ref[part], weight_ref[:, pl.ds(at, half)], 1, 1)
            total = term if total is None else total + term
    normed[...] = total
    gain = as_row(gain_ref)
    x_copy.wait()
    grad_copy.wait()
    step = 128
    out_copies = []
    for i in range(rows // step):
        at = slice(i * step, (i + 1) * step)
        scaled, scale = normalize(x_ref[at, :].astype(F32))
        grad_hidden_ref[at, :] += norm_backward(scaled, scale, normed[at, :] * gain)
        out_copies.append(
            pltpu.make_async_copy(grad_hidden_ref.at[at], input_grad_hbm.at[at], sems.at[5 + i])
        )
        out_copies[-1].start()
    for copy in out_copies:
        copy.wait()


def weights_kernel(
    at_ref,
    scale_ref,
    ffn_gains_ref,
    mixed_hbm,
    attended_hbm,
    probs_hbm,
    came_hbm,
    normed_lines_hbm,
    weight_lines_hbm,
    attended_lines_hbm,
    branch_a_hbm,
    branch_b_hbm,
    mine_hbm,
    send_x_hbm,
    keep_x_hbm,
    send_z_hbm,
    keep_z_hbm,
    send_y_hbm,
    keep_y_hbm,
    mixed_ref,
    attended_ref,
    probs_ref,
    right_ref,
    normed_ref,
    weight_ref,
    out_left_ref,
    branch_ref,
    x_ref,
    z_ref,
    y_ref,
    sums,
    sems,
    out_sems,
):
    seq_count = probs_ref.shape[0]
    pairs, rows, _ = attended_ref.shape
    seq_len = rows // seq_count
    half = right_ref.shape[2]
    core = at_ref[0]
    fetches = [
        pltpu.make_async_copy(
            mixed_hbm.at[pl.ds((2 * part + core) * pairs, pairs)], mixed_ref.at[part], sems.at[part]
        )
        for part in range(3)
    ]
    fetches.append(
        pltpu.make_async_copy(attended_hbm.at[pl.ds(core * pairs, pairs)], attended_ref, sems.at[3])
    )
    for s in range(seq_count):
        fetches.append(
            pltpu.make_async_copy(
                probs_hbm.at[s, pl.ds(core * pairs, pairs)], probs_ref.at[s], sems.at[4 + s]
            )
        )
    later = [
        (came_hbm, right_ref.at[:, rows:]),
        (normed_lines_hbm, normed_ref),
        (weight_lines_hbm, weight_ref),
        (attended_lines_hbm, out_left_ref),
        (branch_a_hbm, branch_ref.at[:rows]),
        (branch_b_hbm, branch_ref.at[rows:]),
    ]
    later = [
        pltpu.make_async_copy(hbm, ref, sems.at[6 + i]) for i, (hbm, ref) in enumerate(later)
    ]
    for copy in (*fetches, *later):
        copy.start()
    for copy in fetches:
        copy.wait()

    def pair(p, _):
        at = pl.ds(pl.multiple_of(p * LANES, LANES), LANES)
        for s in range(seq_count):
            here = slice(s * seq_len, (s + 1) * seq_len)
            grads = attention_pair(
                mixed_ref[0, p, here, :],
                mixed_ref[1, p, here, :],
                mixed_ref[2, p, here, :],
                attended_ref[p, here, :],
                probs_ref[s, p],
            )
            for part in range(3):
                right_ref[part, here, at] = grads[part]
        return 0

    lax.fori_loop(0, pairs, pair, 0)
    leaving = [pltpu.make_async_copy(right_ref.at[:, :rows], mine_hbm, out_sems.at[0])]
    leaving[0].start()
    for copy in later:
        copy.wait()

    for part in range(3):
        total = jnp.zeros((1, half), F32)
        for at in range(0, 2 * rows, 128):
            wide = right_ref[part, at : at + 128, :].astype(F32)
            total = total + jnp.sum(wide, axis=0, keepdims=True)
        sums[part : part + 1, :] = total

    size = x_ref.shape[1]
    lane = lax.broadcasted_iota(jnp.int32, (size, LANES), 1)
    order = order_matrix(at_ref)
    for turn, step in enumerate((1, 0)):
        lines = slice(step * size, (step + 1) * size)
        gain = jnp.zeros((size, 1), F32)
        shift = jnp.zeros((size, 1), F32)
        parts = []
        for part in range(3):
            block = dot(normed_ref[lines, :], right_ref[part])
            weight = weight_ref[lines, part * half : (part + 1) * half].astype(F32)
            gain = gain + jnp.sum(block * weight, axis=1, keepdims=True)
            shift = shift + jnp.sum(sums[part : part + 1, :] * weight, axis=1, keepdims=True)
            parts.append(block.astype(BF16))
        out = dot(out_left_ref[lines, :], branch_ref[...]).astype(BF16)
        x_ref[step, :, :half] = parts[0]
        x_ref[step, :, half:] = out[:, : half // 2]
        side = out[:, half // 2 : 3 * half // 4]
        for group in range(size // 16):
            x, chip = group // 16, group % 16
            here = slice(group * 16, (group + 1) * 16)
            z_ref[step, chip, x, :, :half] = parts[1][here]
            z_ref[step, chip, x, :, half:] = side[here]
        scale = scale_ref[lines, :]
        gain = (gain - scale[:, 1:2] * shift) / scale[:, 0:1]
        ffn = []
        for i in range(size // 256):
            block_at = at_ref[4 + step * (size // 256) + i]
            ffn.append(
                lax.dot_general(
                    order,
                    ffn_gains_ref[:, pl.ds(pl.multiple_of(block_at * 256, 256), 256)],
                    (((1,), (1,)), ((), ())),
                    precision=lax.Precision.HIGHEST,
                    preferred_element_type=F32,
                )
            )
        ffn = jnp.concatenate(ffn, axis=0)
        small = jnp.where(lane == 0, gain, jnp.where(lane == 1, shift, 0.0))
        small = jnp.where(lane == 2, ffn[:, 0:1], jnp.where(lane == 3, ffn[:, 1:2], small))
        small = small.astype(BF16)
        side = out[:, 3 * half // 4 :]
        for group in range(size // 16):
            x, z, y = group // 16, group // 4 % 4, group % 4
            here = slice(group * 16, (group + 1) * 16)
            y_ref[step, y, x, z, :, :half] = parts[2][here]
            y_ref[step, y, x, z, :, half : half + LANES] = side[here]
            y_ref[step, y, x, z, :, half + LANES :] = small[here]
        x_at = pl.ds(2 * step, 2)
        moves = [
            (x_ref.at[step], send_x_hbm if step == 1 else keep_x_hbm),
            (z_ref.at[step, 8:16], send_z_hbm.at[:, x_at]),
            (z_ref.at[step, 0:8], keep_z_hbm.at[:, x_at]),
            (y_ref.at[step, 2:4], send_y_hbm.at[:, x_at]),
            (y_ref.at[step, 0:2], keep_y_hbm.at[:, x_at]),
        ]
        for i, (ref, hbm) in enumerate(moves):
            copy = pltpu.make_async_copy(ref, hbm, out_sems.at[1 + turn * 5 + i])
            copy.start()
            leaving.append(copy)
    for copy in leaving:
        copy.wait()


def second_kernel(kept_ref, first_ref, send_ref):
    send_ref[...] = (kept_ref[...].astype(F32) + first_ref[...].astype(F32)).astype(BF16)


def third_kernel(kept_ref, first_ref, second_ref, send_ref):
    total = kept_ref[...].astype(F32) + first_ref[...].astype(F32) + second_ref[...].astype(F32)
    send_ref[...] = total.astype(BF16)


def merge_kernel(*refs):
    parts = [refs[4 * i : 4 * i + 4] for i in range(3)]
    send_ref, keep_ref = refs[12:]
    for x in range(2):
        for z in range(2):
            for y in range(2):
                at = 0
                for part, spot in zip(parts, ((x, z, y), (z, y, x), (y, x, z))):
                    total = part[0][spot].astype(F32)
                    for ref in part[1:]:
                        total = total + ref[spot].astype(F32)
                    span = total.shape[1]
                    if x == 1:
                        send_ref[z, y, :, at : at + span] = total.astype(BF16)
                    else:
                        keep_ref[z, y, :, at : at + span] = total
                    at += span


def split_kernel(at_ref, kept_ref, came_ref, mine_ref, other_ref, store):
    store[...] = kept_ref[...] + came_ref[...].astype(F32)
    core = at_ref[0]
    mine_ref[...] = store[pl.ds(pl.multiple_of(core * 8, 8), 8), :]
    other_ref[...] = store[pl.ds(pl.multiple_of((1 - core) * 8, 8), 8), :]


def join_kernel(spans, at_ref, mine_ref, other_ref, qkv_ref, out_ref, small_ref):
    half = out_ref.shape[1] // 2
    core = at_ref[0]
    for ref, group in ((mine_ref, core), (other_ref, 1 - core)):
        group_at = group * half
        at, out_at = 0, 0
        for part, span in enumerate(spans):
            spot = pl.multiple_of(2 * part * half + group_at, half)
            qkv_ref[:, pl.ds(spot, half)] = ref[:, at : at + half]
            side = span - half
            spot = pl.multiple_of(group_at + out_at, LANES)
            out_ref[:, pl.ds(spot, side)] = ref[:, at + half : at + span]
            at += span
            out_at += side
    small_ref[...] = mine_ref[:, at : at + LANES] + other_ref[:, at : at + LANES]


def output_kernel(experts, capacity, lines_ref, dispatch_ref, hidden_ref, out_ref, store, came):
    fill_store(store, lines_ref, 0, 3, 3)
    from_lines(store, came, experts, capacity, 0)
    back = dot(dispatch_ref[...], came[...], 0, 0)
    out_ref[...] = (hidden_ref[...] + back).astype(BF16)


def whole(shape):
    return pl.BlockSpec(shape, lambda *_: (0,) * len(shape))


def shaped(shape, dtype):
    return jax.ShapeDtypeStruct(shape, dtype)


def per_device(
    block_input,
    attn_gain,
    attn_shift,
    query_key_value_weight,
    output_weight,
    ffn_gain,
    ffn_shift,
    expert_in,
    expert_out,
    hash_ids,
    seq_lengths,
    prev_counts,
    out_grad,
):
    seq_count, seq_len, width = block_input.shape
    rows = seq_count * seq_len
    chips = lax.axis_size(WIDE)
    experts = chips
    capacity = max(2, 3 * rows // (4 * experts))
    n_slots = experts * capacity
    ff_width = expert_in.shape[2]
    half_ff = ff_width // 2
    half = width // 2
    pairs = HEADS // 2
    lines = 16 * chips
    core = lax.axis_index("narrow").astype(jnp.int32)
    core_at = core.reshape(1)
    other_at = (1 - core).reshape(1)
    x = block_input.reshape(rows, width)
    grad_rows = out_grad.reshape(rows, width)
    w_in = expert_in[0]
    w_out = expert_out[0]
    scales = [v.reshape(8, LANES) for v in (attn_gain, attn_shift, ffn_gain, ffn_shift)]
    smem = pl.BlockSpec(memory_space=pltpu.SMEM)
    vmem = pl.BlockSpec(memory_space=pltpu.VMEM)
    hbm = pl.BlockSpec(memory_space=pl.ANY)
    coordinates = [lax.axis_index(name).astype(jnp.int32) for name in WIDE]
    blocks_x = [places(place, core) ^ coordinates[0] for place in range(4)]
    spot = jnp.stack([core] + coordinates + blocks_x).astype(jnp.int32)

    normed, mixed, probs, attended, hidden, dispatch, send = pl.pallas_call(
        functools.partial(forward_kernel, experts, capacity),
        out_shape=(
            shaped((rows, width), BF16),
            shaped((3 * pairs, rows, LANES), BF16),
            shaped((seq_count, pairs, seq_len, 2 * seq_len), BF16),
            shaped((rows, width), BF16),
            shaped((rows, width), F32),
            shaped((n_slots, rows), BF16),
            shaped((lines, 7 * LANES), BF16),
        ),
        in_specs=[smem] + [vmem] * 6 + [hbm] * 3,
        out_specs=[hbm] * 5 + [vmem] * 2,
        scratch_shapes=[
            pltpu.VMEM((width, 3 * width), BF16),
            pltpu.VMEM((width, width), BF16),
            pltpu.VMEM((rows, width), BF16),
            pltpu.VMEM((rows, width), BF16),
            pltpu.VMEM((3 * pairs, rows, LANES), BF16),
            pltpu.VMEM((seq_count, pairs, seq_len, 2 * seq_len), BF16),
            pltpu.VMEM((rows, width), BF16),
            pltpu.VMEM((rows, width), F32),
            pltpu.VMEM((rows, width), BF16),
            pltpu.VMEM((seq_count, seq_len, 2 * seq_len), F32),
            pltpu.VMEM((7, lines, LANES), F32),
            pltpu.SemaphoreType.DMA((10,)),
        ],
        compiler_params=params(60),
        name="forward",
        cost_estimate=cost(10, 20),
    )(
        seq_lengths,
        hash_ids,
        x,
        *scales,
        query_key_value_weight,
        output_weight,
        grad_rows,
    )
    arrived = exchanged(send)
    normed_other = swapped(normed)
    attended_other = swapped(attended)
    block = width // 4
    column = pl.BlockSpec((rows, block), lambda i, at: (0, at[4 + i]))
    weight_part = [
        pl.BlockSpec((block, half), lambda i, at, part=part: (at[4 + i], 2 * part + at[0]))
        for part in range(3)
    ]
    normed_lines, attended_lines, weight_lines, scale_lines = pl.pallas_call(
        prepare_kernel,
        out_shape=(
            shaped((width, 2 * rows), BF16),
            shaped((width, 2 * rows), BF16),
            shaped((width, 3 * half), BF16),
            shaped((width, LANES), F32),
        ),
        grid_spec=pltpu.PrefetchScalarGridSpec(
            num_scalar_prefetch=1,
            grid=(4,),
            in_specs=[column] * 4 + weight_part + [whole((8, LANES))] * 2,
            out_specs=[
                pl.BlockSpec((block, 2 * rows), lambda i, at: (i, 0)),
                pl.BlockSpec((block, 2 * rows), lambda i, at: (i, 0)),
                pl.BlockSpec((block, 3 * half), lambda i, at: (i, 0)),
                pl.BlockSpec((block, LANES), lambda i, at: (i, 0)),
            ],
        ),
        compiler_params=params(60),
        name="prepare",
        cost_estimate=cost(4, 8),
    )(
        spot,
        normed,
        normed_other,
        attended,
        attended_other,
        query_key_value_weight,
        query_key_value_weight,
        query_key_value_weight,
        *scales[:2],
    )
    arrived, normed_lines = lax.optimization_barrier((arrived, normed_lines))

    chunks = 4
    tile = ff_width // chunks
    half_block = shaped((n_slots, half_ff), BF16)
    active_other, active_mine, lifted_other, lifted_mine, back = pl.pallas_call(
        functools.partial(expert_kernel, experts, capacity),
        out_shape=(
            half_block,
            half_block,
            half_block,
            half_block,
            shaped((lines, 7 * LANES), BF16),
        ),
        in_specs=[smem] + [hbm] * 3,
        out_specs=[hbm] * 4 + [vmem],
        scratch_shapes=[
            pltpu.VMEM((lines, 7 * LANES), BF16),
            pltpu.VMEM((chunks, width, tile), BF16),
            pltpu.VMEM((chunks, tile, width), BF16),
            pltpu.VMEM((n_slots, width), BF16),
            pltpu.VMEM((n_slots, width), BF16),
            pltpu.VMEM((chunks, n_slots, tile), BF16),
            pltpu.VMEM((chunks, n_slots, tile), BF16),
            pltpu.VMEM((6, lines, LANES), F32),
            pltpu.VMEM((n_slots, width), F32),
            pltpu.VMEM((n_slots, width), F32),
            pltpu.SemaphoreType.DMA((1 + 4 * chunks,)),
        ],
        compiler_params=params(60),
        name="expert",
        cost_estimate=cost(16, 25),
    )(spot, arrived, w_in, w_out)
    returned = exchanged(back)

    arrived_other = swapped(arrived)
    active_came = swapped(active_other)
    lifted_came = swapped(lifted_other)
    steps = 4
    tile = half_ff // steps
    early = pl.BlockSpec((n_slots, tile), lambda f: (0, jnp.minimum(f, steps - 1)))
    late = pl.BlockSpec((n_slots, tile), lambda f: (0, jnp.maximum(f - steps, 0)))
    expert_out_grad, expert_in_grad = pl.pallas_call(
        functools.partial(expert_gradients_kernel, experts, capacity, steps),
        out_shape=(shaped((half_ff, width), F32), shaped((width, half_ff), F32)),
        grid=(2 * steps,),
        in_specs=[whole((lines, 7 * LANES))] * 2 + [early] * 2 + [late] * 2,
        out_specs=[
            pl.BlockSpec((tile, width), lambda f: (jnp.minimum(f, steps - 1), 0)),
            pl.BlockSpec((width, tile), lambda f: (0, jnp.maximum(f - steps, 0))),
        ],
        scratch_shapes=[
            pltpu.VMEM((6, lines, LANES), F32),
            pltpu.VMEM((2 * n_slots, width), BF16),
            pltpu.VMEM((2 * n_slots, width), BF16),
        ],
        compiler_params=params(60),
        name="expert_gradients",
        cost_estimate=cost(10, 30),
    )(arrived, arrived_other, active_mine, active_came, lifted_mine, lifted_came)
    returned, expert_out_grad, expert_in_grad = lax.optimization_barrier(
        (returned, expert_out_grad, expert_in_grad)
    )

    half_pairs = pairs // 2
    grad_hidden, branch, branch_out, grad_attended, ffn_gains, mixed_out = pl.pallas_call(
        functools.partial(hidden_kernel, experts, capacity),
        out_shape=(
            shaped((rows, width), F32),
            shaped((rows, half), BF16),
            shaped((rows, half), BF16),
            shaped((pairs, rows, LANES), BF16),
            shaped((8, width), F32),
            shaped((3, rows, half), BF16),
        ),
        in_specs=[smem, vmem, vmem, vmem] + [hbm] * 5,
        out_specs=[hbm, vmem, vmem, hbm, vmem, vmem],
        scratch_shapes=[
            pltpu.VMEM((3, lines, LANES), F32),
            pltpu.VMEM((n_slots, width), BF16),
            pltpu.VMEM((rows, width), F32),
            pltpu.VMEM((rows, width), BF16),
            pltpu.VMEM((rows, width), F32),
            pltpu.VMEM((rows, width), BF16),
            pltpu.VMEM((width, width), BF16),
            pltpu.VMEM((3, half_pairs, rows, LANES), BF16),
            pltpu.VMEM((seq_count, half_pairs, seq_len, 2 * seq_len), BF16),
            pltpu.VMEM((rows, width), F32),
            pltpu.VMEM((pairs, rows, LANES), BF16),
            pltpu.SemaphoreType.DMA((10,)),
        ],
        compiler_params=params(60),
        name="hidden_backward",
        cost_estimate=cost(6, 14),
    )(spot, returned, dispatch, scales[2], hidden, grad_rows, output_weight, mixed, probs)
    mixed_came = swapped(mixed_out)
    branch_other = swapped(branch_out)

    spans = (half + half // 2, half + half // 4, half + half // 2)
    shapes = ((512,), (8, 4, 16), (2, 4, 4, 16))
    mixed_mine, *halves = pl.pallas_call(
        weights_kernel,
        out_shape=[shaped((3, rows, half), BF16)]
        + [shaped(shape + (span,), BF16) for shape, span in zip(shapes, spans) for _ in range(2)],
        in_specs=[smem, vmem, vmem] + [hbm] * 9,
        out_specs=[hbm] * 7,
        scratch_shapes=[
            pltpu.VMEM((3, half_pairs, rows, LANES), BF16),
            pltpu.VMEM((half_pairs, rows, LANES), BF16),
            pltpu.VMEM((seq_count, half_pairs, seq_len, 2 * seq_len), BF16),
            pltpu.VMEM((3, 2 * rows, half), BF16),
            pltpu.VMEM((width, 2 * rows), BF16),
            pltpu.VMEM((width, 3 * half), BF16),
            pltpu.VMEM((width, 2 * rows), BF16),
            pltpu.VMEM((2 * rows, half), BF16),
            pltpu.VMEM((2, 512, spans[0]), BF16),
            pltpu.VMEM((2, 16, 2, 16, spans[1]), BF16),
            pltpu.VMEM((2, 4, 2, 4, 16, spans[2]), BF16),
            pltpu.VMEM((8, half), F32),
            pltpu.SemaphoreType.DMA((12,)),
            pltpu.SemaphoreType.DMA((11,)),
        ],
        compiler_params=params(60),
        name="weight_gradients",
        cost_estimate=cost(10, 20),
    )(
        spot,
        scale_lines,
        ffn_gains,
        mixed,
        grad_attended,
        probs,
        mixed_came,
        normed_lines,
        weight_lines,
        attended_lines,
        branch,
        branch_other,
    )

    input_grad = pl.pallas_call(
        input_kernel,
        out_shape=shaped((rows, width), F32),
        in_specs=[smem, vmem, vmem, vmem, hbm, hbm, hbm],
        out_specs=hbm,
        scratch_shapes=[
            pltpu.VMEM((width, 3 * width), BF16),
            pltpu.VMEM((rows, width), BF16),
            pltpu.VMEM((rows, width), F32),
            pltpu.VMEM((rows, width), F32),
            pltpu.SemaphoreType.DMA((9,)),
        ],
        compiler_params=params(60),
        name="input_backward",
        cost_estimate=cost(6, 14),
    )(spot, mixed_mine, mixed_out, scales[0], query_key_value_weight, x, grad_hidden)

    block_output = pl.pallas_call(
        functools.partial(output_kernel, experts, capacity),
        out_shape=shaped((rows, width), BF16),
        grid=(1,),
        in_specs=[
            whole((lines, 7 * LANES)),
            whole((n_slots, rows)),
            whole((rows, width)),
        ],
        out_specs=whole((rows, width)),
        scratch_shapes=[
            pltpu.VMEM((3, lines, LANES), F32),
            pltpu.VMEM((n_slots, width), BF16),
        ],
        compiler_params=params(60),
        name="block_output",
        cost_estimate=cost(1, 5),
    )(returned, dispatch, hidden)

    orders = ((0, 1, 2), (1, 2, 0), (2, 0, 1))
    sent = [part.reshape(2, 4, 4, 16, -1) for part in halves[0::2]]
    kept = [part.reshape(2, 4, 4, 16, -1) for part in halves[1::2]]
    first = [crossed(part, order[0], True) for part, order in zip(sent, orders)]
    first, input_grad = lax.optimization_barrier((first, input_grad))

    def cut(span, shape, at):
        return pl.BlockSpec(shape + (16, span), lambda *_: at + (0, 0))

    def added(kernel, arrays, shape, spots, name):
        span = arrays[0].shape[-1]
        return pl.pallas_call(
            kernel,
            out_shape=shaped(shape + (16, span), BF16),
            grid=(1,),
            in_specs=[cut(span, shape, at) for at in spots],
            out_specs=whole(shape + (16, span)),
            compiler_params=params(16),
            name=name,
            cost_estimate=cost(0.01, 2),
        )(*arrays)

    second = []
    for k, c, order in zip(kept, first, orders):
        send = added(second_kernel, (k, c), (2, 2, 4), ((0, 1, 0),) * 2, "second")
        second.append(crossed(send, order[1], True))
    third = []
    for k, c, d, order in zip(kept, first, second, orders):
        spots = ((0, 0, 1),) * 3
        send = added(third_kernel, (k, c, d), (2, 2, 2), spots, "third")
        third.append(crossed(send, order[2], True))
    total_span = sum(spans)
    send, keep = pl.pallas_call(
        merge_kernel,
        out_shape=(
            shaped((2, 2, 16, total_span), BF16),
            shaped((2, 2, 16, total_span), F32),
        ),
        grid=(1,),
        in_specs=[cut(span, (2, 2, 2), (0, 0, 0)) for span in spans for _ in range(4)],
        out_specs=[whole((2, 2, 16, total_span))] * 2,
        compiler_params=params(16),
        name="merge",
        cost_estimate=cost(0.01, 4),
    )(*(array for group in zip(kept, first, second, third) for array in group))
    came = crossed(send, 0, False)
    for axis in (1, 2):
        keep = keep + came.astype(F32)
        came = crossed(keep[1].astype(BF16), axis, False)
        keep = keep[0]
    own, other = pl.pallas_call(
        split_kernel,
        out_shape=(shaped((8, total_span), F32), shaped((8, total_span), F32)),
        in_specs=[smem, vmem, vmem],
        out_specs=[vmem, vmem],
        scratch_shapes=[pltpu.VMEM((16, total_span), F32)],
        compiler_params=params(16),
        name="split",
    )(spot, keep, came)
    qkv_grad, out_weight_grad, vectors = pl.pallas_call(
        functools.partial(join_kernel, (*spans[:2], half + half // 4)),
        out_shape=(
            shaped((8, 3 * width), F32),
            shaped((8, width), F32),
            shaped((8, LANES), F32),
        ),
        in_specs=[smem, vmem, vmem],
        out_specs=[vmem] * 3,
        compiler_params=params(16),
        name="join",
    )(spot, own, swapped(other))

    pair = returned[:, 6 * LANES : 6 * LANES + 2].reshape(chips, 16, 2)[:, 0].astype(F32)
    counts = 256.0 * pair[:, 0] + pair[:, 1]
    counts = counts + swapped(counts)
    total_tokens = float(rows * chips * 2)
    new_average = (momentum * prev_counts.astype(F32) + (1.0 - momentum) * counts) * (
        float(experts) / total_tokens
    )
    return (
        block_output.reshape(seq_count, seq_len, width),
        input_grad.reshape(seq_count, seq_len, width),
        vectors[:, 0],
        vectors[:, 1],
        qkv_grad,
        out_weight_grad,
        vectors[:, 2],
        vectors[:, 3],
        expert_in_grad[None],
        expert_out_grad[None],
        new_average,
    )


def solution(mesh):
    finer = Mesh(
        mesh.devices.reshape(4, 4, 4, mesh.shape["narrow"]),
        ("wide_0", "wide_1", "wide_2", "narrow"),
    )
    placed = (
        P(WIDE_NARROW, None, None),
        P(),
        P(),
        P(),
        P(),
        P(),
        P(),
        P(WIDE, None, None),
        P(WIDE, None, None),
        P(WIDE_NARROW, None),
        P(WIDE_NARROW),
        P(),
        P(WIDE_NARROW, None, None),
    )
    return jax.shard_map(
        per_device,
        mesh=finer,
        in_specs=placed,
        out_specs=(
            P(WIDE_NARROW, None, None),
            P(WIDE_NARROW, None, None),
            P(WIDE_NARROW),
            P(WIDE_NARROW),
            P(WIDE_NARROW, None),
            P(WIDE_NARROW, None),
            P(WIDE_NARROW),
            P(WIDE_NARROW),
            P(WIDE, None, "narrow"),
            P(WIDE, "narrow", None),
            P(),
        ),
        check_vma=False,
    )
```

```python
import functools
import math

import jax
import jax.experimental.pallas as pl
import jax.experimental.pallas.tpu as pltpu
import jax.numpy as jnp
from jax import lax
from jax.sharding import Mesh
from jax.sharding import PartitionSpec as P

HEADS = 16
WIDE = ("wide_0", "wide_1", "wide_2")
WIDE_NARROW = ("wide_0", "wide_1", "wide_2", "narrow")

norm_eps = 1e-05
momentum = 0.9
F32 = jnp.float32
BF16 = jnp.bfloat16
LANES = 128
MIB = 1 << 20


def swapped(shard):
    return lax.ppermute(shard, "narrow", [(0, 1), (1, 0)])


def exchanged(lines):
    shard = lines.reshape(lax.axis_size(WIDE), -1, lines.shape[1])
    return lax.all_to_all(shard, WIDE, 0, 0, tiled=True).reshape(lines.shape)


def crossed(shard, axis, first):
    pairs = []
    for i in range(lax.axis_size(WIDE[axis])):
        for core in range(2):
            flip = 1 if first == (core == 0) else 3
            pairs.append((i * 2 + core, (i ^ flip) * 2 + core))
    return lax.ppermute(shard, (WIDE[axis], "narrow"), pairs)


def dot(left, right, left_dim=1, right_dim=0):
    return lax.dot_general(
        left, right, (((left_dim,), (right_dim,)), ((), ())), preferred_element_type=F32
    )


def params(mib):
    return pltpu.CompilerParams(vmem_limit_bytes=mib * MIB)


def cost(gigaflops, megabytes):
    return pl.CostEstimate(
        flops=int(gigaflops * 1e9), bytes_accessed=int(megabytes * 1e6), transcendentals=0
    )


def normalize(features):
    centered = features - jnp.mean(features, axis=-1, keepdims=True)
    spread = jnp.mean(centered * centered, axis=-1, keepdims=True)
    scale = lax.rsqrt(spread + norm_eps)
    return centered * scale, scale


def as_row(tile_ref):
    tile = tile_ref[...].astype(F32)
    return jnp.concatenate([tile[i : i + 1, :] for i in range(tile.shape[0])], axis=1)


def norm_backward(scaled, scale, gained):
    mean = jnp.mean(gained, axis=-1, keepdims=True)
    along = jnp.mean(gained * scaled, axis=-1, keepdims=True)
    return scale * (gained - mean - scaled * along)


def to_lines(store, rows, experts, capacity, lane_tile):
    for rank in range(capacity):
        for part in range(8):
            store[lane_tile + rank, pl.ds(part, experts, stride=8), :] = rows[
                rank * experts : (rank + 1) * experts, part * LANES : (part + 1) * LANES
            ]


def from_lines(store, rows_ref, experts, capacity, lane_tile):
    for rank in range(capacity):
        for part in range(8):
            rows_ref[
                rank * experts : (rank + 1) * experts, part * LANES : (part + 1) * LANES
            ] = store[lane_tile + rank, pl.ds(part, experts, stride=8), :].astype(BF16)


def fill_store(store, lines_ref, lane_tile, count, source_tile):
    for tile in range(count):
        at = (source_tile + tile) * LANES
        store[lane_tile + tile] = lines_ref[:, at : at + LANES].astype(F32)


def spill_store(store, lines_ref, count, target_tile):
    for tile in range(count):
        at = (target_tile + tile) * LANES
        lines_ref[:, at : at + LANES] = store[tile].astype(BF16)


def forward_kernel(
    experts,
    capacity,
    len_ref,
    ids_ref,
    x_ref,
    gain_one_ref,
    shift_one_ref,
    gain_two_ref,
    shift_two_ref,
    qkv_weight_hbm,
    out_weight_hbm,
    grad_hbm,
    normed_hbm,
    mixed_hbm,
    probs_hbm,
    attended_hbm,
    hidden_hbm,
    dispatch_ref,
    send_ref,
    qkv_weight_ref,
    out_weight_ref,
    grad_ref,
    normed_ref,
    mixed_ref,
    probs_ref,
    attended_ref,
    hidden_ref,
    moved_ref,
    barred,
    store,
    sems,
):
    rows, width = x_ref.shape
    seq_count, seq_len = ids_ref.shape
    pieces = 3
    span = 3 * width // pieces

    def fetch(i):
        at = slice(i * span, (i + 1) * span)
        return pltpu.make_async_copy(qkv_weight_hbm.at[:, at], qkv_weight_ref.at[:, at], sems.at[i])

    out_weight_copy = pltpu.make_async_copy(out_weight_hbm, out_weight_ref, sems.at[3])
    grad_copy = pltpu.make_async_copy(grad_hbm, grad_ref, sems.at[4])
    for i in range(pieces):
        fetch(i).start()
    out_weight_copy.start()
    grad_copy.start()
    normed_copy = pltpu.make_async_copy(normed_ref, normed_hbm, sems.at[5])
    mixed_copy = pltpu.make_async_copy(mixed_ref, mixed_hbm, sems.at[6])
    probs_copy = pltpu.make_async_copy(probs_ref, probs_hbm, sems.at[7])
    attended_copy = pltpu.make_async_copy(attended_ref, attended_hbm, sems.at[8])
    hidden_copy = pltpu.make_async_copy(hidden_ref, hidden_hbm, sems.at[9])

    gain_one, shift_one = as_row(gain_one_ref), as_row(shift_one_ref)
    gain_two, shift_two = as_row(gain_two_ref), as_row(shift_two_ref)
    step = 128

    def norm_one(i, _):
        at = pl.ds(pl.multiple_of(i * step, step), step)
        scaled, _ = normalize(x_ref[at, :].astype(F32))
        normed_ref[at, :] = (scaled * gain_one + shift_one).astype(BF16)
        return 0

    lax.fori_loop(0, rows // step, norm_one, 0, unroll=2)
    normed_copy.start()

    ids = jnp.concatenate([ids_ref[s : s + 1, :] for s in range(seq_count)], axis=1)
    lane = lax.broadcasted_iota(jnp.int32, (1, rows), 1)
    length = jnp.where(lane < seq_len, len_ref[0], len_ref[1])
    is_valid = lane % seq_len < length
    member = (lax.broadcasted_iota(jnp.int32, (experts, rows), 0) == ids) & is_valid
    onehot = member.astype(F32)
    earlier = (
        lax.broadcasted_iota(jnp.int32, (rows, rows), 0)
        < lax.broadcasted_iota(jnp.int32, (rows, rows), 1)
    ).astype(F32)
    before = dot(onehot.astype(BF16), earlier.astype(BF16))
    rank = jnp.sum(onehot * before, axis=0, keepdims=True).astype(jnp.int32)
    slot = jnp.where(is_valid & (rank < capacity), rank * experts + ids, -1)
    at_slot = lax.broadcasted_iota(jnp.int32, (experts * capacity, rows), 0)
    dispatch_ref[...] = (at_slot == slot).astype(F32).astype(BF16)
    counts = jnp.sum(onehot, axis=1, keepdims=True)
    upper = jnp.floor(counts * (1.0 / 64.0))
    column = lax.broadcasted_iota(jnp.int32, (experts, LANES), 1)
    store[12] = jnp.zeros(store.shape[1:], F32)
    store[12, pl.ds(0, experts, stride=8), :] = jnp.where(
        column == 0, upper, jnp.where(column == 1, counts - 64.0 * upper, 0.0)
    )

    for i in range(pieces):
        fetch(i).wait()

        def project(j, _):
            at = pl.ds(pl.multiple_of(i * span + j * 512, 512), 512)
            block = dot(normed_ref[...], qkv_weight_ref[:, at]).astype(BF16)
            for tile in range(4):
                mixed_ref[(i * span + j * 512) // LANES + tile] = block[
                    :, tile * LANES : (tile + 1) * LANES
                ]
            return 0

        lax.fori_loop(0, span // 512, project, 0)
    mixed_copy.start()

    pairs = HEADS // 2
    low = (lax.broadcasted_iota(jnp.int32, (1, LANES), 1) < 64).astype(F32)
    score_scale = 1.0 / math.sqrt(width // HEADS)
    low_scaled = (low * score_scale).astype(BF16)
    high_scaled = ((1.0 - low) * score_scale).astype(BF16)
    query_at = lax.broadcasted_iota(jnp.int32, (seq_len, 2 * seq_len), 1) % seq_len
    key_at = lax.broadcasted_iota(jnp.int32, (seq_len, 2 * seq_len), 0)
    for s in range(seq_count):
        allowed = (key_at <= query_at) & (key_at < len_ref[s])
        barred[s] = jnp.where(allowed, 0.0, -3e38)

    def attend(p, _):
        at = pl.multiple_of(p * LANES, LANES)
        for s in range(seq_count):
            here = slice(s * seq_len, (s + 1) * seq_len)
            q = mixed_ref[p, here, :]
            k = mixed_ref[pairs + p, here, :]
            v = mixed_ref[2 * pairs + p, here, :]
            both = jnp.concatenate([q * low_scaled, q * high_scaled], axis=0)
            scores = dot(k, both, 1, 1) + barred[s]
            raised = jnp.exp(scores - jnp.max(scores, axis=0, keepdims=True))
            total = jnp.sum(raised, axis=0, keepdims=True)
            probs = (raised * (1.0 / total)).astype(BF16)
            probs_ref[s, p] = probs
            out = dot(probs, v, 0, 0)
            out = out[:seq_len] * low + out[seq_len:] * (1.0 - low)
            attended_ref[here, pl.ds(at, LANES)] = out.astype(BF16)
        return 0

    lax.fori_loop(0, pairs, attend, 0, unroll=2)
    probs_copy.start()
    attended_copy.start()

    out_weight_copy.wait()

    def norm_two(i, _):
        at = pl.ds(pl.multiple_of(i * 256, 256), 256)
        hidden = x_ref[at, :].astype(F32) + dot(attended_ref[at, :], out_weight_ref[...])
        hidden_ref[at, :] = hidden
        scaled, _ = normalize(hidden)
        moved_ref[at, :] = (scaled * gain_two + shift_two).astype(BF16)
        return 0

    lax.fori_loop(0, rows // 256, norm_two, 0)
    hidden_copy.start()

    grad_copy.wait()
    to_lines(store, dot(dispatch_ref[...], grad_ref[...]), experts, capacity, 6)
    to_lines(store, dot(dispatch_ref[...], moved_ref[...]), experts, capacity, 0)
    spill_store(store, send_ref, 13, 0)
    for copy in (normed_copy, mixed_copy, probs_copy, attended_copy, hidden_copy):
        copy.wait()


def places(position, core):
    near = 1 + 2 * core
    return jnp.where(
        position == 0,
        0,
        jnp.where(position == 1, 4 - near, jnp.where(position == 2, near, 2)),
    )


def order_matrix(at_ref):
    line = lax.broadcasted_iota(jnp.int32, (256, 256), 0)
    column = lax.broadcasted_iota(jnp.int32, (256, 256), 1)
    core, z, y = at_ref[0], at_ref[2], at_ref[3]
    source_z = places(line // 64, core) ^ z
    source_y = places(line // 16 % 4, core) ^ y
    return (column == source_z * 64 + source_y * 16 + line % 16).astype(F32)


def prepare_kernel(
    at_ref,
    normed_a,
    normed_b,
    attended_a,
    attended_b,
    query_ref,
    key_ref,
    value_ref,
    gain_ref,
    shift_ref,
    normed_ref,
    attended_ref,
    weight_ref,
    scale_ref,
):
    order = order_matrix(at_ref).astype(BF16)
    rows = normed_a.shape[0]
    normed_ref[:, :rows] = dot(order, normed_a[...], 1, 1).astype(BF16)
    normed_ref[:, rows:] = dot(order, normed_b[...], 1, 1).astype(BF16)
    attended_ref[:, :rows] = dot(order, attended_a[...], 1, 1).astype(BF16)
    attended_ref[:, rows:] = dot(order, attended_b[...], 1, 1).astype(BF16)
    half = query_ref.shape[1]
    for part, ref in enumerate((query_ref, key_ref, value_ref)):
        weight_ref[:, part * half : (part + 1) * half] = dot(order, ref[...]).astype(BF16)
    tile_at = 2 * at_ref[4 + pl.program_id(0)]
    tile = lax.broadcasted_iota(jnp.int32, (8, LANES), 0)
    line = lax.broadcasted_iota(jnp.int32, (LANES, 256), 0)

    def columns(ref):
        wide = ref[...].astype(F32)
        parts = [
            jnp.sum(jnp.where(tile == tile_at + i, wide, 0.0), axis=0, keepdims=True)
            for i in range(2)
        ]
        return jnp.concatenate(parts, axis=1)

    both = jnp.where(line == 0, columns(gain_ref), jnp.where(line == 1, columns(shift_ref), 0.0))
    scale_ref[...] = dot(order, both.astype(BF16), 1, 1)


def gelu_parts(u):
    inner = 0.7978845608028654 * (u + 0.044715 * (u * u * u))
    t = jnp.tanh(inner)
    half = 0.5 * (1.0 + t)
    slope = half + 0.5 * u * (1.0 - t * t) * (0.7978845608028654 * (1.0 + 0.134145 * (u * u)))
    return u * half, slope


def expert_kernel(
    experts,
    capacity,
    core_ref,
    lines_hbm,
    w_in_hbm,
    w_out_hbm,
    active_other_hbm,
    active_mine_hbm,
    lifted_other_hbm,
    lifted_mine_hbm,
    back_ref,
    lines_ref,
    w_in_ref,
    w_out_ref,
    rows_ref,
    grads_ref,
    active_ref,
    lifted_ref,
    store,
    total,
    produced,
    sems,
):
    chunks, _, tile = w_in_ref.shape
    core = core_ref[0]
    lines_copy = pltpu.make_async_copy(lines_hbm, lines_ref, sems.at[0])
    lines_copy.start()
    fetches = []
    for c in range(chunks):
        group = 1 - core if c < chunks // 2 else core
        at = pl.multiple_of((group * (chunks // 2) + c % (chunks // 2)) * tile, tile)
        fetches.append(
            (
                pltpu.make_async_copy(
                    w_in_hbm.at[:, pl.ds(at, tile)], w_in_ref.at[c], sems.at[1 + c]
                ),
                pltpu.make_async_copy(
                    w_out_hbm.at[pl.ds(at, tile), :], w_out_ref.at[c], sems.at[1 + chunks + c]
                ),
            )
        )
        for copy in fetches[-1]:
            copy.start()
    lines_copy.wait()
    fill_store(store, lines_ref, 0, 6, 0)
    from_lines(store, rows_ref, experts, capacity, 0)

    leaving = []
    for c in range(chunks):
        for copy in fetches[c]:
            copy.wait()
        lifted = dot(rows_ref[...], w_in_ref[c])
        if c == 0:
            fill_store(store, lines_ref, 6, 6, 6)
            from_lines(store, grads_ref, experts, capacity, 6)
        grad_active = dot(grads_ref[...], w_out_ref[c], 1, 1)
        gelu, slope = gelu_parts(lifted)
        active_ref[c] = gelu.astype(BF16)
        lifted_ref[c] = (grad_active * slope).astype(BF16)
        early = c < chunks // 2
        at = slice(c % (chunks // 2) * tile, (c % (chunks // 2) + 1) * tile)
        for i, (ref, hbm) in enumerate(
            (
                (active_ref, active_other_hbm if early else active_mine_hbm),
                (lifted_ref, lifted_other_hbm if early else lifted_mine_hbm),
            )
        ):
            copy = pltpu.make_async_copy(
                ref.at[c], hbm.at[:, at], sems.at[1 + (2 + i) * chunks + c]
            )
            copy.start()
            leaving.append(copy)
        moved = dot(lifted_ref[c], w_in_ref[c], 1, 1)
        total[...] = moved if c == 0 else total[...] + moved
        made = dot(active_ref[c], w_out_ref[c])
        if c == chunks - 1:
            to_lines(store, total, experts, capacity, 0)
            spill_store(store, back_ref, 6, 0)
        produced[...] = made if c == 0 else produced[...] + made

    to_lines(store, produced, experts, capacity, 0)
    spill_store(store, back_ref, 6, 6)
    arrived = lines_ref[:, 12 * LANES : 13 * LANES].astype(F32)
    sums = jnp.sum(arrived, axis=0, keepdims=True)
    column = lax.broadcasted_iota(jnp.int32, sums.shape, 1)
    count = jnp.sum(jnp.where(column == 0, 64.0 * sums, sums), axis=1, keepdims=True)
    upper = jnp.floor(count * (1.0 / 256.0))
    pair = jnp.where(column == 0, upper, jnp.where(column == 1, count - 256.0 * upper, 0.0))
    back_ref[:, 12 * LANES : 13 * LANES] = jnp.broadcast_to(
        pair, (back_ref.shape[0], LANES)
    ).astype(BF16)
    for copy in leaving:
        copy.wait()


def expert_gradients_kernel(
    experts,
    capacity,
    steps,
    lines_a,
    lines_b,
    active_a,
    active_b,
    lifted_a,
    lifted_b,
    out_grad_ref,
    in_grad_ref,
    store,
    rows_ref,
    grads_ref,
):
    f = pl.program_id(0)
    own = rows_ref.shape[0] // 2

    @pl.when(f == 0)
    def _():
        for i, lines in enumerate((lines_a, lines_b)):
            fill_store(store, lines, 0, 12, 0)
            here = pl.ds(i * own, own)
            from_lines(store, rows_ref.at[here], experts, capacity, 0)
            from_lines(store, grads_ref.at[here], experts, capacity, 6)

    @pl.when(f < steps)
    def _():
        active = jnp.concatenate([active_a[...], active_b[...]], axis=0)
        out_grad_ref[...] = dot(active, grads_ref[...], 0, 0)

    @pl.when(f >= steps)
    def _():
        lifted = jnp.concatenate([lifted_a[...], lifted_b[...]], axis=0)
        in_grad_ref[...] = dot(rows_ref[...], lifted, 0, 0)


def attention_pair(q, k, v, grad, probs):
    seq_len = q.shape[0]
    low = (lax.broadcasted_iota(jnp.int32, (1, LANES), 1) < 64).astype(F32)
    score_scale = 1.0 / math.sqrt(64)
    low_half = low.astype(BF16)
    high_half = (1.0 - low).astype(BF16)
    grad_both = jnp.concatenate([grad * low_half, grad * high_half], axis=0)
    query_both = jnp.concatenate([q * low_half, q * high_half], axis=0)
    grad_probs = dot(v, grad_both, 1, 1)
    values = dot(probs, grad_both)
    wide = probs.astype(F32)
    inner = jnp.sum(wide * grad_probs, axis=0, keepdims=True)
    grad_scores = (wide * (grad_probs - inner)).astype(BF16)
    keys = dot(grad_scores, query_both) * score_scale
    queries = dot(grad_scores, k, 0, 0) * score_scale
    queries = queries[:seq_len] * low + queries[seq_len:] * (1.0 - low)
    return queries.astype(BF16), keys.astype(BF16), values.astype(BF16)


def hidden_kernel(
    experts,
    capacity,
    at_ref,
    dispatch_ref,
    gain_ref,
    lines_hbm,
    hidden_hbm,
    grad_hbm,
    weight_hbm,
    mixed_hbm,
    probs_hbm,
    grad_hidden_hbm,
    branch_mine_ref,
    branch_other_ref,
    attended_hbm,
    gains_ref,
    out_hbm,
    lines_ref,
    out_ref,
    store,
    came,
    normed,
    branch_ref,
    hidden_ref,
    grad_ref,
    weight_ref,
    mixed_ref,
    probs_ref,
    grad_hidden_ref,
    attended_ref,
    sems,
):
    rows, width = hidden_ref.shape
    seq_count = probs_ref.shape[0]
    seq_len = rows // seq_count
    pairs = probs_ref.shape[1]
    half = width // 2
    core = at_ref[0]
    other = (1 - core) * pairs
    copies = [
        pltpu.make_async_copy(hidden_hbm, hidden_ref, sems.at[0]),
        pltpu.make_async_copy(grad_hbm, grad_ref, sems.at[1]),
        pltpu.make_async_copy(weight_hbm, weight_ref, sems.at[2]),
    ]
    for part in range(3):
        copies.append(
            pltpu.make_async_copy(
                mixed_hbm.at[pl.ds(2 * part * pairs + other, pairs)],
                mixed_ref.at[part],
                sems.at[3 + part],
            )
        )
    for s in range(seq_count):
        copies.append(
            pltpu.make_async_copy(
                probs_hbm.at[s, pl.ds(other, pairs)], probs_ref.at[s], sems.at[6 + s]
            )
        )
    lines_copy = pltpu.make_async_copy(
        lines_hbm.at[:, : lines_ref.shape[1]], lines_ref, sems.at[10]
    )
    lines_copy.start()
    for copy in copies:
        copy.start()
    grad_hidden_copy = pltpu.make_async_copy(grad_hidden_ref, grad_hidden_hbm, sems.at[8])
    attended_copy = pltpu.make_async_copy(attended_ref, attended_hbm, sems.at[9])

    lines_copy.wait()
    fill_store(store, lines_ref, 0, 6, 0)
    from_lines(store, came, experts, capacity, 0)
    gain = as_row(gain_ref)
    normed[...] = dot(dispatch_ref[...], came[...], 0, 0)
    gains_ref[...] = jnp.zeros_like(gains_ref)
    step = 128
    copies[0].wait()
    copies[1].wait()

    def body(i, _):
        at = pl.ds(pl.multiple_of(i * step, step), step)
        scaled, scale = normalize(hidden_ref[at, :])
        grad = normed[at, :]
        grad_hidden = grad_ref[at, :].astype(F32) + norm_backward(scaled, scale, grad * gain)
        grad_hidden_ref[at, :] = grad_hidden
        branch_ref[at, :] = grad_hidden.astype(BF16)
        gains_ref[0:1, :] += jnp.sum(grad * scaled, axis=0, keepdims=True)
        gains_ref[1:2, :] += jnp.sum(grad, axis=0, keepdims=True)
        return 0

    lax.fori_loop(0, rows // step, body, 0, unroll=2)
    grad_hidden_copy.start()
    branch_mine_ref[...] = branch_ref[:, pl.ds(pl.multiple_of(core * half, half), half)]
    branch_other_ref[...] = branch_ref[:, pl.ds(pl.multiple_of((1 - core) * half, half), half)]
    copies[2].wait()
    grad_attended = dot(branch_ref[...], weight_ref[...], 1, 1).astype(BF16)
    for tile in range(2 * pairs):
        attended_ref[tile] = grad_attended[:, tile * LANES : (tile + 1) * LANES]
    attended_copy.start()
    for copy in copies[3:]:
        copy.wait()

    def leaving(p):
        at = pl.ds(pl.multiple_of(p * LANES, LANES), LANES)
        return pltpu.make_async_copy(out_ref.at[p], out_hbm.at[:, :, at], sems.at[11 + p])

    def pair(p, _):
        for s in range(seq_count):
            here = slice(s * seq_len, (s + 1) * seq_len)
            grads = attention_pair(
                mixed_ref[0, p, here, :],
                mixed_ref[1, p, here, :],
                mixed_ref[2, p, here, :],
                attended_ref[other + p, here, :],
                probs_ref[s, p],
            )
            for part in range(3):
                out_ref[p, part, here, :] = grads[part]
        leaving(p).start()
        return 0

    lax.fori_loop(0, pairs, pair, 0)
    for p in range(pairs):
        leaving(p).wait()
    grad_hidden_copy.wait()
    attended_copy.wait()


def input_kernel(
    at_ref,
    mine_ref,
    other_ref,
    gain_ref,
    weight_hbm,
    x_hbm,
    grad_hidden_hbm,
    input_grad_hbm,
    weight_ref,
    x_ref,
    grad_hidden_ref,
    normed,
    sems,
):
    rows, width = x_ref.shape
    half = width // 2
    core = at_ref[0]
    chunks = []
    for part in range(3):
        at = slice(part * width, (part + 1) * width)
        chunks.append(
            pltpu.make_async_copy(weight_hbm.at[:, at], weight_ref.at[:, at], sems.at[part])
        )
    x_copy = pltpu.make_async_copy(x_hbm, x_ref, sems.at[3])
    grad_copy = pltpu.make_async_copy(grad_hidden_hbm, grad_hidden_ref, sems.at[4])
    for copy in (*chunks, x_copy, grad_copy):
        copy.start()
    total = None
    for part in range(3):
        chunks[part].wait()
        for ref, group in ((mine_ref, core), (other_ref, 1 - core)):
            at = pl.multiple_of(part * width + group * half, half)
            term = dot(ref[part], weight_ref[:, pl.ds(at, half)], 1, 1)
            total = term if total is None else total + term
    normed[...] = total
    gain = as_row(gain_ref)
    x_copy.wait()
    grad_copy.wait()
    step = 128
    out_copies = []
    for i in range(rows // step):
        at = slice(i * step, (i + 1) * step)
        scaled, scale = normalize(x_ref[at, :].astype(F32))
        grad_hidden_ref[at, :] += norm_backward(scaled, scale, normed[at, :] * gain)
        out_copies.append(
            pltpu.make_async_copy(grad_hidden_ref.at[at], input_grad_hbm.at[at], sems.at[5 + i])
        )
        out_copies[-1].start()
    for copy in out_copies:
        copy.wait()


def attention_kernel(
    at_ref,
    mixed_hbm,
    attended_hbm,
    probs_hbm,
    out_hbm,
    mixed_ref,
    attended_ref,
    probs_ref,
    out_ref,
    sems,
    out_sems,
):
    seq_count = probs_ref.shape[0]
    pairs, rows, _ = attended_ref.shape
    seq_len = rows // seq_count
    first = at_ref[0] * pairs

    def fetches(p):
        moves = [
            (mixed_hbm.at[2 * part * pairs + first + p], mixed_ref.at[part, p])
            for part in range(3)
        ]
        moves.append((attended_hbm.at[first + p], attended_ref.at[p]))
        for s in range(seq_count):
            moves.append((probs_hbm.at[s, first + p], probs_ref.at[s, p]))
        return [
            pltpu.make_async_copy(hbm, ref, sems.at[i, p]) for i, (hbm, ref) in enumerate(moves)
        ]

    def leaving(p):
        at = pl.ds(pl.multiple_of(p * LANES, LANES), LANES)
        return pltpu.make_async_copy(out_ref.at[p], out_hbm.at[:, :, at], out_sems.at[p])

    for p in range(pairs):
        for copy in fetches(p):
            copy.start()

    def pair(p, _):
        for copy in fetches(p):
            copy.wait()
        for s in range(seq_count):
            here = slice(s * seq_len, (s + 1) * seq_len)
            grads = attention_pair(
                mixed_ref[0, p, here, :],
                mixed_ref[1, p, here, :],
                mixed_ref[2, p, here, :],
                attended_ref[p, here, :],
                probs_ref[s, p],
            )
            for part in range(3):
                out_ref[p, part, here, :] = grads[part]
        leaving(p).start()
        return 0

    lax.fori_loop(0, pairs, pair, 0)
    for p in range(pairs):
        leaving(p).wait()


def weights_kernel(
    at_ref,
    scale_ref,
    ffn_gains_ref,
    mine_hbm,
    came_hbm,
    normed_lines_hbm,
    weight_lines_hbm,
    attended_lines_hbm,
    branch_a_hbm,
    branch_b_hbm,
    send_x_hbm,
    keep_x_hbm,
    send_z_hbm,
    keep_z_hbm,
    send_y_hbm,
    keep_y_hbm,
    right_ref,
    normed_ref,
    weight_ref,
    out_left_ref,
    branch_ref,
    x_ref,
    z_ref,
    y_ref,
    sums,
    sems,
    out_sems,
):
    rows = branch_ref.shape[0] // 2
    half = right_ref.shape[2]
    fetches = [
        (mine_hbm, right_ref.at[:, :rows]),
        (came_hbm, right_ref.at[:, rows:]),
        (normed_lines_hbm, normed_ref),
        (branch_a_hbm, branch_ref.at[:rows]),
        (branch_b_hbm, branch_ref.at[rows:]),
        (attended_lines_hbm, out_left_ref),
        (weight_lines_hbm, weight_ref),
    ]
    fetches = [
        pltpu.make_async_copy(hbm, ref, sems.at[i]) for i, (hbm, ref) in enumerate(fetches)
    ]
    for copy in fetches:
        copy.start()
    leaving = []
    for copy in fetches[:3]:
        copy.wait()
    size = x_ref.shape[1]
    lane = lax.broadcasted_iota(jnp.int32, (size, LANES), 1)
    order = order_matrix(at_ref)
    for turn, step in enumerate((1, 0)):
        lines = slice(step * size, (step + 1) * size)
        blocks = [dot(normed_ref[lines, :], right_ref[part]) for part in range(3)]
        if turn == 0:
            for part in range(3):
                total = jnp.zeros((1, half), F32)
                for at in range(0, 2 * rows, 128):
                    wide = right_ref[part, at : at + 128, :].astype(F32)
                    total = total + jnp.sum(wide, axis=0, keepdims=True)
                sums[part : part + 1, :] = total
            for copy in fetches[3:6]:
                copy.wait()
        out = dot(out_left_ref[lines, :], branch_ref[...]).astype(BF16)
        if turn == 0:
            fetches[6].wait()
        gain = jnp.zeros((size, 1), F32)
        shift = jnp.zeros((size, 1), F32)
        for part in range(3):
            weight = weight_ref[lines, part * half : (part + 1) * half].astype(F32)
            gain = gain + jnp.sum(blocks[part] * weight, axis=1, keepdims=True)
            shift = shift + jnp.sum(sums[part : part + 1, :] * weight, axis=1, keepdims=True)
        parts = [block.astype(BF16) for block in blocks]
        x_ref[step, :, :half] = parts[0]
        x_ref[step, :, half:] = out[:, : half // 2]
        side = out[:, half // 2 : 3 * half // 4]
        for group in range(size // 16):
            x, chip = group // 16, group % 16
            here = slice(group * 16, (group + 1) * 16)
            z_ref[step, chip, x, :, :half] = parts[1][here]
            z_ref[step, chip, x, :, half:] = side[here]
        scale = scale_ref[lines, :]
        gain = (gain - scale[:, 1:2] * shift) / scale[:, 0:1]
        ffn = []
        for i in range(size // 256):
            block_at = at_ref[4 + step * (size // 256) + i]
            ffn.append(
                lax.dot_general(
                    order,
                    ffn_gains_ref[:, pl.ds(pl.multiple_of(block_at * 256, 256), 256)],
                    (((1,), (1,)), ((), ())),
                    precision=lax.Precision.HIGHEST,
                    preferred_element_type=F32,
                )
            )
        ffn = jnp.concatenate(ffn, axis=0)
        small = jnp.where(lane == 0, gain, jnp.where(lane == 1, shift, 0.0))
        small = jnp.where(lane == 2, ffn[:, 0:1], jnp.where(lane == 3, ffn[:, 1:2], small))
        small = small.astype(BF16)
        side = out[:, 3 * half // 4 :]
        for group in range(size // 16):
            x, z, y = group // 16, group // 4 % 4, group % 4
            here = slice(group * 16, (group + 1) * 16)
            y_ref[step, y, x, z, :, :half] = parts[2][here]
            y_ref[step, y, x, z, :, half : half + LANES] = side[here]
            y_ref[step, y, x, z, :, half + LANES :] = small[here]
        x_at = pl.ds(2 * step, 2)
        moves = [
            (x_ref.at[step], send_x_hbm if step == 1 else keep_x_hbm),
            (z_ref.at[step, 8:16], send_z_hbm.at[:, x_at]),
            (z_ref.at[step, 0:8], keep_z_hbm.at[:, x_at]),
            (y_ref.at[step, 2:4], send_y_hbm.at[:, x_at]),
            (y_ref.at[step, 0:2], keep_y_hbm.at[:, x_at]),
        ]
        for i, (ref, hbm) in enumerate(moves):
            copy = pltpu.make_async_copy(ref, hbm, out_sems.at[turn * 5 + i])
            copy.start()
            leaving.append(copy)
    for copy in leaving:
        copy.wait()


def second_kernel(kept_ref, first_ref, send_ref):
    send_ref[...] = (kept_ref[...].astype(F32) + first_ref[...].astype(F32)).astype(BF16)


def third_kernel(kept_ref, first_ref, second_ref, send_ref):
    total = kept_ref[...].astype(F32) + first_ref[...].astype(F32) + second_ref[...].astype(F32)
    send_ref[...] = total.astype(BF16)


def merge_kernel(*refs):
    parts = [refs[4 * i : 4 * i + 4] for i in range(3)]
    send_ref, keep_ref = refs[12:]
    for x in range(2):
        for z in range(2):
            for y in range(2):
                at = 0
                for part, spot in zip(parts, ((x, z, y), (z, y, x), (y, x, z))):
                    total = part[0][spot].astype(F32)
                    for ref in part[1:]:
                        total = total + ref[spot].astype(F32)
                    span = total.shape[1]
                    if x == 1:
                        send_ref[z, y, :, at : at + span] = total.astype(BF16)
                    else:
                        keep_ref[z, y, :, at : at + span] = total
                    at += span


def split_kernel(at_ref, kept_ref, came_ref, mine_ref, other_ref, store):
    store[...] = kept_ref[...] + came_ref[...].astype(F32)
    core = at_ref[0]
    mine_ref[...] = store[pl.ds(pl.multiple_of(core * 8, 8), 8), :]
    other_ref[...] = store[pl.ds(pl.multiple_of((1 - core) * 8, 8), 8), :]


def join_kernel(spans, at_ref, mine_ref, other_ref, qkv_ref, out_ref, small_ref):
    half = out_ref.shape[1] // 2
    core = at_ref[0]
    for ref, group in ((mine_ref, core), (other_ref, 1 - core)):
        group_at = group * half
        at, out_at = 0, 0
        for part, span in enumerate(spans):
            spot = pl.multiple_of(2 * part * half + group_at, half)
            qkv_ref[:, pl.ds(spot, half)] = ref[:, at : at + half]
            side = span - half
            spot = pl.multiple_of(group_at + out_at, LANES)
            out_ref[:, pl.ds(spot, side)] = ref[:, at + half : at + span]
            at += span
            out_at += side
    small_ref[...] = mine_ref[:, at : at + LANES] + other_ref[:, at : at + LANES]


def output_kernel(experts, capacity, lines_ref, dispatch_ref, hidden_ref, out_ref, store, came):
    fill_store(store, lines_ref, 0, 6, 6)
    from_lines(store, came, experts, capacity, 0)
    back = dot(dispatch_ref[...], came[...], 0, 0)
    out_ref[...] = (hidden_ref[...] + back).astype(BF16)


def whole(shape):
    return pl.BlockSpec(shape, lambda *_: (0,) * len(shape))


def shaped(shape, dtype):
    return jax.ShapeDtypeStruct(shape, dtype)


def per_device(
    block_input,
    attn_gain,
    attn_shift,
    query_key_value_weight,
    output_weight,
    ffn_gain,
    ffn_shift,
    expert_in,
    expert_out,
    hash_ids,
    seq_lengths,
    prev_counts,
    out_grad,
):
    seq_count, seq_len, width = block_input.shape
    rows = seq_count * seq_len
    chips = lax.axis_size(WIDE)
    experts = chips
    capacity = max(2, 3 * rows // (4 * experts))
    n_slots = experts * capacity
    ff_width = expert_in.shape[2]
    half_ff = ff_width // 2
    half = width // 2
    pairs = HEADS // 2
    lines = 8 * chips
    core = lax.axis_index("narrow").astype(jnp.int32)
    core_at = core.reshape(1)
    other_at = (1 - core).reshape(1)
    x = block_input.reshape(rows, width)
    grad_rows = out_grad.reshape(rows, width)
    w_in = expert_in[0]
    w_out = expert_out[0]
    scales = [v.reshape(8, LANES) for v in (attn_gain, attn_shift, ffn_gain, ffn_shift)]
    smem = pl.BlockSpec(memory_space=pltpu.SMEM)
    vmem = pl.BlockSpec(memory_space=pltpu.VMEM)
    hbm = pl.BlockSpec(memory_space=pl.ANY)
    coordinates = [lax.axis_index(name).astype(jnp.int32) for name in WIDE]
    blocks_x = [places(place, core) ^ coordinates[0] for place in range(4)]
    spot = jnp.stack([core] + coordinates + blocks_x).astype(jnp.int32)

    normed, mixed, probs, attended, hidden, dispatch, send = pl.pallas_call(
        functools.partial(forward_kernel, experts, capacity),
        out_shape=(
            shaped((rows, width), BF16),
            shaped((3 * pairs, rows, LANES), BF16),
            shaped((seq_count, pairs, seq_len, 2 * seq_len), BF16),
            shaped((rows, width), BF16),
            shaped((rows, width), F32),
            shaped((n_slots, rows), BF16),
            shaped((lines, 13 * LANES), BF16),
        ),
        in_specs=[smem] + [vmem] * 6 + [hbm] * 3,
        out_specs=[hbm] * 5 + [vmem] * 2,
        scratch_shapes=[
            pltpu.VMEM((width, 3 * width), BF16),
            pltpu.VMEM((width, width), BF16),
            pltpu.VMEM((rows, width), BF16),
            pltpu.VMEM((rows, width), BF16),
            pltpu.VMEM((3 * pairs, rows, LANES), BF16),
            pltpu.VMEM((seq_count, pairs, seq_len, 2 * seq_len), BF16),
            pltpu.VMEM((rows, width), BF16),
            pltpu.VMEM((rows, width), F32),
            pltpu.VMEM((rows, width), BF16),
            pltpu.VMEM((seq_count, seq_len, 2 * seq_len), F32),
            pltpu.VMEM((13, lines, LANES), F32),
            pltpu.SemaphoreType.DMA((10,)),
        ],
        compiler_params=params(60),
        name="forward",
        cost_estimate=cost(10, 20),
    )(
        seq_lengths,
        hash_ids,
        x,
        *scales,
        query_key_value_weight,
        output_weight,
        grad_rows,
    )
    arrived = exchanged(send)
    normed_other = swapped(normed)
    attended_other = swapped(attended)
    block = width // 4
    column = pl.BlockSpec((rows, block), lambda i, at: (0, at[4 + i]))
    weight_part = [
        pl.BlockSpec((block, half), lambda i, at, part=part: (at[4 + i], 2 * part + at[0]))
        for part in range(3)
    ]
    normed_lines, attended_lines, weight_lines, scale_lines = pl.pallas_call(
        prepare_kernel,
        out_shape=(
            shaped((width, 2 * rows), BF16),
            shaped((width, 2 * rows), BF16),
            shaped((width, 3 * half), BF16),
            shaped((width, LANES), F32),
        ),
        grid_spec=pltpu.PrefetchScalarGridSpec(
            num_scalar_prefetch=1,
            grid=(4,),
            in_specs=[column] * 4 + weight_part + [whole((8, LANES))] * 2,
            out_specs=[
                pl.BlockSpec((block, 2 * rows), lambda i, at: (i, 0)),
                pl.BlockSpec((block, 2 * rows), lambda i, at: (i, 0)),
                pl.BlockSpec((block, 3 * half), lambda i, at: (i, 0)),
                pl.BlockSpec((block, LANES), lambda i, at: (i, 0)),
            ],
        ),
        compiler_params=params(60),
        name="prepare",
        cost_estimate=cost(4, 8),
    )(
        spot,
        normed,
        normed_other,
        attended,
        attended_other,
        query_key_value_weight,
        query_key_value_weight,
        query_key_value_weight,
        *scales[:2],
    )
    arrived, normed_lines = lax.optimization_barrier((arrived, normed_lines))

    chunks = 4
    tile = ff_width // chunks
    half_block = shaped((n_slots, half_ff), BF16)
    active_other, active_mine, lifted_other, lifted_mine, back = pl.pallas_call(
        functools.partial(expert_kernel, experts, capacity),
        out_shape=(
            half_block,
            half_block,
            half_block,
            half_block,
            shaped((lines, 13 * LANES), BF16),
        ),
        in_specs=[smem] + [hbm] * 3,
        out_specs=[hbm] * 4 + [vmem],
        scratch_shapes=[
            pltpu.VMEM((lines, 13 * LANES), BF16),
            pltpu.VMEM((chunks, width, tile), BF16),
            pltpu.VMEM((chunks, tile, width), BF16),
            pltpu.VMEM((n_slots, width), BF16),
            pltpu.VMEM((n_slots, width), BF16),
            pltpu.VMEM((chunks, n_slots, tile), BF16),
            pltpu.VMEM((chunks, n_slots, tile), BF16),
            pltpu.VMEM((12, lines, LANES), F32),
            pltpu.VMEM((n_slots, width), F32),
            pltpu.VMEM((n_slots, width), F32),
            pltpu.SemaphoreType.DMA((1 + 4 * chunks,)),
        ],
        compiler_params=params(60),
        name="expert",
        cost_estimate=cost(16, 25),
    )(spot, arrived, w_in, w_out)
    returned = exchanged(back)

    arrived_other = swapped(arrived)
    active_came = swapped(active_other)
    lifted_came = swapped(lifted_other)
    steps = 4
    tile = half_ff // steps
    early = pl.BlockSpec((n_slots, tile), lambda f: (0, jnp.minimum(f, steps - 1)))
    late = pl.BlockSpec((n_slots, tile), lambda f: (0, jnp.maximum(f - steps, 0)))
    expert_out_grad, expert_in_grad = pl.pallas_call(
        functools.partial(expert_gradients_kernel, experts, capacity, steps),
        out_shape=(shaped((half_ff, width), F32), shaped((width, half_ff), F32)),
        grid=(2 * steps,),
        in_specs=[whole((lines, 13 * LANES))] * 2 + [early] * 2 + [late] * 2,
        out_specs=[
            pl.BlockSpec((tile, width), lambda f: (jnp.minimum(f, steps - 1), 0)),
            pl.BlockSpec((width, tile), lambda f: (0, jnp.maximum(f - steps, 0))),
        ],
        scratch_shapes=[
            pltpu.VMEM((12, lines, LANES), F32),
            pltpu.VMEM((2 * n_slots, width), BF16),
            pltpu.VMEM((2 * n_slots, width), BF16),
        ],
        compiler_params=params(60),
        name="expert_gradients",
        cost_estimate=cost(10, 30),
    )(arrived, arrived_other, active_mine, active_came, lifted_mine, lifted_came)
    returned, expert_out_grad, expert_in_grad = lax.optimization_barrier(
        (returned, expert_out_grad, expert_in_grad)
    )

    half_pairs = pairs // 2
    grad_hidden, branch, branch_out, grad_attended, ffn_gains, mixed_out = pl.pallas_call(
        functools.partial(hidden_kernel, experts, capacity),
        out_shape=(
            shaped((rows, width), F32),
            shaped((rows, half), BF16),
            shaped((rows, half), BF16),
            shaped((pairs, rows, LANES), BF16),
            shaped((8, width), F32),
            shaped((3, rows, half), BF16),
        ),
        in_specs=[smem, vmem, vmem] + [hbm] * 6,
        out_specs=[hbm, vmem, vmem, hbm, vmem, hbm],
        scratch_shapes=[
            pltpu.VMEM((lines, 6 * LANES), BF16),
            pltpu.VMEM((half_pairs, 3, rows, LANES), BF16),
            pltpu.VMEM((6, lines, LANES), F32),
            pltpu.VMEM((n_slots, width), BF16),
            pltpu.VMEM((rows, width), F32),
            pltpu.VMEM((rows, width), BF16),
            pltpu.VMEM((rows, width), F32),
            pltpu.VMEM((rows, width), BF16),
            pltpu.VMEM((width, width), BF16),
            pltpu.VMEM((3, half_pairs, rows, LANES), BF16),
            pltpu.VMEM((seq_count, half_pairs, seq_len, 2 * seq_len), BF16),
            pltpu.VMEM((rows, width), F32),
            pltpu.VMEM((pairs, rows, LANES), BF16),
            pltpu.SemaphoreType.DMA((11 + half_pairs,)),
        ],
        compiler_params=params(60),
        name="hidden_backward",
        cost_estimate=cost(6, 14),
    )(spot, dispatch, scales[2], returned, hidden, grad_rows, output_weight, mixed, probs)
    mixed_came = swapped(mixed_out)
    branch_other = swapped(branch_out)

    spans = (half + half // 2, half + half // 4, half + half // 2)
    shapes = ((512,), (8, 4, 16), (2, 4, 4, 16))
    mixed_mine = pl.pallas_call(
        attention_kernel,
        out_shape=shaped((3, rows, half), BF16),
        in_specs=[smem] + [hbm] * 3,
        out_specs=hbm,
        scratch_shapes=[
            pltpu.VMEM((3, half_pairs, rows, LANES), BF16),
            pltpu.VMEM((half_pairs, rows, LANES), BF16),
            pltpu.VMEM((seq_count, half_pairs, seq_len, 2 * seq_len), BF16),
            pltpu.VMEM((half_pairs, 3, rows, LANES), BF16),
            pltpu.SemaphoreType.DMA((6, half_pairs)),
            pltpu.SemaphoreType.DMA((half_pairs,)),
        ],
        compiler_params=params(60),
        name="attention_backward",
        cost_estimate=cost(4, 5),
    )(spot, mixed, grad_attended, probs)
    halves = pl.pallas_call(
        weights_kernel,
        out_shape=[
            shaped(shape + (span,), BF16) for shape, span in zip(shapes, spans) for _ in range(2)
        ],
        in_specs=[smem, vmem, vmem] + [hbm] * 7,
        out_specs=[hbm] * 6,
        scratch_shapes=[
            pltpu.VMEM((3, 2 * rows, half), BF16),
            pltpu.VMEM((width, 2 * rows), BF16),
            pltpu.VMEM((width, 3 * half), BF16),
            pltpu.VMEM((width, 2 * rows), BF16),
            pltpu.VMEM((2 * rows, half), BF16),
            pltpu.VMEM((2, 512, spans[0]), BF16),
            pltpu.VMEM((2, 16, 2, 16, spans[1]), BF16),
            pltpu.VMEM((2, 4, 2, 4, 16, spans[2]), BF16),
            pltpu.VMEM((8, half), F32),
            pltpu.SemaphoreType.DMA((7,)),
            pltpu.SemaphoreType.DMA((10,)),
        ],
        compiler_params=params(60),
        name="weight_gradients",
        cost_estimate=cost(8, 20),
    )(
        spot,
        scale_lines,
        ffn_gains,
        mixed_mine,
        mixed_came,
        normed_lines,
        weight_lines,
        attended_lines,
        branch,
        branch_other,
    )

    input_grad = pl.pallas_call(
        input_kernel,
        out_shape=shaped((rows, width), F32),
        in_specs=[smem, vmem, vmem, vmem, hbm, hbm, hbm],
        out_specs=hbm,
        scratch_shapes=[
            pltpu.VMEM((width, 3 * width), BF16),
            pltpu.VMEM((rows, width), BF16),
            pltpu.VMEM((rows, width), F32),
            pltpu.VMEM((rows, width), F32),
            pltpu.SemaphoreType.DMA((9,)),
        ],
        compiler_params=params(60),
        name="input_backward",
        cost_estimate=cost(6, 14),
    )(spot, mixed_mine, mixed_out, scales[0], query_key_value_weight, x, grad_hidden)

    block_output = pl.pallas_call(
        functools.partial(output_kernel, experts, capacity),
        out_shape=shaped((rows, width), BF16),
        grid=(1,),
        in_specs=[
            whole((lines, 13 * LANES)),
            whole((n_slots, rows)),
            whole((rows, width)),
        ],
        out_specs=whole((rows, width)),
        scratch_shapes=[
            pltpu.VMEM((6, lines, LANES), F32),
            pltpu.VMEM((n_slots, width), BF16),
        ],
        compiler_params=params(60),
        name="block_output",
        cost_estimate=cost(1, 5),
    )(returned, dispatch, hidden)

    orders = ((0, 1, 2), (1, 2, 0), (2, 0, 1))
    sent = [part.reshape(2, 4, 4, 16, -1) for part in halves[0::2]]
    kept = [part.reshape(2, 4, 4, 16, -1) for part in halves[1::2]]
    first = [crossed(part, order[0], True) for part, order in zip(sent, orders)]
    first, input_grad = lax.optimization_barrier((first, input_grad))

    def cut(span, shape, at):
        return pl.BlockSpec(shape + (16, span), lambda *_: at + (0, 0))

    def added(kernel, arrays, shape, spots, name):
        span = arrays[0].shape[-1]
        return pl.pallas_call(
            kernel,
            out_shape=shaped(shape + (16, span), BF16),
            grid=(1,),
            in_specs=[cut(span, shape, at) for at in spots],
            out_specs=whole(shape + (16, span)),
            compiler_params=params(16),
            name=name,
            cost_estimate=cost(0.01, 2),
        )(*arrays)

    second = []
    for k, c, order in zip(kept, first, orders):
        send = added(second_kernel, (k, c), (2, 2, 4), ((0, 1, 0),) * 2, "second")
        second.append(crossed(send, order[1], True))
    third = []
    for k, c, d, order in zip(kept, first, second, orders):
        spots = ((0, 0, 1),) * 3
        send = added(third_kernel, (k, c, d), (2, 2, 2), spots, "third")
        third.append(crossed(send, order[2], True))
    total_span = sum(spans)
    send, keep = pl.pallas_call(
        merge_kernel,
        out_shape=(
            shaped((2, 2, 16, total_span), BF16),
            shaped((2, 2, 16, total_span), F32),
        ),
        grid=(1,),
        in_specs=[cut(span, (2, 2, 2), (0, 0, 0)) for span in spans for _ in range(4)],
        out_specs=[whole((2, 2, 16, total_span))] * 2,
        compiler_params=params(16),
        name="merge",
        cost_estimate=cost(0.01, 4),
    )(*(array for group in zip(kept, first, second, third) for array in group))
    came = crossed(send, 0, False)
    for axis in (1, 2):
        keep = keep + came.astype(F32)
        came = crossed(keep[1].astype(BF16), axis, False)
        keep = keep[0]
    own, other = pl.pallas_call(
        split_kernel,
        out_shape=(shaped((8, total_span), F32), shaped((8, total_span), F32)),
        in_specs=[smem, vmem, vmem],
        out_specs=[vmem, vmem],
        scratch_shapes=[pltpu.VMEM((16, total_span), F32)],
        compiler_params=params(16),
        name="split",
    )(spot, keep, came)
    qkv_grad, out_weight_grad, vectors = pl.pallas_call(
        functools.partial(join_kernel, (*spans[:2], half + half // 4)),
        out_shape=(
            shaped((8, 3 * width), F32),
            shaped((8, width), F32),
            shaped((8, LANES), F32),
        ),
        in_specs=[smem, vmem, vmem],
        out_specs=[vmem] * 3,
        compiler_params=params(16),
        name="join",
    )(spot, own, swapped(other))

    pair = returned[:, 12 * LANES : 12 * LANES + 2].reshape(chips, 8, 2)[:, 0].astype(F32)
    counts = 256.0 * pair[:, 0] + pair[:, 1]
    counts = counts + swapped(counts)
    total_tokens = float(rows * chips * 2)
    new_average = (momentum * prev_counts.astype(F32) + (1.0 - momentum) * counts) * (
        float(experts) / total_tokens
    )
    return (
        block_output.reshape(seq_count, seq_len, width),
        input_grad.reshape(seq_count, seq_len, width),
        vectors[:, 0],
        vectors[:, 1],
        qkv_grad,
        out_weight_grad,
        vectors[:, 2],
        vectors[:, 3],
        expert_in_grad[None],
        expert_out_grad[None],
        new_average,
    )


def solution(mesh):
    finer = Mesh(
        mesh.devices.reshape(4, 4, 4, mesh.shape["narrow"]),
        ("wide_0", "wide_1", "wide_2", "narrow"),
    )
    placed = (
        P(WIDE_NARROW, None, None),
        P(),
        P(),
        P(),
        P(),
        P(),
        P(),
        P(WIDE, None, None),
        P(WIDE, None, None),
        P(WIDE_NARROW, None),
        P(WIDE_NARROW),
        P(),
        P(WIDE_NARROW, None, None),
    )
    return jax.shard_map(
        per_device,
        mesh=finer,
        in_specs=placed,
        out_specs=(
            P(WIDE_NARROW, None, None),
            P(WIDE_NARROW, None, None),
            P(WIDE_NARROW),
            P(WIDE_NARROW),
            P(WIDE_NARROW, None),
            P(WIDE_NARROW, None),
            P(WIDE_NARROW),
            P(WIDE_NARROW),
            P(WIDE, None, "narrow"),
            P(WIDE, "narrow", None),
            P(),
        ),
        check_vma=False,
    )
```

```python
import functools
import math

import jax
import jax.experimental.pallas as pl
import jax.experimental.pallas.tpu as pltpu
import jax.numpy as jnp
from jax import lax
from jax.sharding import Mesh
from jax.sharding import PartitionSpec as P

HEADS = 16
WIDE = ("wide_0", "wide_1", "wide_2")
WIDE_NARROW = ("wide_0", "wide_1", "wide_2", "narrow")

norm_eps = 1e-05
momentum = 0.9
F32 = jnp.float32
BF16 = jnp.bfloat16
LANES = 128
MIB = 1 << 20


def swapped(shard):
    return lax.ppermute(shard, "narrow", [(0, 1), (1, 0)])


def exchanged(lines):
    shard = lines.reshape(lax.axis_size(WIDE), -1, lines.shape[1])
    return lax.all_to_all(shard, WIDE, 0, 0, tiled=True).reshape(lines.shape)


def crossed(shard, axis, first):
    pairs = []
    for i in range(lax.axis_size(WIDE[axis])):
        for core in range(2):
            flip = 1 if first == (core == 0) else 3
            pairs.append((i * 2 + core, (i ^ flip) * 2 + core))
    return lax.ppermute(shard, (WIDE[axis], "narrow"), pairs)


def dot(left, right, left_dim=1, right_dim=0):
    return lax.dot_general(
        left, right, (((left_dim,), (right_dim,)), ((), ())), preferred_element_type=F32
    )


def params(mib):
    return pltpu.CompilerParams(vmem_limit_bytes=mib * MIB)


def cost(gigaflops, megabytes):
    return pl.CostEstimate(
        flops=int(gigaflops * 1e9), bytes_accessed=int(megabytes * 1e6), transcendentals=0
    )


def normalize(features):
    centered = features - jnp.mean(features, axis=-1, keepdims=True)
    spread = jnp.mean(centered * centered, axis=-1, keepdims=True)
    scale = lax.rsqrt(spread + norm_eps)
    return centered * scale, scale


def as_row(tile_ref):
    tile = tile_ref[...].astype(F32)
    return jnp.concatenate([tile[i : i + 1, :] for i in range(tile.shape[0])], axis=1)


def norm_backward(scaled, scale, gained):
    mean = jnp.mean(gained, axis=-1, keepdims=True)
    along = jnp.mean(gained * scaled, axis=-1, keepdims=True)
    return scale * (gained - mean - scaled * along)


def to_lines(store, rows, experts, capacity, lane_tile):
    for rank in range(capacity):
        for part in range(8):
            store[lane_tile + rank, pl.ds(part, experts, stride=8), :] = rows[
                rank * experts : (rank + 1) * experts, part * LANES : (part + 1) * LANES
            ]


def from_lines(store, rows_ref, experts, capacity, lane_tile):
    for rank in range(capacity):
        for part in range(8):
            rows_ref[
                rank * experts : (rank + 1) * experts, part * LANES : (part + 1) * LANES
            ] = store[lane_tile + rank, pl.ds(part, experts, stride=8), :].astype(BF16)


def fill_store(store, lines_ref, lane_tile, count, source_tile):
    for tile in range(count):
        at = (source_tile + tile) * LANES
        store[lane_tile + tile] = lines_ref[:, at : at + LANES].astype(F32)


def spill_store(store, lines_ref, count, target_tile):
    for tile in range(count):
        at = (target_tile + tile) * LANES
        lines_ref[:, at : at + LANES] = store[tile].astype(BF16)


def forward_kernel(
    experts,
    capacity,
    len_ref,
    ids_ref,
    x_ref,
    gain_one_ref,
    shift_one_ref,
    gain_two_ref,
    shift_two_ref,
    qkv_weight_hbm,
    out_weight_hbm,
    grad_hbm,
    normed_hbm,
    mixed_hbm,
    probs_hbm,
    attended_hbm,
    hidden_hbm,
    dispatch_ref,
    send_ref,
    qkv_weight_ref,
    out_weight_ref,
    grad_ref,
    normed_ref,
    mixed_ref,
    probs_ref,
    attended_ref,
    hidden_ref,
    moved_ref,
    barred,
    store,
    sems,
):
    rows, width = x_ref.shape
    seq_count, seq_len = ids_ref.shape
    pieces = 3
    span = 3 * width // pieces

    def fetch(i):
        at = slice(i * span, (i + 1) * span)
        return pltpu.make_async_copy(qkv_weight_hbm.at[:, at], qkv_weight_ref.at[:, at], sems.at[i])

    out_weight_copy = pltpu.make_async_copy(out_weight_hbm, out_weight_ref, sems.at[3])
    grad_copy = pltpu.make_async_copy(grad_hbm, grad_ref, sems.at[4])
    for i in range(pieces):
        fetch(i).start()
    out_weight_copy.start()
    grad_copy.start()
    normed_copy = pltpu.make_async_copy(normed_ref, normed_hbm, sems.at[5])
    mixed_copy = pltpu.make_async_copy(mixed_ref, mixed_hbm, sems.at[6])
    probs_copy = pltpu.make_async_copy(probs_ref, probs_hbm, sems.at[7])
    attended_copy = pltpu.make_async_copy(attended_ref, attended_hbm, sems.at[8])
    hidden_copy = pltpu.make_async_copy(hidden_ref, hidden_hbm, sems.at[9])

    gain_one, shift_one = as_row(gain_one_ref), as_row(shift_one_ref)
    gain_two, shift_two = as_row(gain_two_ref), as_row(shift_two_ref)
    step = 128

    def norm_one(i, _):
        at = pl.ds(pl.multiple_of(i * step, step), step)
        scaled, _ = normalize(x_ref[at, :].astype(F32))
        normed_ref[at, :] = (scaled * gain_one + shift_one).astype(BF16)
        return 0

    lax.fori_loop(0, rows // step, norm_one, 0, unroll=2)
    normed_copy.start()

    ids = jnp.concatenate([ids_ref[s : s + 1, :] for s in range(seq_count)], axis=1)
    lane = lax.broadcasted_iota(jnp.int32, (1, rows), 1)
    length = jnp.where(lane < seq_len, len_ref[0], len_ref[1])
    is_valid = lane % seq_len < length
    member = (lax.broadcasted_iota(jnp.int32, (experts, rows), 0) == ids) & is_valid
    onehot = member.astype(F32)
    earlier = (
        lax.broadcasted_iota(jnp.int32, (rows, rows), 0)
        < lax.broadcasted_iota(jnp.int32, (rows, rows), 1)
    ).astype(F32)
    before = dot(onehot.astype(BF16), earlier.astype(BF16))
    rank = jnp.sum(onehot * before, axis=0, keepdims=True).astype(jnp.int32)
    slot = jnp.where(is_valid & (rank < capacity), rank * experts + ids, -1)
    at_slot = lax.broadcasted_iota(jnp.int32, (experts * capacity, rows), 0)
    dispatch_ref[...] = (at_slot == slot).astype(F32).astype(BF16)
    counts = jnp.sum(onehot, axis=1, keepdims=True)
    upper = jnp.floor(counts * (1.0 / 64.0))
    column = lax.broadcasted_iota(jnp.int32, (experts, LANES), 1)
    store[12] = jnp.zeros(store.shape[1:], F32)
    store[12, pl.ds(0, experts, stride=8), :] = jnp.where(
        column == 0, upper, jnp.where(column == 1, counts - 64.0 * upper, 0.0)
    )

    for i in range(pieces):
        fetch(i).wait()

        def project(j, _):
            at = pl.ds(pl.multiple_of(i * span + j * 512, 512), 512)
            block = dot(normed_ref[...], qkv_weight_ref[:, at]).astype(BF16)
            for tile in range(4):
                mixed_ref[(i * span + j * 512) // LANES + tile] = block[
                    :, tile * LANES : (tile + 1) * LANES
                ]
            return 0

        lax.fori_loop(0, span // 512, project, 0)
    mixed_copy.start()

    pairs = HEADS // 2
    low = (lax.broadcasted_iota(jnp.int32, (1, LANES), 1) < 64).astype(F32)
    score_scale = 1.0 / math.sqrt(width // HEADS)
    low_scaled = (low * score_scale).astype(BF16)
    high_scaled = ((1.0 - low) * score_scale).astype(BF16)
    query_at = lax.broadcasted_iota(jnp.int32, (seq_len, 2 * seq_len), 1) % seq_len
    key_at = lax.broadcasted_iota(jnp.int32, (seq_len, 2 * seq_len), 0)
    for s in range(seq_count):
        allowed = (key_at <= query_at) & (key_at < len_ref[s])
        barred[s] = jnp.where(allowed, 0.0, -3e38)

    def attend(p, _):
        at = pl.multiple_of(p * LANES, LANES)
        for s in range(seq_count):
            here = slice(s * seq_len, (s + 1) * seq_len)
            q = mixed_ref[p, here, :]
            k = mixed_ref[pairs + p, here, :]
            v = mixed_ref[2 * pairs + p, here, :]
            both = jnp.concatenate([q * low_scaled, q * high_scaled], axis=0)
            scores = dot(k, both, 1, 1) + barred[s]
            raised = jnp.exp(scores - jnp.max(scores, axis=0, keepdims=True))
            total = jnp.sum(raised, axis=0, keepdims=True)
            probs = (raised * (1.0 / total)).astype(BF16)
            probs_ref[s, p] = probs
            out = dot(probs, v, 0, 0)
            out = out[:seq_len] * low + out[seq_len:] * (1.0 - low)
            attended_ref[here, pl.ds(at, LANES)] = out.astype(BF16)
        return 0

    lax.fori_loop(0, pairs, attend, 0, unroll=4)
    probs_copy.start()
    attended_copy.start()

    out_weight_copy.wait()

    def norm_two(i, _):
        at = pl.ds(pl.multiple_of(i * 256, 256), 256)
        hidden = x_ref[at, :].astype(F32) + dot(attended_ref[at, :], out_weight_ref[...])
        hidden_ref[at, :] = hidden
        scaled, _ = normalize(hidden)
        moved_ref[at, :] = (scaled * gain_two + shift_two).astype(BF16)
        return 0

    lax.fori_loop(0, rows // 256, norm_two, 0, unroll=True)
    hidden_copy.start()

    grad_copy.wait()
    to_lines(store, dot(dispatch_ref[...], grad_ref[...]), experts, capacity, 6)
    to_lines(store, dot(dispatch_ref[...], moved_ref[...]), experts, capacity, 0)
    spill_store(store, send_ref, 13, 0)
    for copy in (normed_copy, mixed_copy, probs_copy, attended_copy, hidden_copy):
        copy.wait()


def places(position, core):
    near = 1 + 2 * core
    return jnp.where(
        position == 0,
        0,
        jnp.where(position == 1, 4 - near, jnp.where(position == 2, near, 2)),
    )


def order_matrix(at_ref):
    line = lax.broadcasted_iota(jnp.int32, (256, 256), 0)
    column = lax.broadcasted_iota(jnp.int32, (256, 256), 1)
    core, z, y = at_ref[0], at_ref[2], at_ref[3]
    source_z = places(line // 64, core) ^ z
    source_y = places(line // 16 % 4, core) ^ y
    return (column == source_z * 64 + source_y * 16 + line % 16).astype(F32)


def prepare_kernel(
    at_ref,
    normed_a,
    normed_b,
    attended_a,
    attended_b,
    query_ref,
    key_ref,
    value_ref,
    gain_ref,
    shift_ref,
    normed_ref,
    attended_ref,
    weight_ref,
    scale_ref,
):
    order = order_matrix(at_ref).astype(BF16)
    rows = normed_a.shape[0]
    normed_ref[:, :rows] = dot(order, normed_a[...], 1, 1).astype(BF16)
    normed_ref[:, rows:] = dot(order, normed_b[...], 1, 1).astype(BF16)
    attended_ref[:, :rows] = dot(order, attended_a[...], 1, 1).astype(BF16)
    attended_ref[:, rows:] = dot(order, attended_b[...], 1, 1).astype(BF16)
    half = query_ref.shape[1]
    for part, ref in enumerate((query_ref, key_ref, value_ref)):
        weight_ref[:, part * half : (part + 1) * half] = dot(order, ref[...]).astype(BF16)
    tile_at = 2 * at_ref[4 + pl.program_id(0)]
    tile = lax.broadcasted_iota(jnp.int32, (8, LANES), 0)
    line = lax.broadcasted_iota(jnp.int32, (LANES, 256), 0)

    def columns(ref):
        wide = ref[...].astype(F32)
        parts = [
            jnp.sum(jnp.where(tile == tile_at + i, wide, 0.0), axis=0, keepdims=True)
            for i in range(2)
        ]
        return jnp.concatenate(parts, axis=1)

    both = jnp.where(line == 0, columns(gain_ref), jnp.where(line == 1, columns(shift_ref), 0.0))
    scale_ref[...] = dot(order, both.astype(BF16), 1, 1)


def gelu_parts(u):
    inner = 0.7978845608028654 * (u + 0.044715 * (u * u * u))
    t = jnp.tanh(inner)
    half = 0.5 * (1.0 + t)
    slope = half + 0.5 * u * (1.0 - t * t) * (0.7978845608028654 * (1.0 + 0.134145 * (u * u)))
    return u * half, slope


def expert_kernel(
    experts,
    capacity,
    core_ref,
    lines_hbm,
    w_in_hbm,
    w_out_hbm,
    active_other_hbm,
    active_mine_hbm,
    lifted_other_hbm,
    lifted_mine_hbm,
    back_ref,
    lines_ref,
    w_in_ref,
    w_out_ref,
    rows_ref,
    grads_ref,
    active_ref,
    lifted_ref,
    store,
    total,
    produced,
    sems,
):
    chunks, _, tile = w_in_ref.shape
    core = core_ref[0]
    lines_copy = pltpu.make_async_copy(lines_hbm, lines_ref, sems.at[0])
    lines_copy.start()
    fetches = []
    for c in range(chunks):
        group = 1 - core if c < chunks // 2 else core
        at = pl.multiple_of((group * (chunks // 2) + c % (chunks // 2)) * tile, tile)
        fetches.append(
            (
                pltpu.make_async_copy(
                    w_in_hbm.at[:, pl.ds(at, tile)], w_in_ref.at[c], sems.at[1 + c]
                ),
                pltpu.make_async_copy(
                    w_out_hbm.at[pl.ds(at, tile), :], w_out_ref.at[c], sems.at[1 + chunks + c]
                ),
            )
        )
        for copy in fetches[-1]:
            copy.start()
    lines_copy.wait()
    fill_store(store, lines_ref, 0, 6, 0)
    from_lines(store, rows_ref, experts, capacity, 0)

    leaving = []
    for c in range(chunks):
        for copy in fetches[c]:
            copy.wait()
        lifted = dot(rows_ref[...], w_in_ref[c])
        if c == 0:
            fill_store(store, lines_ref, 6, 6, 6)
            from_lines(store, grads_ref, experts, capacity, 6)
        grad_active = dot(grads_ref[...], w_out_ref[c], 1, 1)
        gelu, slope = gelu_parts(lifted)
        active_ref[c] = gelu.astype(BF16)
        lifted_ref[c] = (grad_active * slope).astype(BF16)
        early = c < chunks // 2
        at = slice(c % (chunks // 2) * tile, (c % (chunks // 2) + 1) * tile)
        for i, (ref, hbm) in enumerate(
            (
                (active_ref, active_other_hbm if early else active_mine_hbm),
                (lifted_ref, lifted_other_hbm if early else lifted_mine_hbm),
            )
        ):
            copy = pltpu.make_async_copy(
                ref.at[c], hbm.at[:, at], sems.at[1 + (2 + i) * chunks + c]
            )
            copy.start()
            leaving.append(copy)
        moved = dot(lifted_ref[c], w_in_ref[c], 1, 1)
        total[...] = moved if c == 0 else total[...] + moved
        made = dot(active_ref[c], w_out_ref[c])
        if c == chunks - 1:
            to_lines(store, total, experts, capacity, 0)
            spill_store(store, back_ref, 6, 0)
        produced[...] = made if c == 0 else produced[...] + made

    to_lines(store, produced, experts, capacity, 0)
    spill_store(store, back_ref, 6, 6)
    arrived = lines_ref[:, 12 * LANES : 13 * LANES].astype(F32)
    sums = jnp.sum(arrived, axis=0, keepdims=True)
    column = lax.broadcasted_iota(jnp.int32, sums.shape, 1)
    count = jnp.sum(jnp.where(column == 0, 64.0 * sums, sums), axis=1, keepdims=True)
    upper = jnp.floor(count * (1.0 / 256.0))
    pair = jnp.where(column == 0, upper, jnp.where(column == 1, count - 256.0 * upper, 0.0))
    back_ref[:, 12 * LANES : 13 * LANES] = jnp.broadcast_to(
        pair, (back_ref.shape[0], LANES)
    ).astype(BF16)
    for copy in leaving:
        copy.wait()


def expert_gradients_kernel(
    experts,
    capacity,
    steps,
    lines_a,
    lines_b,
    active_a,
    active_b,
    lifted_a,
    lifted_b,
    out_grad_ref,
    in_grad_ref,
    store,
    rows_ref,
    grads_ref,
):
    f = pl.program_id(0)
    own = rows_ref.shape[0] // 2

    @pl.when(f == 0)
    def _():
        for i, lines in enumerate((lines_a, lines_b)):
            fill_store(store, lines, 0, 12, 0)
            here = pl.ds(i * own, own)
            from_lines(store, rows_ref.at[here], experts, capacity, 0)
            from_lines(store, grads_ref.at[here], experts, capacity, 6)

    @pl.when(f < steps)
    def _():
        active = jnp.concatenate([active_a[...], active_b[...]], axis=0)
        out_grad_ref[...] = dot(active, grads_ref[...], 0, 0)

    @pl.when(f >= steps)
    def _():
        lifted = jnp.concatenate([lifted_a[...], lifted_b[...]], axis=0)
        in_grad_ref[...] = dot(rows_ref[...], lifted, 0, 0)


def attention_pair(q, k, v, grad, probs):
    seq_len = q.shape[0]
    low = (lax.broadcasted_iota(jnp.int32, (1, LANES), 1) < 64).astype(F32)
    score_scale = 1.0 / math.sqrt(64)
    low_half = low.astype(BF16)
    high_half = (1.0 - low).astype(BF16)
    grad_both = jnp.concatenate([grad * low_half, grad * high_half], axis=0)
    query_both = jnp.concatenate([q * low_half, q * high_half], axis=0)
    grad_probs = dot(v, grad_both, 1, 1)
    values = dot(probs, grad_both)
    wide = probs.astype(F32)
    inner = jnp.sum(wide * grad_probs, axis=0, keepdims=True)
    grad_scores = (wide * (grad_probs - inner)).astype(BF16)
    keys = dot(grad_scores, query_both) * score_scale
    queries = dot(grad_scores, k, 0, 0) * score_scale
    queries = queries[:seq_len] * low + queries[seq_len:] * (1.0 - low)
    return queries.astype(BF16), keys.astype(BF16), values.astype(BF16)


def hidden_kernel(
    experts,
    capacity,
    at_ref,
    dispatch_ref,
    gain_ref,
    lines_hbm,
    hidden_hbm,
    grad_hbm,
    weight_hbm,
    mixed_hbm,
    probs_hbm,
    grad_hidden_hbm,
    branch_mine_ref,
    branch_other_ref,
    attended_hbm,
    gains_ref,
    out_hbm,
    lines_ref,
    out_ref,
    store,
    came,
    normed,
    branch_ref,
    hidden_ref,
    grad_ref,
    weight_ref,
    mixed_ref,
    probs_ref,
    grad_hidden_ref,
    attended_ref,
    sems,
):
    rows, width = hidden_ref.shape
    seq_count = probs_ref.shape[0]
    seq_len = rows // seq_count
    pairs = probs_ref.shape[1]
    half = width // 2
    core = at_ref[0]
    other = (1 - core) * pairs
    copies = [
        pltpu.make_async_copy(hidden_hbm, hidden_ref, sems.at[0]),
        pltpu.make_async_copy(grad_hbm, grad_ref, sems.at[1]),
        pltpu.make_async_copy(weight_hbm, weight_ref, sems.at[2]),
    ]
    for part in range(3):
        copies.append(
            pltpu.make_async_copy(
                mixed_hbm.at[pl.ds(2 * part * pairs + other, pairs)],
                mixed_ref.at[part],
                sems.at[3 + part],
            )
        )
    for s in range(seq_count):
        copies.append(
            pltpu.make_async_copy(
                probs_hbm.at[s, pl.ds(other, pairs)], probs_ref.at[s], sems.at[6 + s]
            )
        )
    lines_copy = pltpu.make_async_copy(
        lines_hbm.at[:, : lines_ref.shape[1]], lines_ref, sems.at[10]
    )
    lines_copy.start()
    for copy in copies:
        copy.start()
    grad_hidden_copy = pltpu.make_async_copy(grad_hidden_ref, grad_hidden_hbm, sems.at[8])
    attended_copy = pltpu.make_async_copy(attended_ref, attended_hbm, sems.at[9])

    lines_copy.wait()
    fill_store(store, lines_ref, 0, 6, 0)
    from_lines(store, came, experts, capacity, 0)
    gain = as_row(gain_ref)
    normed[...] = dot(dispatch_ref[...], came[...], 0, 0)
    gains_ref[...] = jnp.zeros_like(gains_ref)
    step = 128
    copies[0].wait()
    copies[1].wait()

    def body(i, _):
        at = pl.ds(pl.multiple_of(i * step, step), step)
        scaled, scale = normalize(hidden_ref[at, :])
        grad = normed[at, :]
        grad_hidden = grad_ref[at, :].astype(F32) + norm_backward(scaled, scale, grad * gain)
        grad_hidden_ref[at, :] = grad_hidden
        branch_ref[at, :] = grad_hidden.astype(BF16)
        gains_ref[0:1, :] += jnp.sum(grad * scaled, axis=0, keepdims=True)
        gains_ref[1:2, :] += jnp.sum(grad, axis=0, keepdims=True)
        return 0

    lax.fori_loop(0, rows // step, body, 0, unroll=2)
    grad_hidden_copy.start()
    branch_mine_ref[...] = branch_ref[:, pl.ds(pl.multiple_of(core * half, half), half)]
    branch_other_ref[...] = branch_ref[:, pl.ds(pl.multiple_of((1 - core) * half, half), half)]
    copies[2].wait()
    grad_attended = dot(branch_ref[...], weight_ref[...], 1, 1).astype(BF16)
    for tile in range(2 * pairs):
        attended_ref[tile] = grad_attended[:, tile * LANES : (tile + 1) * LANES]
    attended_copy.start()
    for copy in copies[3:]:
        copy.wait()

    def leaving(p):
        at = pl.ds(pl.multiple_of(p * LANES, LANES), LANES)
        return pltpu.make_async_copy(out_ref.at[p], out_hbm.at[:, :, at], sems.at[11 + p])

    def pair(p, _):
        for s in range(seq_count):
            here = slice(s * seq_len, (s + 1) * seq_len)
            grads = attention_pair(
                mixed_ref[0, p, here, :],
                mixed_ref[1, p, here, :],
                mixed_ref[2, p, here, :],
                attended_ref[other + p, here, :],
                probs_ref[s, p],
            )
            for part in range(3):
                out_ref[p, part, here, :] = grads[part]
        leaving(p).start()
        return 0

    lax.fori_loop(0, pairs, pair, 0, unroll=2)
    for p in range(pairs):
        leaving(p).wait()
    grad_hidden_copy.wait()
    attended_copy.wait()


def input_kernel(
    at_ref,
    mine_ref,
    other_ref,
    gain_ref,
    weight_hbm,
    x_hbm,
    grad_hidden_hbm,
    input_grad_hbm,
    weight_ref,
    x_ref,
    grad_hidden_ref,
    normed,
    sems,
):
    rows, width = x_ref.shape
    half = width // 2
    core = at_ref[0]
    chunks = []
    for part in range(3):
        at = slice(part * width, (part + 1) * width)
        chunks.append(
            pltpu.make_async_copy(weight_hbm.at[:, at], weight_ref.at[:, at], sems.at[part])
        )
    x_copy = pltpu.make_async_copy(x_hbm, x_ref, sems.at[3])
    grad_copy = pltpu.make_async_copy(grad_hidden_hbm, grad_hidden_ref, sems.at[4])
    for copy in (*chunks, x_copy, grad_copy):
        copy.start()
    total = None
    for part in range(3):
        chunks[part].wait()
        for ref, group in ((mine_ref, core), (other_ref, 1 - core)):
            at = pl.multiple_of(part * width + group * half, half)
            term = dot(ref[part], weight_ref[:, pl.ds(at, half)], 1, 1)
            total = term if total is None else total + term
    normed[...] = total
    gain = as_row(gain_ref)
    x_copy.wait()
    grad_copy.wait()
    step = 128
    out_copies = []
    for i in range(rows // step):
        at = slice(i * step, (i + 1) * step)
        scaled, scale = normalize(x_ref[at, :].astype(F32))
        grad_hidden_ref[at, :] += norm_backward(scaled, scale, normed[at, :] * gain)
        out_copies.append(
            pltpu.make_async_copy(grad_hidden_ref.at[at], input_grad_hbm.at[at], sems.at[5 + i])
        )
        out_copies[-1].start()
    for copy in out_copies:
        copy.wait()


def attention_kernel(
    at_ref,
    mixed_hbm,
    attended_hbm,
    probs_hbm,
    out_hbm,
    mixed_ref,
    attended_ref,
    probs_ref,
    out_ref,
    sems,
    out_sems,
):
    seq_count = probs_ref.shape[0]
    pairs, rows, _ = attended_ref.shape
    seq_len = rows // seq_count
    first = at_ref[0] * pairs

    def fetches(p):
        moves = [
            (mixed_hbm.at[2 * part * pairs + first + p], mixed_ref.at[part, p])
            for part in range(3)
        ]
        moves.append((attended_hbm.at[first + p], attended_ref.at[p]))
        for s in range(seq_count):
            moves.append((probs_hbm.at[s, first + p], probs_ref.at[s, p]))
        return [
            pltpu.make_async_copy(hbm, ref, sems.at[i, p]) for i, (hbm, ref) in enumerate(moves)
        ]

    def leaving(p):
        at = pl.ds(pl.multiple_of(p * LANES, LANES), LANES)
        return pltpu.make_async_copy(out_ref.at[p], out_hbm.at[:, :, at], out_sems.at[p])

    for p in range(pairs):
        for copy in fetches(p):
            copy.start()

    def pair(p, _):
        for copy in fetches(p):
            copy.wait()
        for s in range(seq_count):
            here = slice(s * seq_len, (s + 1) * seq_len)
            grads = attention_pair(
                mixed_ref[0, p, here, :],
                mixed_ref[1, p, here, :],
                mixed_ref[2, p, here, :],
                attended_ref[p, here, :],
                probs_ref[s, p],
            )
            for part in range(3):
                out_ref[p, part, here, :] = grads[part]
        leaving(p).start()
        return 0

    lax.fori_loop(0, pairs, pair, 0, unroll=2)
    for p in range(pairs):
        leaving(p).wait()


def weights_kernel(
    at_ref,
    scale_ref,
    ffn_gains_ref,
    mine_hbm,
    came_hbm,
    normed_lines_hbm,
    weight_lines_hbm,
    attended_lines_hbm,
    branch_a_hbm,
    branch_b_hbm,
    send_x_hbm,
    keep_x_hbm,
    send_z_hbm,
    keep_z_hbm,
    send_y_hbm,
    keep_y_hbm,
    right_ref,
    normed_ref,
    weight_ref,
    out_left_ref,
    branch_ref,
    x_ref,
    z_ref,
    y_ref,
    sums,
    sems,
    out_sems,
):
    rows = branch_ref.shape[0] // 2
    half = right_ref.shape[2]
    fetches = [
        (mine_hbm, right_ref.at[:, :rows]),
        (came_hbm, right_ref.at[:, rows:]),
        (normed_lines_hbm, normed_ref),
        (branch_a_hbm, branch_ref.at[:rows]),
        (branch_b_hbm, branch_ref.at[rows:]),
        (attended_lines_hbm, out_left_ref),
        (weight_lines_hbm, weight_ref),
    ]
    fetches = [
        pltpu.make_async_copy(hbm, ref, sems.at[i]) for i, (hbm, ref) in enumerate(fetches)
    ]
    for copy in fetches:
        copy.start()
    leaving = []
    for copy in fetches[:3]:
        copy.wait()
    size = x_ref.shape[1]
    lane = lax.broadcasted_iota(jnp.int32, (size, LANES), 1)
    order = order_matrix(at_ref)
    for turn, step in enumerate((1, 0)):
        lines = slice(step * size, (step + 1) * size)
        blocks = [dot(normed_ref[lines, :], right_ref[part]) for part in range(3)]
        if turn == 0:
            for part in range(3):
                total = jnp.zeros((1, half), F32)
                for at in range(0, 2 * rows, 128):
                    wide = right_ref[part, at : at + 128, :].astype(F32)
                    total = total + jnp.sum(wide, axis=0, keepdims=True)
                sums[part : part + 1, :] = total
            for copy in fetches[3:6]:
                copy.wait()
        out = dot(out_left_ref[lines, :], branch_ref[...]).astype(BF16)
        if turn == 0:
            fetches[6].wait()
        gain = jnp.zeros((size, 1), F32)
        shift = jnp.zeros((size, 1), F32)
        for part in range(3):
            weight = weight_ref[lines, part * half : (part + 1) * half].astype(F32)
            gain = gain + jnp.sum(blocks[part] * weight, axis=1, keepdims=True)
            shift = shift + jnp.sum(sums[part : part + 1, :] * weight, axis=1, keepdims=True)
        parts = [block.astype(BF16) for block in blocks]
        x_ref[step, :, :half] = parts[0]
        x_ref[step, :, half:] = out[:, : half // 2]
        side = out[:, half // 2 : 3 * half // 4]
        for group in range(size // 16):
            x, chip = group // 16, group % 16
            here = slice(group * 16, (group + 1) * 16)
            z_ref[step, chip, x, :, :half] = parts[1][here]
            z_ref[step, chip, x, :, half:] = side[here]
        scale = scale_ref[lines, :]
        gain = (gain - scale[:, 1:2] * shift) / scale[:, 0:1]
        ffn = []
        for i in range(size // 256):
            block_at = at_ref[4 + step * (size // 256) + i]
            ffn.append(
                lax.dot_general(
                    order,
                    ffn_gains_ref[:, pl.ds(pl.multiple_of(block_at * 256, 256), 256)],
                    (((1,), (1,)), ((), ())),
                    precision=lax.Precision.HIGHEST,
                    preferred_element_type=F32,
                )
            )
        ffn = jnp.concatenate(ffn, axis=0)
        small = jnp.where(lane == 0, gain, jnp.where(lane == 1, shift, 0.0))
        small = jnp.where(lane == 2, ffn[:, 0:1], jnp.where(lane == 3, ffn[:, 1:2], small))
        small = small.astype(BF16)
        side = out[:, 3 * half // 4 :]
        for group in range(size // 16):
            x, z, y = group // 16, group // 4 % 4, group % 4
            here = slice(group * 16, (group + 1) * 16)
            y_ref[step, y, x, z, :, :half] = parts[2][here]
            y_ref[step, y, x, z, :, half : half + LANES] = side[here]
            y_ref[step, y, x, z, :, half + LANES :] = small[here]
        x_at = pl.ds(2 * step, 2)
        moves = [
            (x_ref.at[step], send_x_hbm if step == 1 else keep_x_hbm),
            (z_ref.at[step, 8:16], send_z_hbm.at[:, x_at]),
            (z_ref.at[step, 0:8], keep_z_hbm.at[:, x_at]),
            (y_ref.at[step, 2:4], send_y_hbm.at[:, x_at]),
            (y_ref.at[step, 0:2], keep_y_hbm.at[:, x_at]),
        ]
        for i, (ref, hbm) in enumerate(moves):
            copy = pltpu.make_async_copy(ref, hbm, out_sems.at[turn * 5 + i])
            copy.start()
            leaving.append(copy)
    for copy in leaving:
        copy.wait()


def second_kernel(kept_ref, first_ref, send_ref):
    send_ref[...] = (kept_ref[...].astype(F32) + first_ref[...].astype(F32)).astype(BF16)


def third_kernel(kept_ref, first_ref, second_ref, send_ref):
    total = kept_ref[...].astype(F32) + first_ref[...].astype(F32) + second_ref[...].astype(F32)
    send_ref[...] = total.astype(BF16)


def merge_kernel(*refs):
    parts = [refs[4 * i : 4 * i + 4] for i in range(3)]
    send_ref, keep_ref = refs[12:]
    for x in range(2):
        for z in range(2):
            for y in range(2):
                at = 0
                for part, spot in zip(parts, ((x, z, y), (z, y, x), (y, x, z))):
                    total = part[0][spot].astype(F32)
                    for ref in part[1:]:
                        total = total + ref[spot].astype(F32)
                    span = total.shape[1]
                    if x == 1:
                        send_ref[z, y, :, at : at + span] = total.astype(BF16)
                    else:
                        keep_ref[z, y, :, at : at + span] = total
                    at += span


def split_kernel(at_ref, kept_ref, came_ref, mine_ref, other_ref, store):
    store[...] = kept_ref[...] + came_ref[...].astype(F32)
    core = at_ref[0]
    mine_ref[...] = store[pl.ds(pl.multiple_of(core * 8, 8), 8), :]
    other_ref[...] = store[pl.ds(pl.multiple_of((1 - core) * 8, 8), 8), :]


def join_kernel(spans, at_ref, mine_ref, other_ref, qkv_ref, out_ref, small_ref):
    half = out_ref.shape[1] // 2
    core = at_ref[0]
    for ref, group in ((mine_ref, core), (other_ref, 1 - core)):
        group_at = group * half
        at, out_at = 0, 0
        for part, span in enumerate(spans):
            spot = pl.multiple_of(2 * part * half + group_at, half)
            qkv_ref[:, pl.ds(spot, half)] = ref[:, at : at + half]
            side = span - half
            spot = pl.multiple_of(group_at + out_at, LANES)
            out_ref[:, pl.ds(spot, side)] = ref[:, at + half : at + span]
            at += span
            out_at += side
    small_ref[...] = mine_ref[:, at : at + LANES] + other_ref[:, at : at + LANES]


def output_kernel(experts, capacity, lines_ref, dispatch_ref, hidden_ref, out_ref, store, came):
    fill_store(store, lines_ref, 0, 6, 6)
    from_lines(store, came, experts, capacity, 0)
    back = dot(dispatch_ref[...], came[...], 0, 0)
    out_ref[...] = (hidden_ref[...] + back).astype(BF16)


def whole(shape):
    return pl.BlockSpec(shape, lambda *_: (0,) * len(shape))


def shaped(shape, dtype):
    return jax.ShapeDtypeStruct(shape, dtype)


def per_device(
    block_input,
    attn_gain,
    attn_shift,
    query_key_value_weight,
    output_weight,
    ffn_gain,
    ffn_shift,
    expert_in,
    expert_out,
    hash_ids,
    seq_lengths,
    prev_counts,
    out_grad,
):
    seq_count, seq_len, width = block_input.shape
    rows = seq_count * seq_len
    chips = lax.axis_size(WIDE)
    experts = chips
    capacity = max(2, 3 * rows // (4 * experts))
    n_slots = experts * capacity
    ff_width = expert_in.shape[2]
    half_ff = ff_width // 2
    half = width // 2
    pairs = HEADS // 2
    lines = 8 * chips
    core = lax.axis_index("narrow").astype(jnp.int32)
    core_at = core.reshape(1)
    other_at = (1 - core).reshape(1)
    x = block_input.reshape(rows, width)
    grad_rows = out_grad.reshape(rows, width)
    w_in = expert_in[0]
    w_out = expert_out[0]
    scales = [v.reshape(8, LANES) for v in (attn_gain, attn_shift, ffn_gain, ffn_shift)]
    smem = pl.BlockSpec(memory_space=pltpu.SMEM)
    vmem = pl.BlockSpec(memory_space=pltpu.VMEM)
    hbm = pl.BlockSpec(memory_space=pl.ANY)
    coordinates = [lax.axis_index(name).astype(jnp.int32) for name in WIDE]
    blocks_x = [places(place, core) ^ coordinates[0] for place in range(4)]
    spot = jnp.stack([core] + coordinates + blocks_x).astype(jnp.int32)

    normed, mixed, probs, attended, hidden, dispatch, send = pl.pallas_call(
        functools.partial(forward_kernel, experts, capacity),
        out_shape=(
            shaped((rows, width), BF16),
            shaped((3 * pairs, rows, LANES), BF16),
            shaped((seq_count, pairs, seq_len, 2 * seq_len), BF16),
            shaped((rows, width), BF16),
            shaped((rows, width), F32),
            shaped((n_slots, rows), BF16),
            shaped((lines, 13 * LANES), BF16),
        ),
        in_specs=[smem] + [vmem] * 6 + [hbm] * 3,
        out_specs=[hbm] * 5 + [vmem] * 2,
        scratch_shapes=[
            pltpu.VMEM((width, 3 * width), BF16),
            pltpu.VMEM((width, width), BF16),
            pltpu.VMEM((rows, width), BF16),
            pltpu.VMEM((rows, width), BF16),
            pltpu.VMEM((3 * pairs, rows, LANES), BF16),
            pltpu.VMEM((seq_count, pairs, seq_len, 2 * seq_len), BF16),
            pltpu.VMEM((rows, width), BF16),
            pltpu.VMEM((rows, width), F32),
            pltpu.VMEM((rows, width), BF16),
            pltpu.VMEM((seq_count, seq_len, 2 * seq_len), F32),
            pltpu.VMEM((13, lines, LANES), F32),
            pltpu.SemaphoreType.DMA((10,)),
        ],
        compiler_params=params(60),
        name="forward",
        cost_estimate=cost(10, 20),
    )(
        seq_lengths,
        hash_ids,
        x,
        *scales,
        query_key_value_weight,
        output_weight,
        grad_rows,
    )
    arrived = exchanged(send)
    normed_other = swapped(normed)
    attended_other = swapped(attended)
    block = width // 4
    column = pl.BlockSpec((rows, block), lambda i, at: (0, at[4 + i]))
    weight_part = [
        pl.BlockSpec((block, half), lambda i, at, part=part: (at[4 + i], 2 * part + at[0]))
        for part in range(3)
    ]
    normed_lines, attended_lines, weight_lines, scale_lines = pl.pallas_call(
        prepare_kernel,
        out_shape=(
            shaped((width, 2 * rows), BF16),
            shaped((width, 2 * rows), BF16),
            shaped((width, 3 * half), BF16),
            shaped((width, LANES), F32),
        ),
        grid_spec=pltpu.PrefetchScalarGridSpec(
            num_scalar_prefetch=1,
            grid=(4,),
            in_specs=[column] * 4 + weight_part + [whole((8, LANES))] * 2,
            out_specs=[
                pl.BlockSpec((block, 2 * rows), lambda i, at: (i, 0)),
                pl.BlockSpec((block, 2 * rows), lambda i, at: (i, 0)),
                pl.BlockSpec((block, 3 * half), lambda i, at: (i, 0)),
                pl.BlockSpec((block, LANES), lambda i, at: (i, 0)),
            ],
        ),
        compiler_params=params(60),
        name="prepare",
        cost_estimate=cost(4, 8),
    )(
        spot,
        normed,
        normed_other,
        attended,
        attended_other,
        query_key_value_weight,
        query_key_value_weight,
        query_key_value_weight,
        *scales[:2],
    )
    arrived, normed_lines = lax.optimization_barrier((arrived, normed_lines))

    chunks = 4
    tile = ff_width // chunks
    half_block = shaped((n_slots, half_ff), BF16)
    active_other, active_mine, lifted_other, lifted_mine, back = pl.pallas_call(
        functools.partial(expert_kernel, experts, capacity),
        out_shape=(
            half_block,
            half_block,
            half_block,
            half_block,
            shaped((lines, 13 * LANES), BF16),
        ),
        in_specs=[smem] + [hbm] * 3,
        out_specs=[hbm] * 4 + [vmem],
        scratch_shapes=[
            pltpu.VMEM((lines, 13 * LANES), BF16),
            pltpu.VMEM((chunks, width, tile), BF16),
            pltpu.VMEM((chunks, tile, width), BF16),
            pltpu.VMEM((n_slots, width), BF16),
            pltpu.VMEM((n_slots, width), BF16),
            pltpu.VMEM((chunks, n_slots, tile), BF16),
            pltpu.VMEM((chunks, n_slots, tile), BF16),
            pltpu.VMEM((12, lines, LANES), F32),
            pltpu.VMEM((n_slots, width), F32),
            pltpu.VMEM((n_slots, width), F32),
            pltpu.SemaphoreType.DMA((1 + 4 * chunks,)),
        ],
        compiler_params=params(60),
        name="expert",
        cost_estimate=cost(16, 25),
    )(spot, arrived, w_in, w_out)
    returned = exchanged(back)

    arrived_other = swapped(arrived)
    active_came = swapped(active_other)
    lifted_came = swapped(lifted_other)
    steps = 4
    tile = half_ff // steps
    early = pl.BlockSpec((n_slots, tile), lambda f: (0, jnp.minimum(f, steps - 1)))
    late = pl.BlockSpec((n_slots, tile), lambda f: (0, jnp.maximum(f - steps, 0)))
    expert_out_grad, expert_in_grad = pl.pallas_call(
        functools.partial(expert_gradients_kernel, experts, capacity, steps),
        out_shape=(shaped((half_ff, width), F32), shaped((width, half_ff), F32)),
        grid=(2 * steps,),
        in_specs=[whole((lines, 13 * LANES))] * 2 + [early] * 2 + [late] * 2,
        out_specs=[
            pl.BlockSpec((tile, width), lambda f: (jnp.minimum(f, steps - 1), 0)),
            pl.BlockSpec((width, tile), lambda f: (0, jnp.maximum(f - steps, 0))),
        ],
        scratch_shapes=[
            pltpu.VMEM((12, lines, LANES), F32),
            pltpu.VMEM((2 * n_slots, width), BF16),
            pltpu.VMEM((2 * n_slots, width), BF16),
        ],
        compiler_params=params(60),
        name="expert_gradients",
        cost_estimate=cost(10, 30),
    )(arrived, arrived_other, active_mine, active_came, lifted_mine, lifted_came)
    returned, expert_out_grad, expert_in_grad = lax.optimization_barrier(
        (returned, expert_out_grad, expert_in_grad)
    )

    half_pairs = pairs // 2
    grad_hidden, branch, branch_out, grad_attended, ffn_gains, mixed_out = pl.pallas_call(
        functools.partial(hidden_kernel, experts, capacity),
        out_shape=(
            shaped((rows, width), F32),
            shaped((rows, half), BF16),
            shaped((rows, half), BF16),
            shaped((pairs, rows, LANES), BF16),
            shaped((8, width), F32),
            shaped((3, rows, half), BF16),
        ),
        in_specs=[smem, vmem, vmem] + [hbm] * 6,
        out_specs=[hbm, vmem, vmem, hbm, vmem, hbm],
        scratch_shapes=[
            pltpu.VMEM((lines, 6 * LANES), BF16),
            pltpu.VMEM((half_pairs, 3, rows, LANES), BF16),
            pltpu.VMEM((6, lines, LANES), F32),
            pltpu.VMEM((n_slots, width), BF16),
            pltpu.VMEM((rows, width), F32),
            pltpu.VMEM((rows, width), BF16),
            pltpu.VMEM((rows, width), F32),
            pltpu.VMEM((rows, width), BF16),
            pltpu.VMEM((width, width), BF16),
            pltpu.VMEM((3, half_pairs, rows, LANES), BF16),
            pltpu.VMEM((seq_count, half_pairs, seq_len, 2 * seq_len), BF16),
            pltpu.VMEM((rows, width), F32),
            pltpu.VMEM((pairs, rows, LANES), BF16),
            pltpu.SemaphoreType.DMA((11 + half_pairs,)),
        ],
        compiler_params=params(60),
        name="hidden_backward",
        cost_estimate=cost(6, 14),
    )(spot, dispatch, scales[2], returned, hidden, grad_rows, output_weight, mixed, probs)
    mixed_came = swapped(mixed_out)
    branch_other = swapped(branch_out)

    spans = (half + half // 2, half + half // 4, half + half // 2)
    shapes = ((512,), (8, 4, 16), (2, 4, 4, 16))
    mixed_mine = pl.pallas_call(
        attention_kernel,
        out_shape=shaped((3, rows, half), BF16),
        in_specs=[smem] + [hbm] * 3,
        out_specs=hbm,
        scratch_shapes=[
            pltpu.VMEM((3, half_pairs, rows, LANES), BF16),
            pltpu.VMEM((half_pairs, rows, LANES), BF16),
            pltpu.VMEM((seq_count, half_pairs, seq_len, 2 * seq_len), BF16),
            pltpu.VMEM((half_pairs, 3, rows, LANES), BF16),
            pltpu.SemaphoreType.DMA((6, half_pairs)),
            pltpu.SemaphoreType.DMA((half_pairs,)),
        ],
        compiler_params=params(60),
        name="attention_backward",
        cost_estimate=cost(4, 5),
    )(spot, mixed, grad_attended, probs)
    halves = pl.pallas_call(
        weights_kernel,
        out_shape=[
            shaped(shape + (span,), BF16) for shape, span in zip(shapes, spans) for _ in range(2)
        ],
        in_specs=[smem, vmem, vmem] + [hbm] * 7,
        out_specs=[hbm] * 6,
        scratch_shapes=[
            pltpu.VMEM((3, 2 * rows, half), BF16),
            pltpu.VMEM((width, 2 * rows), BF16),
            pltpu.VMEM((width, 3 * half), BF16),
            pltpu.VMEM((width, 2 * rows), BF16),
            pltpu.VMEM((2 * rows, half), BF16),
            pltpu.VMEM((2, 512, spans[0]), BF16),
            pltpu.VMEM((2, 16, 2, 16, spans[1]), BF16),
            pltpu.VMEM((2, 4, 2, 4, 16, spans[2]), BF16),
            pltpu.VMEM((8, half), F32),
            pltpu.SemaphoreType.DMA((7,)),
            pltpu.SemaphoreType.DMA((10,)),
        ],
        compiler_params=params(60),
        name="weight_gradients",
        cost_estimate=cost(8, 20),
    )(
        spot,
        scale_lines,
        ffn_gains,
        mixed_mine,
        mixed_came,
        normed_lines,
        weight_lines,
        attended_lines,
        branch,
        branch_other,
    )

    input_grad = pl.pallas_call(
        input_kernel,
        out_shape=shaped((rows, width), F32),
        in_specs=[smem, vmem, vmem, vmem, hbm, hbm, hbm],
        out_specs=hbm,
        scratch_shapes=[
            pltpu.VMEM((width, 3 * width), BF16),
            pltpu.VMEM((rows, width), BF16),
            pltpu.VMEM((rows, width), F32),
            pltpu.VMEM((rows, width), F32),
            pltpu.SemaphoreType.DMA((9,)),
        ],
        compiler_params=params(60),
        name="input_backward",
        cost_estimate=cost(6, 14),
    )(spot, mixed_mine, mixed_out, scales[0], query_key_value_weight, x, grad_hidden)

    block_output = pl.pallas_call(
        functools.partial(output_kernel, experts, capacity),
        out_shape=shaped((rows, width), BF16),
        grid=(1,),
        in_specs=[
            whole((lines, 13 * LANES)),
            whole((n_slots, rows)),
            whole((rows, width)),
        ],
        out_specs=whole((rows, width)),
        scratch_shapes=[
            pltpu.VMEM((6, lines, LANES), F32),
            pltpu.VMEM((n_slots, width), BF16),
        ],
        compiler_params=params(60),
        name="block_output",
        cost_estimate=cost(1, 5),
    )(returned, dispatch, hidden)

    orders = ((0, 1, 2), (1, 2, 0), (2, 0, 1))
    sent = [part.reshape(2, 4, 4, 16, -1) for part in halves[0::2]]
    kept = [part.reshape(2, 4, 4, 16, -1) for part in halves[1::2]]
    first = [crossed(part, order[0], True) for part, order in zip(sent, orders)]
    first, input_grad = lax.optimization_barrier((first, input_grad))

    def cut(span, shape, at):
        return pl.BlockSpec(shape + (16, span), lambda *_: at + (0, 0))

    def added(kernel, arrays, shape, spots, name):
        span = arrays[0].shape[-1]
        return pl.pallas_call(
            kernel,
            out_shape=shaped(shape + (16, span), BF16),
            grid=(1,),
            in_specs=[cut(span, shape, at) for at in spots],
            out_specs=whole(shape + (16, span)),
            compiler_params=params(16),
            name=name,
            cost_estimate=cost(0.01, 2),
        )(*arrays)

    second = []
    for k, c, order in zip(kept, first, orders):
        send = added(second_kernel, (k, c), (2, 2, 4), ((0, 1, 0),) * 2, "second")
        second.append(crossed(send, order[1], True))
    third = []
    for k, c, d, order in zip(kept, first, second, orders):
        spots = ((0, 0, 1),) * 3
        send = added(third_kernel, (k, c, d), (2, 2, 2), spots, "third")
        third.append(crossed(send, order[2], True))
    total_span = sum(spans)
    send, keep = pl.pallas_call(
        merge_kernel,
        out_shape=(
            shaped((2, 2, 16, total_span), BF16),
            shaped((2, 2, 16, total_span), F32),
        ),
        grid=(1,),
        in_specs=[cut(span, (2, 2, 2), (0, 0, 0)) for span in spans for _ in range(4)],
        out_specs=[whole((2, 2, 16, total_span))] * 2,
        compiler_params=params(16),
        name="merge",
        cost_estimate=cost(0.01, 4),
    )(*(array for group in zip(kept, first, second, third) for array in group))
    came = crossed(send, 0, False)
    for axis in (1, 2):
        keep = keep + came.astype(F32)
        came = crossed(keep[1].astype(BF16), axis, False)
        keep = keep[0]
    own, other = pl.pallas_call(
        split_kernel,
        out_shape=(shaped((8, total_span), F32), shaped((8, total_span), F32)),
        in_specs=[smem, vmem, vmem],
        out_specs=[vmem, vmem],
        scratch_shapes=[pltpu.VMEM((16, total_span), F32)],
        compiler_params=params(16),
        name="split",
    )(spot, keep, came)
    qkv_grad, out_weight_grad, vectors = pl.pallas_call(
        functools.partial(join_kernel, (*spans[:2], half + half // 4)),
        out_shape=(
            shaped((8, 3 * width), F32),
            shaped((8, width), F32),
            shaped((8, LANES), F32),
        ),
        in_specs=[smem, vmem, vmem],
        out_specs=[vmem] * 3,
        compiler_params=params(16),
        name="join",
    )(spot, own, swapped(other))

    pair = returned[:, 12 * LANES : 12 * LANES + 2].reshape(chips, 8, 2)[:, 0].astype(F32)
    counts = 256.0 * pair[:, 0] + pair[:, 1]
    counts = counts + swapped(counts)
    total_tokens = float(rows * chips * 2)
    new_average = (momentum * prev_counts.astype(F32) + (1.0 - momentum) * counts) * (
        float(experts) / total_tokens
    )
    return (
        block_output.reshape(seq_count, seq_len, width),
        input_grad.reshape(seq_count, seq_len, width),
        vectors[:, 0],
        vectors[:, 1],
        qkv_grad,
        out_weight_grad,
        vectors[:, 2],
        vectors[:, 3],
        expert_in_grad[None],
        expert_out_grad[None],
        new_average,
    )


def solution(mesh):
    finer = Mesh(
        mesh.devices.reshape(4, 4, 4, mesh.shape["narrow"]),
        ("wide_0", "wide_1", "wide_2", "narrow"),
    )
    placed = (
        P(WIDE_NARROW, None, None),
        P(),
        P(),
        P(),
        P(),
        P(),
        P(),
        P(WIDE, None, None),
        P(WIDE, None, None),
        P(WIDE_NARROW, None),
        P(WIDE_NARROW),
        P(),
        P(WIDE_NARROW, None, None),
    )
    return jax.shard_map(
        per_device,
        mesh=finer,
        in_specs=placed,
        out_specs=(
            P(WIDE_NARROW, None, None),
            P(WIDE_NARROW, None, None),
            P(WIDE_NARROW),
            P(WIDE_NARROW),
            P(WIDE_NARROW, None),
            P(WIDE_NARROW, None),
            P(WIDE_NARROW),
            P(WIDE_NARROW),
            P(WIDE, None, "narrow"),
            P(WIDE, "narrow", None),
            P(),
        ),
        check_vma=False,
    )
```

```python
import functools
import math

import jax
import jax.experimental.pallas as pl
import jax.experimental.pallas.tpu as pltpu
import jax.numpy as jnp
from jax import lax
from jax.sharding import Mesh
from jax.sharding import PartitionSpec as P

HEADS = 16
WIDE = ("wide_0", "wide_1", "wide_2")
WIDE_NARROW = ("wide_0", "wide_1", "wide_2", "narrow")

norm_eps = 1e-05
momentum = 0.9
F32 = jnp.float32
BF16 = jnp.bfloat16
LANES = 128
MIB = 1 << 20


def swapped(shard):
    return lax.ppermute(shard, "narrow", [(0, 1), (1, 0)])


def exchanged(lines):
    shard = lines.reshape(lax.axis_size(WIDE), -1, lines.shape[1])
    return lax.all_to_all(shard, WIDE, 0, 0, tiled=True).reshape(lines.shape)


def crossed(shard, axis, first):
    pairs = []
    for i in range(lax.axis_size(WIDE[axis])):
        for core in range(2):
            flip = 1 if first == (core == 0) else 3
            pairs.append((i * 2 + core, (i ^ flip) * 2 + core))
    return lax.ppermute(shard, (WIDE[axis], "narrow"), pairs)


def dot(left, right, left_dim=1, right_dim=0):
    return lax.dot_general(
        left, right, (((left_dim,), (right_dim,)), ((), ())), preferred_element_type=F32
    )


def params(mib):
    return pltpu.CompilerParams(vmem_limit_bytes=mib * MIB)


def cost(gigaflops, megabytes):
    return pl.CostEstimate(
        flops=int(gigaflops * 1e9), bytes_accessed=int(megabytes * 1e6), transcendentals=0
    )


def normalize(features):
    centered = features - jnp.mean(features, axis=-1, keepdims=True)
    spread = jnp.mean(centered * centered, axis=-1, keepdims=True)
    scale = lax.rsqrt(spread + norm_eps)
    return centered * scale, scale


def as_row(tile_ref):
    tile = tile_ref[...].astype(F32)
    return jnp.concatenate([tile[i : i + 1, :] for i in range(tile.shape[0])], axis=1)


def norm_backward(scaled, scale, gained):
    mean = jnp.mean(gained, axis=-1, keepdims=True)
    along = jnp.mean(gained * scaled, axis=-1, keepdims=True)
    return scale * (gained - mean - scaled * along)


def to_lines(store, rows, experts, capacity, lane_tile):
    for rank in range(capacity):
        for part in range(8):
            store[lane_tile + rank, pl.ds(part, experts, stride=8), :] = rows[
                rank * experts : (rank + 1) * experts, part * LANES : (part + 1) * LANES
            ]


def from_lines(store, rows_ref, experts, capacity, lane_tile):
    for rank in range(capacity):
        for part in range(8):
            rows_ref[
                rank * experts : (rank + 1) * experts, part * LANES : (part + 1) * LANES
            ] = store[lane_tile + rank, pl.ds(part, experts, stride=8), :].astype(BF16)


def fill_store(store, lines_ref, lane_tile, count, source_tile):
    for tile in range(count):
        at = (source_tile + tile) * LANES
        store[lane_tile + tile] = lines_ref[:, at : at + LANES].astype(F32)


def spill_store(store, lines_ref, count, target_tile):
    for tile in range(count):
        at = (target_tile + tile) * LANES
        lines_ref[:, at : at + LANES] = store[tile].astype(BF16)


def unpack(store, lines_ref, rows_ref, experts, count, source_tile):
    def body(rank, _):
        at = pl.ds(pl.multiple_of((source_tile + rank) * LANES, LANES), LANES)
        store[...] = lines_ref[:, at].astype(F32)
        here = pl.ds(pl.multiple_of(rank * experts, experts), experts)
        for part in range(8):
            rows_ref[here, part * LANES : (part + 1) * LANES] = store[
                pl.ds(part, experts, stride=8), :
            ].astype(BF16)
        return 0

    lax.fori_loop(0, count, body, 0)


def forward_kernel(
    experts,
    capacity,
    len_ref,
    ids_ref,
    x_ref,
    gain_one_ref,
    shift_one_ref,
    gain_two_ref,
    shift_two_ref,
    qkv_weight_hbm,
    out_weight_hbm,
    grad_hbm,
    normed_hbm,
    mixed_hbm,
    probs_hbm,
    attended_hbm,
    hidden_hbm,
    dispatch_ref,
    send_ref,
    qkv_weight_ref,
    out_weight_ref,
    grad_ref,
    normed_ref,
    mixed_ref,
    probs_ref,
    attended_ref,
    hidden_ref,
    moved_ref,
    barred,
    store,
    sems,
):
    rows, width = x_ref.shape
    seq_count, seq_len = ids_ref.shape
    pieces = 3
    span = 3 * width // pieces

    def fetch(i):
        at = slice(i * span, (i + 1) * span)
        return pltpu.make_async_copy(qkv_weight_hbm.at[:, at], qkv_weight_ref.at[:, at], sems.at[i])

    out_weight_copy = pltpu.make_async_copy(out_weight_hbm, out_weight_ref, sems.at[3])
    grad_copy = pltpu.make_async_copy(grad_hbm, grad_ref, sems.at[4])
    for i in range(pieces):
        fetch(i).start()
    out_weight_copy.start()
    grad_copy.start()
    normed_copy = pltpu.make_async_copy(normed_ref, normed_hbm, sems.at[5])
    mixed_copy = pltpu.make_async_copy(mixed_ref, mixed_hbm, sems.at[6])
    probs_copy = pltpu.make_async_copy(probs_ref, probs_hbm, sems.at[7])
    attended_copy = pltpu.make_async_copy(attended_ref, attended_hbm, sems.at[8])
    hidden_copy = pltpu.make_async_copy(hidden_ref, hidden_hbm, sems.at[9])

    gain_one, shift_one = as_row(gain_one_ref), as_row(shift_one_ref)
    gain_two, shift_two = as_row(gain_two_ref), as_row(shift_two_ref)
    step = 128

    def norm_one(i, _):
        at = pl.ds(pl.multiple_of(i * step, step), step)
        scaled, _ = normalize(x_ref[at, :].astype(F32))
        normed_ref[at, :] = (scaled * gain_one + shift_one).astype(BF16)
        return 0

    lax.fori_loop(0, rows // step, norm_one, 0)
    normed_copy.start()

    ids = jnp.concatenate([ids_ref[s : s + 1, :] for s in range(seq_count)], axis=1)
    lane = lax.broadcasted_iota(jnp.int32, (1, rows), 1)
    length = jnp.where(lane < seq_len, len_ref[0], len_ref[1])
    is_valid = lane % seq_len < length
    member = (lax.broadcasted_iota(jnp.int32, (experts, rows), 0) == ids) & is_valid
    onehot = member.astype(F32)
    earlier = (
        lax.broadcasted_iota(jnp.int32, (rows, rows), 0)
        < lax.broadcasted_iota(jnp.int32, (rows, rows), 1)
    ).astype(F32)
    before = dot(onehot.astype(BF16), earlier.astype(BF16))
    rank = jnp.sum(onehot * before, axis=0, keepdims=True).astype(jnp.int32)
    slot = jnp.where(is_valid & (rank < capacity), rank * experts + ids, -1)
    at_slot = lax.broadcasted_iota(jnp.int32, (experts * capacity, rows), 0)
    dispatch_ref[...] = (at_slot == slot).astype(F32).astype(BF16)
    counts = jnp.sum(onehot, axis=1, keepdims=True)
    upper = jnp.floor(counts * (1.0 / 64.0))
    column = lax.broadcasted_iota(jnp.int32, (experts, LANES), 1)
    store[12] = jnp.zeros(store.shape[1:], F32)
    store[12, pl.ds(0, experts, stride=8), :] = jnp.where(
        column == 0, upper, jnp.where(column == 1, counts - 64.0 * upper, 0.0)
    )

    for i in range(pieces):
        fetch(i).wait()

        def project(j, _):
            at = pl.ds(pl.multiple_of(i * span + j * 512, 512), 512)
            block = dot(normed_ref[...], qkv_weight_ref[:, at]).astype(BF16)
            for tile in range(4):
                mixed_ref[(i * span + j * 512) // LANES + tile] = block[
                    :, tile * LANES : (tile + 1) * LANES
                ]
            return 0

        lax.fori_loop(0, span // 512, project, 0)
    mixed_copy.start()

    pairs = HEADS // 2
    low = (lax.broadcasted_iota(jnp.int32, (1, LANES), 1) < 64).astype(F32)
    score_scale = 1.0 / math.sqrt(width // HEADS)
    low_scaled = (low * score_scale).astype(BF16)
    high_scaled = ((1.0 - low) * score_scale).astype(BF16)
    query_at = lax.broadcasted_iota(jnp.int32, (seq_len, 2 * seq_len), 1) % seq_len
    key_at = lax.broadcasted_iota(jnp.int32, (seq_len, 2 * seq_len), 0)
    for s in range(seq_count):
        allowed = (key_at <= query_at) & (key_at < len_ref[s])
        barred[s] = jnp.where(allowed, 0.0, -3e38)

    def attend(p, _):
        at = pl.multiple_of(p * LANES, LANES)
        for s in range(seq_count):
            here = slice(s * seq_len, (s + 1) * seq_len)
            q = mixed_ref[p, here, :]
            k = mixed_ref[pairs + p, here, :]
            v = mixed_ref[2 * pairs + p, here, :]
            both = jnp.concatenate([q * low_scaled, q * high_scaled], axis=0)
            scores = dot(k, both, 1, 1) + barred[s]
            raised = jnp.exp(scores - jnp.max(scores, axis=0, keepdims=True))
            total = jnp.sum(raised, axis=0, keepdims=True)
            probs = (raised * (1.0 / total)).astype(BF16)
            probs_ref[s, p] = probs
            out = dot(probs, v, 0, 0)
            out = out[:seq_len] * low + out[seq_len:] * (1.0 - low)
            attended_ref[here, pl.ds(at, LANES)] = out.astype(BF16)
        return 0

    lax.fori_loop(0, pairs, attend, 0, unroll=2)
    probs_copy.start()
    attended_copy.start()

    out_weight_copy.wait()

    def norm_two(i, _):
        at = pl.ds(pl.multiple_of(i * 256, 256), 256)
        hidden = x_ref[at, :].astype(F32) + dot(attended_ref[at, :], out_weight_ref[...])
        hidden_ref[at, :] = hidden
        scaled, _ = normalize(hidden)
        moved_ref[at, :] = (scaled * gain_two + shift_two).astype(BF16)
        return 0

    lax.fori_loop(0, rows // 256, norm_two, 0)
    hidden_copy.start()

    grad_copy.wait()
    to_lines(store, dot(dispatch_ref[...], grad_ref[...]), experts, capacity, 6)
    to_lines(store, dot(dispatch_ref[...], moved_ref[...]), experts, capacity, 0)
    spill_store(store, send_ref, 13, 0)
    for copy in (normed_copy, mixed_copy, probs_copy, attended_copy, hidden_copy):
        copy.wait()


def places(position, core):
    near = 1 + 2 * core
    return jnp.where(
        position == 0,
        0,
        jnp.where(position == 1, 4 - near, jnp.where(position == 2, near, 2)),
    )


def order_matrix(at_ref):
    line = lax.broadcasted_iota(jnp.int32, (256, 256), 0)
    column = lax.broadcasted_iota(jnp.int32, (256, 256), 1)
    core, z, y = at_ref[0], at_ref[2], at_ref[3]
    source_z = places(line // 64, core) ^ z
    source_y = places(line // 16 % 4, core) ^ y
    return (column == source_z * 64 + source_y * 16 + line % 16).astype(F32)


def prepare_kernel(
    at_ref,
    normed_a,
    normed_b,
    attended_a,
    attended_b,
    query_ref,
    key_ref,
    value_ref,
    gain_ref,
    shift_ref,
    normed_ref,
    attended_ref,
    weight_ref,
    scale_ref,
):
    order = order_matrix(at_ref).astype(BF16)
    rows = normed_a.shape[0]
    normed_ref[:, :rows] = dot(order, normed_a[...], 1, 1).astype(BF16)
    normed_ref[:, rows:] = dot(order, normed_b[...], 1, 1).astype(BF16)
    attended_ref[:, :rows] = dot(order, attended_a[...], 1, 1).astype(BF16)
    attended_ref[:, rows:] = dot(order, attended_b[...], 1, 1).astype(BF16)
    half = query_ref.shape[1]
    for part, ref in enumerate((query_ref, key_ref, value_ref)):
        weight_ref[:, part * half : (part + 1) * half] = dot(order, ref[...]).astype(BF16)
    tile_at = 2 * at_ref[4 + pl.program_id(0)]
    tile = lax.broadcasted_iota(jnp.int32, (8, LANES), 0)
    line = lax.broadcasted_iota(jnp.int32, (LANES, 256), 0)

    def columns(ref):
        wide = ref[...].astype(F32)
        parts = [
            jnp.sum(jnp.where(tile == tile_at + i, wide, 0.0), axis=0, keepdims=True)
            for i in range(2)
        ]
        return jnp.concatenate(parts, axis=1)

    both = jnp.where(line == 0, columns(gain_ref), jnp.where(line == 1, columns(shift_ref), 0.0))
    scale_ref[...] = dot(order, both.astype(BF16), 1, 1)


def gelu_parts(u):
    inner = 0.7978845608028654 * (u + 0.044715 * (u * u * u))
    t = jnp.tanh(inner)
    half = 0.5 * (1.0 + t)
    slope = half + 0.5 * u * (1.0 - t * t) * (0.7978845608028654 * (1.0 + 0.134145 * (u * u)))
    return u * half, slope


def expert_kernel(
    experts,
    capacity,
    core_ref,
    lines_hbm,
    w_in_hbm,
    w_out_hbm,
    active_other_hbm,
    active_mine_hbm,
    lifted_other_hbm,
    lifted_mine_hbm,
    back_ref,
    lines_ref,
    w_in_ref,
    w_out_ref,
    rows_ref,
    grads_ref,
    active_ref,
    lifted_ref,
    store,
    total,
    produced,
    sems,
    weight_sems,
    out_sems,
):
    chunks, _, tile = w_in_ref.shape
    core = core_ref[0]
    early = chunks // 2
    lines_copy = pltpu.make_async_copy(lines_hbm, lines_ref, sems.at[0])
    lines_copy.start()

    def fetches(c):
        group = jnp.where(c < early, 1 - core, core)
        at = pl.multiple_of((group * early + c % early) * tile, tile)
        return (
            pltpu.make_async_copy(
                w_in_hbm.at[:, pl.ds(at, tile)], w_in_ref.at[c], weight_sems.at[0, c]
            ),
            pltpu.make_async_copy(
                w_out_hbm.at[pl.ds(at, tile), :], w_out_ref.at[c], weight_sems.at[1, c]
            ),
        )

    def leaving(c, is_early):
        at = pl.ds(pl.multiple_of(c % early * tile, tile), tile)
        active_hbm = active_other_hbm if is_early else active_mine_hbm
        lifted_hbm = lifted_other_hbm if is_early else lifted_mine_hbm
        return (
            pltpu.make_async_copy(active_ref.at[c], active_hbm.at[:, at], out_sems.at[0, c]),
            pltpu.make_async_copy(lifted_ref.at[c], lifted_hbm.at[:, at], out_sems.at[1, c]),
        )

    for c in range(chunks):
        for copy in fetches(c):
            copy.start()
    lines_copy.wait()
    unpack(store.at[0], lines_ref, rows_ref, experts, capacity, 0)

    def chunk(c, first=False, last=False):
        for copy in fetches(c):
            copy.wait()
        lifted = dot(rows_ref[...], w_in_ref[c])
        if first:
            fill_store(store, lines_ref, 6, 6, 6)
            from_lines(store, grads_ref, experts, capacity, 6)
        grad_active = dot(grads_ref[...], w_out_ref[c], 1, 1)
        gelu, slope = gelu_parts(lifted)
        active_ref[c] = gelu.astype(BF16)
        lifted_ref[c] = (grad_active * slope).astype(BF16)
        if first or last:
            for copy in leaving(c, first):
                copy.start()
        moved = dot(lifted_ref[c], w_in_ref[c], 1, 1)
        total[...] = moved if first else total[...] + moved
        made = dot(active_ref[c], w_out_ref[c])
        if last:
            to_lines(store, total, experts, capacity, 0)
            spill_store(store, back_ref, 6, 0)
        produced[...] = made if first else produced[...] + made

    def middle(c, _):
        chunk(c)
        for is_early in (True, False):

            @pl.when((c < early) == is_early)
            def _():
                for copy in leaving(c, is_early):
                    copy.start()

        return 0

    chunk(0, first=True)
    lax.fori_loop(1, chunks - 1, middle, 0)
    chunk(chunks - 1, last=True)

    to_lines(store, produced, experts, capacity, 0)
    spill_store(store, back_ref, 6, 6)
    arrived = lines_ref[:, 12 * LANES : 13 * LANES].astype(F32)
    sums = jnp.sum(arrived, axis=0, keepdims=True)
    column = lax.broadcasted_iota(jnp.int32, sums.shape, 1)
    count = jnp.sum(jnp.where(column == 0, 64.0 * sums, sums), axis=1, keepdims=True)
    upper = jnp.floor(count * (1.0 / 256.0))
    pair = jnp.where(column == 0, upper, jnp.where(column == 1, count - 256.0 * upper, 0.0))
    back_ref[:, 12 * LANES : 13 * LANES] = jnp.broadcast_to(
        pair, (back_ref.shape[0], LANES)
    ).astype(BF16)
    for c in range(chunks):
        for copy in leaving(c, c < early):
            copy.wait()


def expert_gradients_kernel(
    experts,
    capacity,
    steps,
    lines_a,
    lines_b,
    active_a,
    active_b,
    lifted_a,
    lifted_b,
    out_grad_ref,
    in_grad_ref,
    store,
    rows_ref,
    grads_ref,
):
    f = pl.program_id(0)
    own = rows_ref.shape[0] // 2

    @pl.when(f == 0)
    def _():
        for i, lines in enumerate((lines_a, lines_b)):
            here = pl.ds(i * own, own)
            unpack(store, lines, rows_ref.at[here], experts, capacity, 0)
            unpack(store, lines, grads_ref.at[here], experts, capacity, capacity)

    @pl.when(f < steps)
    def _():
        active = jnp.concatenate([active_a[...], active_b[...]], axis=0)
        out_grad_ref[...] = dot(active, grads_ref[...], 0, 0)

    @pl.when(f >= steps)
    def _():
        lifted = jnp.concatenate([lifted_a[...], lifted_b[...]], axis=0)
        in_grad_ref[...] = dot(rows_ref[...], lifted, 0, 0)


def attention_pair(q, k, v, grad, probs):
    seq_len = q.shape[0]
    low = (lax.broadcasted_iota(jnp.int32, (1, LANES), 1) < 64).astype(F32)
    score_scale = 1.0 / math.sqrt(64)
    low_half = low.astype(BF16)
    high_half = (1.0 - low).astype(BF16)
    grad_both = jnp.concatenate([grad * low_half, grad * high_half], axis=0)
    query_both = jnp.concatenate([q * low_half, q * high_half], axis=0)
    grad_probs = dot(v, grad_both, 1, 1)
    values = dot(probs, grad_both)
    wide = probs.astype(F32)
    inner = jnp.sum(wide * grad_probs, axis=0, keepdims=True)
    grad_scores = (wide * (grad_probs - inner)).astype(BF16)
    keys = dot(grad_scores, query_both) * score_scale
    queries = dot(grad_scores, k, 0, 0) * score_scale
    queries = queries[:seq_len] * low + queries[seq_len:] * (1.0 - low)
    return queries.astype(BF16), keys.astype(BF16), values.astype(BF16)


def hidden_kernel(
    experts,
    capacity,
    at_ref,
    dispatch_ref,
    gain_ref,
    lines_hbm,
    hidden_hbm,
    grad_hbm,
    weight_hbm,
    mixed_hbm,
    probs_hbm,
    grad_hidden_hbm,
    branch_mine_ref,
    branch_other_ref,
    attended_hbm,
    gains_ref,
    out_hbm,
    lines_ref,
    out_ref,
    store,
    came,
    normed,
    branch_ref,
    hidden_ref,
    grad_ref,
    weight_ref,
    mixed_ref,
    probs_ref,
    grad_hidden_ref,
    attended_ref,
    sems,
):
    rows, width = hidden_ref.shape
    seq_count = probs_ref.shape[0]
    seq_len = rows // seq_count
    pairs = probs_ref.shape[1]
    half = width // 2
    core = at_ref[0]
    other = (1 - core) * pairs
    copies = [
        pltpu.make_async_copy(hidden_hbm, hidden_ref, sems.at[0]),
        pltpu.make_async_copy(grad_hbm, grad_ref, sems.at[1]),
        pltpu.make_async_copy(weight_hbm, weight_ref, sems.at[2]),
    ]
    for part in range(3):
        copies.append(
            pltpu.make_async_copy(
                mixed_hbm.at[pl.ds(2 * part * pairs + other, pairs)],
                mixed_ref.at[part],
                sems.at[3 + part],
            )
        )
    for s in range(seq_count):
        copies.append(
            pltpu.make_async_copy(
                probs_hbm.at[s, pl.ds(other, pairs)], probs_ref.at[s], sems.at[6 + s]
            )
        )
    lines_copy = pltpu.make_async_copy(
        lines_hbm.at[:, : lines_ref.shape[1]], lines_ref, sems.at[10]
    )
    lines_copy.start()
    for copy in copies:
        copy.start()
    grad_hidden_copy = pltpu.make_async_copy(grad_hidden_ref, grad_hidden_hbm, sems.at[8])
    attended_copy = pltpu.make_async_copy(attended_ref, attended_hbm, sems.at[9])

    lines_copy.wait()
    fill_store(store, lines_ref, 0, 6, 0)
    from_lines(store, came, experts, capacity, 0)
    gain = as_row(gain_ref)
    normed[...] = dot(dispatch_ref[...], came[...], 0, 0)
    gains_ref[...] = jnp.zeros_like(gains_ref)
    step = 128
    copies[0].wait()
    copies[1].wait()

    def body(i, _):
        at = pl.ds(pl.multiple_of(i * step, step), step)
        scaled, scale = normalize(hidden_ref[at, :])
        grad = normed[at, :]
        grad_hidden = grad_ref[at, :].astype(F32) + norm_backward(scaled, scale, grad * gain)
        grad_hidden_ref[at, :] = grad_hidden
        branch_ref[at, :] = grad_hidden.astype(BF16)
        gains_ref[0:1, :] += jnp.sum(grad * scaled, axis=0, keepdims=True)
        gains_ref[1:2, :] += jnp.sum(grad, axis=0, keepdims=True)
        return 0

    lax.fori_loop(0, rows // step, body, 0)
    grad_hidden_copy.start()
    branch_mine_ref[...] = branch_ref[:, pl.ds(pl.multiple_of(core * half, half), half)]
    branch_other_ref[...] = branch_ref[:, pl.ds(pl.multiple_of((1 - core) * half, half), half)]
    copies[2].wait()

    def project(i, _):
        at = pl.ds(pl.multiple_of(i * 256, 256), 256)
        block = dot(branch_ref[at, :], weight_ref[...], 1, 1).astype(BF16)
        for tile in range(2 * pairs):
            attended_ref[tile, at, :] = block[:, tile * LANES : (tile + 1) * LANES]
        return 0

    lax.fori_loop(0, rows // 256, project, 0)
    attended_copy.start()
    for copy in copies[3:]:
        copy.wait()

    def leaving(p):
        at = pl.ds(pl.multiple_of(p * LANES, LANES), LANES)
        return pltpu.make_async_copy(out_ref.at[p], out_hbm.at[:, :, at], sems.at[11 + p])

    def pair(p, _):
        for s in range(seq_count):
            here = slice(s * seq_len, (s + 1) * seq_len)
            grads = attention_pair(
                mixed_ref[0, p, here, :],
                mixed_ref[1, p, here, :],
                mixed_ref[2, p, here, :],
                attended_ref[other + p, here, :],
                probs_ref[s, p],
            )
            for part in range(3):
                out_ref[p, part, here, :] = grads[part]
        leaving(p).start()
        return 0

    lax.fori_loop(0, pairs, pair, 0)
    for p in range(pairs):
        leaving(p).wait()
    grad_hidden_copy.wait()
    attended_copy.wait()


def input_kernel(
    at_ref,
    mine_ref,
    other_ref,
    gain_ref,
    weight_hbm,
    x_hbm,
    grad_hidden_hbm,
    input_grad_hbm,
    weight_ref,
    x_ref,
    grad_hidden_ref,
    normed,
    sems,
):
    rows, width = x_ref.shape
    half = width // 2
    core = at_ref[0]

    def fetch(part):
        at = pl.ds(pl.multiple_of(part * width, width), width)
        return pltpu.make_async_copy(weight_hbm.at[:, at], weight_ref.at[:, at], sems.at[part])

    x_copy = pltpu.make_async_copy(x_hbm, x_ref, sems.at[3])
    grad_copy = pltpu.make_async_copy(grad_hidden_hbm, grad_hidden_ref, sems.at[4])
    for copy in (fetch(0), fetch(1), fetch(2), x_copy, grad_copy):
        copy.start()
    normed[...] = jnp.zeros_like(normed)

    def product(part, _):
        fetch(part).wait()
        terms = []
        for ref, group in ((mine_ref, core), (other_ref, 1 - core)):
            at = pl.multiple_of(part * width + group * half, half)
            terms.append(dot(ref[part], weight_ref[:, pl.ds(at, half)], 1, 1))
        normed[...] += terms[0] + terms[1]
        return 0

    lax.fori_loop(0, 3, product, 0)
    gain = as_row(gain_ref)
    x_copy.wait()
    grad_copy.wait()
    step = 128

    def leaving(i):
        at = pl.ds(pl.multiple_of(i * step, step), step)
        return pltpu.make_async_copy(
            grad_hidden_ref.at[at], input_grad_hbm.at[at], sems.at[5 + i]
        )

    def body(i, _):
        at = pl.ds(pl.multiple_of(i * step, step), step)
        scaled, scale = normalize(x_ref[at, :].astype(F32))
        grad_hidden_ref[at, :] += norm_backward(scaled, scale, normed[at, :] * gain)
        leaving(i).start()
        return 0

    lax.fori_loop(0, rows // step, body, 0)
    for i in range(rows // step):
        leaving(i).wait()


def attention_kernel(
    at_ref,
    mixed_hbm,
    attended_hbm,
    probs_hbm,
    out_hbm,
    mixed_ref,
    attended_ref,
    probs_ref,
    out_ref,
    sems,
    out_sems,
):
    seq_count = probs_ref.shape[0]
    pairs, rows, _ = attended_ref.shape
    seq_len = rows // seq_count
    first = at_ref[0] * pairs

    def fetches(p):
        moves = [
            (mixed_hbm.at[2 * part * pairs + first + p], mixed_ref.at[part, p])
            for part in range(3)
        ]
        moves.append((attended_hbm.at[first + p], attended_ref.at[p]))
        for s in range(seq_count):
            moves.append((probs_hbm.at[s, first + p], probs_ref.at[s, p]))
        return [
            pltpu.make_async_copy(hbm, ref, sems.at[i, p]) for i, (hbm, ref) in enumerate(moves)
        ]

    def leaving(p):
        at = pl.ds(pl.multiple_of(p * LANES, LANES), LANES)
        return pltpu.make_async_copy(out_ref.at[p], out_hbm.at[:, :, at], out_sems.at[p])

    for p in range(pairs):
        for copy in fetches(p):
            copy.start()

    def pair(p, _):
        for copy in fetches(p):
            copy.wait()
        for s in range(seq_count):
            here = slice(s * seq_len, (s + 1) * seq_len)
            grads = attention_pair(
                mixed_ref[0, p, here, :],
                mixed_ref[1, p, here, :],
                mixed_ref[2, p, here, :],
                attended_ref[p, here, :],
                probs_ref[s, p],
            )
            for part in range(3):
                out_ref[p, part, here, :] = grads[part]
        leaving(p).start()
        return 0

    lax.fori_loop(0, pairs, pair, 0)
    for p in range(pairs):
        leaving(p).wait()


def weights_kernel(
    at_ref,
    scale_ref,
    ffn_gains_ref,
    mine_hbm,
    came_hbm,
    normed_lines_hbm,
    weight_lines_hbm,
    attended_lines_hbm,
    branch_a_hbm,
    branch_b_hbm,
    send_x_hbm,
    keep_x_hbm,
    send_z_hbm,
    keep_z_hbm,
    send_y_hbm,
    keep_y_hbm,
    right_ref,
    normed_ref,
    weight_ref,
    out_left_ref,
    branch_ref,
    x_ref,
    z_ref,
    y_ref,
    blocks,
    sums,
    sems,
    out_sems,
):
    rows = branch_ref.shape[0] // 2
    half = right_ref.shape[2]
    fetches = [
        (mine_hbm, right_ref.at[:, :rows]),
        (came_hbm, right_ref.at[:, rows:]),
        (normed_lines_hbm, normed_ref),
        (branch_a_hbm, branch_ref.at[:rows]),
        (branch_b_hbm, branch_ref.at[rows:]),
        (attended_lines_hbm, out_left_ref),
        (weight_lines_hbm, weight_ref),
    ]
    fetches = [
        pltpu.make_async_copy(hbm, ref, sems.at[i]) for i, (hbm, ref) in enumerate(fetches)
    ]
    for copy in fetches:
        copy.start()
    leaving = []
    for copy in fetches[:3]:
        copy.wait()
    size = x_ref.shape[1]
    lane = lax.broadcasted_iota(jnp.int32, (size, LANES), 1)
    order = order_matrix(at_ref)
    for turn, step in enumerate((1, 0)):
        lines = slice(step * size, (step + 1) * size)

        def product(part, _):
            blocks[part] = dot(normed_ref[lines, :], right_ref[part])
            return 0

        lax.fori_loop(0, 3, product, 0)
        if turn == 0:
            for part in range(3):
                total = jnp.zeros((1, half), F32)
                for at in range(0, 2 * rows, 128):
                    wide = right_ref[part, at : at + 128, :].astype(F32)
                    total = total + jnp.sum(wide, axis=0, keepdims=True)
                sums[part : part + 1, :] = total
            for copy in fetches[3:6]:
                copy.wait()
        out = dot(out_left_ref[lines, :], branch_ref[...]).astype(BF16)
        if turn == 0:
            fetches[6].wait()
        gain = jnp.zeros((size, 1), F32)
        shift = jnp.zeros((size, 1), F32)
        for part in range(3):
            weight = weight_ref[lines, part * half : (part + 1) * half].astype(F32)
            gain = gain + jnp.sum(blocks[part] * weight, axis=1, keepdims=True)
            shift = shift + jnp.sum(sums[part : part + 1, :] * weight, axis=1, keepdims=True)
        parts = [blocks[part].astype(BF16) for part in range(3)]
        x_ref[step, :, :half] = parts[0]
        x_ref[step, :, half:] = out[:, : half // 2]
        side = out[:, half // 2 : 3 * half // 4]
        for group in range(size // 16):
            x, chip = group // 16, group % 16
            here = slice(group * 16, (group + 1) * 16)
            z_ref[step, chip, x, :, :half] = parts[1][here]
            z_ref[step, chip, x, :, half:] = side[here]
        scale = scale_ref[lines, :]
        gain = (gain - scale[:, 1:2] * shift) / scale[:, 0:1]
        ffn = []
        for i in range(size // 256):
            block_at = at_ref[4 + step * (size // 256) + i]
            ffn.append(
                lax.dot_general(
                    order,
                    ffn_gains_ref[:, pl.ds(pl.multiple_of(block_at * 256, 256), 256)],
                    (((1,), (1,)), ((), ())),
                    precision=lax.Precision.HIGHEST,
                    preferred_element_type=F32,
                )
            )
        ffn = jnp.concatenate(ffn, axis=0)
        small = jnp.where(lane == 0, gain, jnp.where(lane == 1, shift, 0.0))
        small = jnp.where(lane == 2, ffn[:, 0:1], jnp.where(lane == 3, ffn[:, 1:2], small))
        small = small.astype(BF16)
        side = out[:, 3 * half // 4 :]
        for group in range(size // 16):
            x, z, y = group // 16, group // 4 % 4, group % 4
            here = slice(group * 16, (group + 1) * 16)
            y_ref[step, y, x, z, :, :half] = parts[2][here]
            y_ref[step, y, x, z, :, half : half + LANES] = side[here]
            y_ref[step, y, x, z, :, half + LANES :] = small[here]
        x_at = pl.ds(2 * step, 2)
        moves = [
            (x_ref.at[step], send_x_hbm if step == 1 else keep_x_hbm),
            (z_ref.at[step, 8:16], send_z_hbm.at[:, x_at]),
            (z_ref.at[step, 0:8], keep_z_hbm.at[:, x_at]),
            (y_ref.at[step, 2:4], send_y_hbm.at[:, x_at]),
            (y_ref.at[step, 0:2], keep_y_hbm.at[:, x_at]),
        ]
        for i, (ref, hbm) in enumerate(moves):
            copy = pltpu.make_async_copy(ref, hbm, out_sems.at[turn * 5 + i])
            copy.start()
            leaving.append(copy)
    for copy in leaving:
        copy.wait()


def second_kernel(kept_ref, first_ref, send_ref):
    send_ref[...] = (kept_ref[...].astype(F32) + first_ref[...].astype(F32)).astype(BF16)


def third_kernel(kept_ref, first_ref, second_ref, send_ref):
    total = kept_ref[...].astype(F32) + first_ref[...].astype(F32) + second_ref[...].astype(F32)
    send_ref[...] = total.astype(BF16)


def merge_kernel(*refs):
    parts = [refs[4 * i : 4 * i + 4] for i in range(3)]
    send_ref, keep_ref = refs[12:]
    for x in range(2):
        for z in range(2):
            for y in range(2):
                at = 0
                for part, spot in zip(parts, ((x, z, y), (z, y, x), (y, x, z))):
                    total = part[0][spot].astype(F32)
                    for ref in part[1:]:
                        total = total + ref[spot].astype(F32)
                    span = total.shape[1]
                    if x == 1:
                        send_ref[z, y, :, at : at + span] = total.astype(BF16)
                    else:
                        keep_ref[z, y, :, at : at + span] = total
                    at += span


def split_kernel(at_ref, kept_ref, came_ref, mine_ref, other_ref, store):
    store[...] = kept_ref[...] + came_ref[...].astype(F32)
    core = at_ref[0]
    mine_ref[...] = store[pl.ds(pl.multiple_of(core * 8, 8), 8), :]
    other_ref[...] = store[pl.ds(pl.multiple_of((1 - core) * 8, 8), 8), :]


def join_kernel(spans, at_ref, mine_ref, other_ref, qkv_ref, out_ref, small_ref):
    half = out_ref.shape[1] // 2
    core = at_ref[0]
    for ref, group in ((mine_ref, core), (other_ref, 1 - core)):
        group_at = group * half
        at, out_at = 0, 0
        for part, span in enumerate(spans):
            spot = pl.multiple_of(2 * part * half + group_at, half)
            qkv_ref[:, pl.ds(spot, half)] = ref[:, at : at + half]
            side = span - half
            spot = pl.multiple_of(group_at + out_at, LANES)
            out_ref[:, pl.ds(spot, side)] = ref[:, at + half : at + span]
            at += span
            out_at += side
    small_ref[...] = mine_ref[:, at : at + LANES] + other_ref[:, at : at + LANES]


def output_kernel(experts, capacity, lines_ref, dispatch_ref, hidden_ref, out_ref, store, came):
    unpack(store, lines_ref, came, experts, capacity, capacity)
    back = dot(dispatch_ref[...], came[...], 0, 0)
    out_ref[...] = (hidden_ref[...] + back).astype(BF16)


def whole(shape):
    return pl.BlockSpec(shape, lambda *_: (0,) * len(shape))


def shaped(shape, dtype):
    return jax.ShapeDtypeStruct(shape, dtype)


def per_device(
    block_input,
    attn_gain,
    attn_shift,
    query_key_value_weight,
    output_weight,
    ffn_gain,
    ffn_shift,
    expert_in,
    expert_out,
    hash_ids,
    seq_lengths,
    prev_counts,
    out_grad,
):
    seq_count, seq_len, width = block_input.shape
    rows = seq_count * seq_len
    chips = lax.axis_size(WIDE)
    experts = chips
    capacity = max(2, 3 * rows // (4 * experts))
    n_slots = experts * capacity
    ff_width = expert_in.shape[2]
    half_ff = ff_width // 2
    half = width // 2
    pairs = HEADS // 2
    lines = 8 * chips
    core = lax.axis_index("narrow").astype(jnp.int32)
    core_at = core.reshape(1)
    other_at = (1 - core).reshape(1)
    x = block_input.reshape(rows, width)
    grad_rows = out_grad.reshape(rows, width)
    w_in = expert_in[0]
    w_out = expert_out[0]
    scales = [v.reshape(8, LANES) for v in (attn_gain, attn_shift, ffn_gain, ffn_shift)]
    smem = pl.BlockSpec(memory_space=pltpu.SMEM)
    vmem = pl.BlockSpec(memory_space=pltpu.VMEM)
    hbm = pl.BlockSpec(memory_space=pl.ANY)
    coordinates = [lax.axis_index(name).astype(jnp.int32) for name in WIDE]
    blocks_x = [places(place, core) ^ coordinates[0] for place in range(4)]
    spot = jnp.stack([core] + coordinates + blocks_x).astype(jnp.int32)

    normed, mixed, probs, attended, hidden, dispatch, send = pl.pallas_call(
        functools.partial(forward_kernel, experts, capacity),
        out_shape=(
            shaped((rows, width), BF16),
            shaped((3 * pairs, rows, LANES), BF16),
            shaped((seq_count, pairs, seq_len, 2 * seq_len), BF16),
            shaped((rows, width), BF16),
            shaped((rows, width), F32),
            shaped((n_slots, rows), BF16),
            shaped((lines, 13 * LANES), BF16),
        ),
        in_specs=[smem] + [vmem] * 6 + [hbm] * 3,
        out_specs=[hbm] * 5 + [vmem] * 2,
        scratch_shapes=[
            pltpu.VMEM((width, 3 * width), BF16),
            pltpu.VMEM((width, width), BF16),
            pltpu.VMEM((rows, width), BF16),
            pltpu.VMEM((rows, width), BF16),
            pltpu.VMEM((3 * pairs, rows, LANES), BF16),
            pltpu.VMEM((seq_count, pairs, seq_len, 2 * seq_len), BF16),
            pltpu.VMEM((rows, width), BF16),
            pltpu.VMEM((rows, width), F32),
            pltpu.VMEM((rows, width), BF16),
            pltpu.VMEM((seq_count, seq_len, 2 * seq_len), F32),
            pltpu.VMEM((13, lines, LANES), F32),
            pltpu.SemaphoreType.DMA((10,)),
        ],
        compiler_params=params(60),
        name="forward",
        cost_estimate=cost(10, 20),
    )(
        seq_lengths,
        hash_ids,
        x,
        *scales,
        query_key_value_weight,
        output_weight,
        grad_rows,
    )
    arrived = exchanged(send)
    normed_other = swapped(normed)
    attended_other = swapped(attended)
    block = width // 4
    column = pl.BlockSpec((rows, block), lambda i, at: (0, at[4 + i]))
    weight_part = [
        pl.BlockSpec((block, half), lambda i, at, part=part: (at[4 + i], 2 * part + at[0]))
        for part in range(3)
    ]
    normed_lines, attended_lines, weight_lines, scale_lines = pl.pallas_call(
        prepare_kernel,
        out_shape=(
            shaped((width, 2 * rows), BF16),
            shaped((width, 2 * rows), BF16),
            shaped((width, 3 * half), BF16),
            shaped((width, LANES), F32),
        ),
        grid_spec=pltpu.PrefetchScalarGridSpec(
            num_scalar_prefetch=1,
            grid=(4,),
            in_specs=[column] * 4 + weight_part + [whole((8, LANES))] * 2,
            out_specs=[
                pl.BlockSpec((block, 2 * rows), lambda i, at: (i, 0)),
                pl.BlockSpec((block, 2 * rows), lambda i, at: (i, 0)),
                pl.BlockSpec((block, 3 * half), lambda i, at: (i, 0)),
                pl.BlockSpec((block, LANES), lambda i, at: (i, 0)),
            ],
        ),
        compiler_params=params(60),
        name="prepare",
        cost_estimate=cost(4, 8),
    )(
        spot,
        normed,
        normed_other,
        attended,
        attended_other,
        query_key_value_weight,
        query_key_value_weight,
        query_key_value_weight,
        *scales[:2],
    )
    arrived, normed_lines = lax.optimization_barrier((arrived, normed_lines))

    chunks = 4
    tile = ff_width // chunks
    half_block = shaped((n_slots, half_ff), BF16)
    active_other, active_mine, lifted_other, lifted_mine, back = pl.pallas_call(
        functools.partial(expert_kernel, experts, capacity),
        out_shape=(
            half_block,
            half_block,
            half_block,
            half_block,
            shaped((lines, 13 * LANES), BF16),
        ),
        in_specs=[smem] + [hbm] * 3,
        out_specs=[hbm] * 4 + [vmem],
        scratch_shapes=[
            pltpu.VMEM((lines, 13 * LANES), BF16),
            pltpu.VMEM((chunks, width, tile), BF16),
            pltpu.VMEM((chunks, tile, width), BF16),
            pltpu.VMEM((n_slots, width), BF16),
            pltpu.VMEM((n_slots, width), BF16),
            pltpu.VMEM((chunks, n_slots, tile), BF16),
            pltpu.VMEM((chunks, n_slots, tile), BF16),
            pltpu.VMEM((12, lines, LANES), F32),
            pltpu.VMEM((n_slots, width), F32),
            pltpu.VMEM((n_slots, width), F32),
            pltpu.SemaphoreType.DMA((1,)),
            pltpu.SemaphoreType.DMA((2, chunks)),
            pltpu.SemaphoreType.DMA((2, chunks)),
        ],
        compiler_params=params(60),
        name="expert",
        cost_estimate=cost(16, 25),
    )(spot, arrived, w_in, w_out)
    returned = exchanged(back)

    arrived_other = swapped(arrived)
    active_came = swapped(active_other)
    lifted_came = swapped(lifted_other)
    steps = 4
    tile = half_ff // steps
    early = pl.BlockSpec((n_slots, tile), lambda f: (0, jnp.minimum(f, steps - 1)))
    late = pl.BlockSpec((n_slots, tile), lambda f: (0, jnp.maximum(f - steps, 0)))
    expert_out_grad, expert_in_grad = pl.pallas_call(
        functools.partial(expert_gradients_kernel, experts, capacity, steps),
        out_shape=(shaped((half_ff, width), F32), shaped((width, half_ff), F32)),
        grid=(2 * steps,),
        in_specs=[whole((lines, 13 * LANES))] * 2 + [early] * 2 + [late] * 2,
        out_specs=[
            pl.BlockSpec((tile, width), lambda f: (jnp.minimum(f, steps - 1), 0)),
            pl.BlockSpec((width, tile), lambda f: (0, jnp.maximum(f - steps, 0))),
        ],
        scratch_shapes=[
            pltpu.VMEM((lines, LANES), F32),
            pltpu.VMEM((2 * n_slots, width), BF16),
            pltpu.VMEM((2 * n_slots, width), BF16),
        ],
        compiler_params=params(60),
        name="expert_gradients",
        cost_estimate=cost(10, 30),
    )(arrived, arrived_other, active_mine, active_came, lifted_mine, lifted_came)
    returned, expert_out_grad, expert_in_grad = lax.optimization_barrier(
        (returned, expert_out_grad, expert_in_grad)
    )

    half_pairs = pairs // 2
    grad_hidden, branch, branch_out, grad_attended, ffn_gains, mixed_out = pl.pallas_call(
        functools.partial(hidden_kernel, experts, capacity),
        out_shape=(
            shaped((rows, width), F32),
            shaped((rows, half), BF16),
            shaped((rows, half), BF16),
            shaped((pairs, rows, LANES), BF16),
            shaped((8, width), F32),
            shaped((3, rows, half), BF16),
        ),
        in_specs=[smem, vmem, vmem] + [hbm] * 6,
        out_specs=[hbm, vmem, vmem, hbm, vmem, hbm],
        scratch_shapes=[
            pltpu.VMEM((lines, 6 * LANES), BF16),
            pltpu.VMEM((half_pairs, 3, rows, LANES), BF16),
            pltpu.VMEM((6, lines, LANES), F32),
            pltpu.VMEM((n_slots, width), BF16),
            pltpu.VMEM((rows, width), F32),
            pltpu.VMEM((rows, width), BF16),
            pltpu.VMEM((rows, width), F32),
            pltpu.VMEM((rows, width), BF16),
            pltpu.VMEM((width, width), BF16),
            pltpu.VMEM((3, half_pairs, rows, LANES), BF16),
            pltpu.VMEM((seq_count, half_pairs, seq_len, 2 * seq_len), BF16),
            pltpu.VMEM((rows, width), F32),
            pltpu.VMEM((pairs, rows, LANES), BF16),
            pltpu.SemaphoreType.DMA((11 + half_pairs,)),
        ],
        compiler_params=params(60),
        name="hidden_backward",
        cost_estimate=cost(6, 14),
    )(spot, dispatch, scales[2], returned, hidden, grad_rows, output_weight, mixed, probs)
    mixed_came = swapped(mixed_out)
    branch_other = swapped(branch_out)

    spans = (half + half // 2, half + half // 4, half + half // 2)
    shapes = ((512,), (8, 4, 16), (2, 4, 4, 16))
    size = width // 2
    mixed_mine = pl.pallas_call(
        attention_kernel,
        out_shape=shaped((3, rows, half), BF16),
        in_specs=[smem] + [hbm] * 3,
        out_specs=hbm,
        scratch_shapes=[
            pltpu.VMEM((3, half_pairs, rows, LANES), BF16),
            pltpu.VMEM((half_pairs, rows, LANES), BF16),
            pltpu.VMEM((seq_count, half_pairs, seq_len, 2 * seq_len), BF16),
            pltpu.VMEM((half_pairs, 3, rows, LANES), BF16),
            pltpu.SemaphoreType.DMA((6, half_pairs)),
            pltpu.SemaphoreType.DMA((half_pairs,)),
        ],
        compiler_params=params(60),
        name="attention_backward",
        cost_estimate=cost(4, 5),
    )(spot, mixed, grad_attended, probs)
    halves = pl.pallas_call(
        weights_kernel,
        out_shape=[
            shaped(shape + (span,), BF16) for shape, span in zip(shapes, spans) for _ in range(2)
        ],
        in_specs=[smem, vmem, vmem] + [hbm] * 7,
        out_specs=[hbm] * 6,
        scratch_shapes=[
            pltpu.VMEM((3, 2 * rows, half), BF16),
            pltpu.VMEM((width, 2 * rows), BF16),
            pltpu.VMEM((width, 3 * half), BF16),
            pltpu.VMEM((width, 2 * rows), BF16),
            pltpu.VMEM((2 * rows, half), BF16),
            pltpu.VMEM((2, 512, spans[0]), BF16),
            pltpu.VMEM((2, 16, 2, 16, spans[1]), BF16),
            pltpu.VMEM((2, 4, 2, 4, 16, spans[2]), BF16),
            pltpu.VMEM((3, size, half), F32),
            pltpu.VMEM((8, half), F32),
            pltpu.SemaphoreType.DMA((7,)),
            pltpu.SemaphoreType.DMA((10,)),
        ],
        compiler_params=params(60),
        name="weight_gradients",
        cost_estimate=cost(8, 20),
    )(
        spot,
        scale_lines,
        ffn_gains,
        mixed_mine,
        mixed_came,
        normed_lines,
        weight_lines,
        attended_lines,
        branch,
        branch_other,
    )

    input_grad = pl.pallas_call(
        input_kernel,
        out_shape=shaped((rows, width), F32),
        in_specs=[smem, vmem, vmem, vmem, hbm, hbm, hbm],
        out_specs=hbm,
        scratch_shapes=[
            pltpu.VMEM((width, 3 * width), BF16),
            pltpu.VMEM((rows, width), BF16),
            pltpu.VMEM((rows, width), F32),
            pltpu.VMEM((rows, width), F32),
            pltpu.SemaphoreType.DMA((9,)),
        ],
        compiler_params=params(60),
        name="input_backward",
        cost_estimate=cost(6, 14),
    )(spot, mixed_mine, mixed_out, scales[0], query_key_value_weight, x, grad_hidden)

    block_output = pl.pallas_call(
        functools.partial(output_kernel, experts, capacity),
        out_shape=shaped((rows, width), BF16),
        grid=(1,),
        in_specs=[
            whole((lines, 13 * LANES)),
            whole((n_slots, rows)),
            whole((rows, width)),
        ],
        out_specs=whole((rows, width)),
        scratch_shapes=[
            pltpu.VMEM((lines, LANES), F32),
            pltpu.VMEM((n_slots, width), BF16),
        ],
        compiler_params=params(60),
        name="block_output",
        cost_estimate=cost(1, 5),
    )(returned, dispatch, hidden)

    orders = ((0, 1, 2), (1, 2, 0), (2, 0, 1))
    sent = [part.reshape(2, 4, 4, 16, -1) for part in halves[0::2]]
    kept = [part.reshape(2, 4, 4, 16, -1) for part in halves[1::2]]
    first = [crossed(part, order[0], True) for part, order in zip(sent, orders)]
    first, input_grad = lax.optimization_barrier((first, input_grad))

    def cut(span, shape, at):
        return pl.BlockSpec(shape + (16, span), lambda *_: at + (0, 0))

    def added(kernel, arrays, shape, spots, name):
        span = arrays[0].shape[-1]
        return pl.pallas_call(
            kernel,
            out_shape=shaped(shape + (16, span), BF16),
            grid=(1,),
            in_specs=[cut(span, shape, at) for at in spots],
            out_specs=whole(shape + (16, span)),
            compiler_params=params(16),
            name=name,
            cost_estimate=cost(0.01, 2),
        )(*arrays)

    second = []
    for k, c, order in zip(kept, first, orders):
        send = added(second_kernel, (k, c), (2, 2, 4), ((0, 1, 0),) * 2, "second")
        second.append(crossed(send, order[1], True))
    third = []
    for k, c, d, order in zip(kept, first, second, orders):
        spots = ((0, 0, 1),) * 3
        send = added(third_kernel, (k, c, d), (2, 2, 2), spots, "third")
        third.append(crossed(send, order[2], True))
    total_span = sum(spans)
    send, keep = pl.pallas_call(
        merge_kernel,
        out_shape=(
            shaped((2, 2, 16, total_span), BF16),
            shaped((2, 2, 16, total_span), F32),
        ),
        grid=(1,),
        in_specs=[cut(span, (2, 2, 2), (0, 0, 0)) for span in spans for _ in range(4)],
        out_specs=[whole((2, 2, 16, total_span))] * 2,
        compiler_params=params(16),
        name="merge",
        cost_estimate=cost(0.01, 4),
    )(*(array for group in zip(kept, first, second, third) for array in group))
    came = crossed(send, 0, False)
    for axis in (1, 2):
        keep = keep + came.astype(F32)
        came = crossed(keep[1].astype(BF16), axis, False)
        keep = keep[0]
    own, other = pl.pallas_call(
        split_kernel,
        out_shape=(shaped((8, total_span), F32), shaped((8, total_span), F32)),
        in_specs=[smem, vmem, vmem],
        out_specs=[vmem, vmem],
        scratch_shapes=[pltpu.VMEM((16, total_span), F32)],
        compiler_params=params(16),
        name="split",
    )(spot, keep, came)
    qkv_grad, out_weight_grad, vectors = pl.pallas_call(
        functools.partial(join_kernel, (*spans[:2], half + half // 4)),
        out_shape=(
            shaped((8, 3 * width), F32),
            shaped((8, width), F32),
            shaped((8, LANES), F32),
        ),
        in_specs=[smem, vmem, vmem],
        out_specs=[vmem] * 3,
        compiler_params=params(16),
        name="join",
    )(spot, own, swapped(other))

    pair = returned[:, 12 * LANES : 12 * LANES + 2].reshape(chips, 8, 2)[:, 0].astype(F32)
    counts = 256.0 * pair[:, 0] + pair[:, 1]
    counts = counts + swapped(counts)
    total_tokens = float(rows * chips * 2)
    new_average = (momentum * prev_counts.astype(F32) + (1.0 - momentum) * counts) * (
        float(experts) / total_tokens
    )
    return (
        block_output.reshape(seq_count, seq_len, width),
        input_grad.reshape(seq_count, seq_len, width),
        vectors[:, 0],
        vectors[:, 1],
        qkv_grad,
        out_weight_grad,
        vectors[:, 2],
        vectors[:, 3],
        expert_in_grad[None],
        expert_out_grad[None],
        new_average,
    )


def solution(mesh):
    finer = Mesh(
        mesh.devices.reshape(4, 4, 4, mesh.shape["narrow"]),
        ("wide_0", "wide_1", "wide_2", "narrow"),
    )
    placed = (
        P(WIDE_NARROW, None, None),
        P(),
        P(),
        P(),
        P(),
        P(),
        P(),
        P(WIDE, None, None),
        P(WIDE, None, None),
        P(WIDE_NARROW, None),
        P(WIDE_NARROW),
        P(),
        P(WIDE_NARROW, None, None),
    )
    return jax.shard_map(
        per_device,
        mesh=finer,
        in_specs=placed,
        out_specs=(
            P(WIDE_NARROW, None, None),
            P(WIDE_NARROW, None, None),
            P(WIDE_NARROW),
            P(WIDE_NARROW),
            P(WIDE_NARROW, None),
            P(WIDE_NARROW, None),
            P(WIDE_NARROW),
            P(WIDE_NARROW),
            P(WIDE, None, "narrow"),
            P(WIDE, "narrow", None),
            P(),
        ),
        check_vma=False,
    )
```
